32 devices in a mesh: dp: 8 (over z, core), tensor: 4 (over y, x).
Axes of the slice: x: 2, y: 2, z: 4, core: 2. Of those that a mesh axis runs over, the one named last changes fastest.
Arguments:
- tokens: bfloat16 [16384, 2560], P(('dp', 'tensor')), may hold values from -6 to 6
- segments: int32 [16, 1024], P('dp'), may hold values from -1 to 16, as said below
- attn_gain: bfloat16 [2560], P('dp'), may hold values from 0.5 to 1.5
- w_query: bfloat16 [2560, 2560], P('dp', 'tensor'), may hold values from -0.125 to 0.125
- w_key: bfloat16 [2560, 640], P('dp', 'tensor'), may hold values from -0.125 to 0.125
- w_value: bfloat16 [2560, 640], P('dp', 'tensor'), may hold values from -0.125 to 0.125
- w_out: bfloat16 [2560, 2560], P('tensor', 'dp'), may hold values from -1 to 1
- mlp_gain: bfloat16 [2560], P('dp'), may hold values from 0.5 to 1.5
- w_gate: bfloat16 [2560, 6912], P('dp', 'tensor'), may hold values from -0.125 to 0.125
- w_up: bfloat16 [2560, 6912], P('dp', 'tensor'), may hold values from -0.125 to 0.125
- w_down: bfloat16 [6912, 2560], P('tensor', 'dp'), may hold values from -0.078125 to 0.078125
- out_grad: bfloat16 [16384, 2560], P(('dp', 'tensor')), may hold values from -6 to 6
Outputs:
- output: bfloat16 [16384, 2560], P(('dp', 'tensor'))
- input_grad: float32 [16384, 2560], P(('dp', 'tensor'))
- attn_gain_grad: float32 [2560], P(('dp', 'tensor'))
- w_query_grad: float32 [2560, 2560], P('dp', 'tensor')
- w_key_grad: float32 [2560, 640], P('dp', 'tensor')
- w_value_grad: float32 [2560, 640], P('dp', 'tensor')
- w_out_grad: float32 [2560, 2560], P('tensor', 'dp')
- mlp_gain_grad: float32 [2560], P(('dp', 'tensor'))
- w_gate_grad: float32 [2560, 6912], P('dp', 'tensor')
- w_up_grad: float32 [2560, 6912], P('dp', 'tensor')
- w_down_grad: float32 [6912, 2560], P('tensor', 'dp')
The draws below stay inside these ranges and needn't reach their ends.
Inputs may be any that keep to these rules, and one draw needn't show every extreme that they name: `segments`: in each sequence the segment numbers start at 0 and rise by one from document to document; padding, marked -1, fills only the end; each document has 60 to 800 tokens.
All inputs are finite; a program needn't handle non-finite values.
Results may differ from the reference program's by a relative error of at most 0.023.
Values may be sent and summed in bfloat16 or wider, within the bound.
No kernel may reach another device: no remote copies, remote signals or barrier semaphores. Data moves between devices by JAX's collectives and lax.ppermute only.
A program may use at most 320 MiB of HBM per device.

```python
import math
import jax
import jax.numpy as jnp
from jax import lax

D = 2560
HEADS = 32
KV = 8
HD = 80
FF = 6912
WINDOW = 4096
LEN = 1024
NSEQ = 16
TOKENS = 16384
DOC_MIN = 60
DOC_MAX = 800


def draw_segments(key, part):
    key = jax.random.fold_in(key, 7)
    doc_slots = LEN // DOC_MIN + 1
    lengths = jax.random.randint(key, (NSEQ, doc_slots), DOC_MIN, DOC_MAX + 1)
    chosen = jax.random.randint(jax.random.fold_in(key, 11), (), 0, NSEQ)
    rows = jnp.arange(NSEQ, dtype=jnp.int32)[:, None]
    lengths = jnp.where(rows == chosen, DOC_MIN, lengths)
    ends = jnp.cumsum(lengths, axis=1)
    places = jnp.arange(LEN, dtype=jnp.int32)
    doc_ids = jnp.sum((places[None, :, None] >= ends[:, None, :]).astype(jnp.int32), axis=2)
    doc_end = jnp.take_along_axis(ends, doc_ids, axis=1)
    return jnp.where(doc_end <= LEN, doc_ids, -1).astype(jnp.int32)


def steps_of(own_key, extent, shards, smallest, high):
    loudness, own = 1.0, jax.random.fold_in(own_key, 6)
    for axis_at, parts in shards:
        draws = jnp.exp(jax.random.uniform(jax.random.fold_in(own, axis_at), (parts,), jnp.float32, smallest / len(shards), high / len(shards)))
        loudness = loudness * jnp.repeat(draws, extent[axis_at] // parts).reshape([-1 if axis == axis_at else 1 for axis in range(len(extent))])
    return loudness


def scatter_about(key, extent, scale, bound, cuts=(), kind=jnp.bfloat16):
    entries = jax.random.normal(key, extent, jnp.float32) * scale
    if len(cuts) > 0:
        entries = steps_of(key, extent, cuts, -0.22, 0.18) * entries
    return jnp.clip(entries, min=-bound, max=bound).astype(kind)


def setup_inputs(seed: int = 0) -> dict:
    splits = jax.random.split(jax.random.key(seed), 13)
    return {
        "tokens": scatter_about(splits[0], (TOKENS, D), 1.0, 6.0, ((0, 32),)),
        "segments": draw_segments(jax.random.fold_in(splits[12], 71), 0),
        "attn_gain": jnp.clip(1.0 + 0.1 * jax.random.normal(splits[2], (D,), jnp.float32), 0.5, 1.5).astype(jnp.bfloat16),
        "w_query": scatter_about(splits[3], (D, HEADS * HD), D ** -0.5, 0.125, ((0, 8), (1, 4))),
        "w_key": scatter_about(splits[4], (D, KV * HD), D ** -0.5, 0.125, ((0, 8), (1, 4))),
        "w_value": scatter_about(splits[5], (D, KV * HD), D ** -0.5, 0.125, ((0, 8), (1, 4))),
        "w_out": scatter_about(splits[6], (HEADS * HD, D), (D // 64) ** -0.5, 1.0, ((0, 4), (1, 8))),
        "mlp_gain": jnp.clip(1.0 + 0.1 * jax.random.normal(splits[7], (D,), jnp.float32), 0.5, 1.5).astype(jnp.bfloat16),
        "w_gate": scatter_about(splits[8], (D, FF), D ** -0.5, 0.125, ((0, 8), (1, 4))),
        "w_up": scatter_about(splits[9], (D, FF), D ** -0.5, 0.125, ((0, 8), (1, 4))),
        "w_down": scatter_about(splits[10], (FF, D), FF ** -0.5, 0.078125, ((0, 4), (1, 8))),
        "out_grad": scatter_about(splits[11], (TOKENS, D), 1.0, 6.0, ((0, 32),)),
    }


EPS = 1e-05
THETA = 10000.0
NEG = -1e+30

@jax.custom_vjp
def low(v):
    return lax.optimization_barrier(v.astype(jnp.bfloat16)).astype(jnp.float32)

@jax.custom_vjp
def low_back(v):
    return v

def low_keep(v):
    return (low(v), None)

def low_pass(kept, grad):
    return (grad,)

def back_keep(v):
    return (v, None)

def back_low(kept, grad):
    return (low(grad),)
low.defvjp(low_keep, low_pass)
low_back.defvjp(back_keep, back_low)

def matmul(left, right):
    return jnp.dot(left, right, precision=lax.Precision.HIGHEST)

def scaled_norm(inputs, gain_row):
    return inputs * lax.rsqrt(lax.optimization_barrier(jnp.mean(inputs * inputs, axis=-1, keepdims=True)) + EPS) * gain_row

def doc_positions(seg_table):
    places = jnp.arange(seg_table.shape[-1], dtype=jnp.int32)
    previous = jnp.concatenate([seg_table[:, :1] - 1, seg_table[:, :-1]], axis=1)
    doc_start = lax.cummax(jnp.where(seg_table != previous, places[None, :], 0), axis=1)
    return places[None, :] - doc_start

def rope_tables(positions, head_size):
    half_width = head_size // 2
    frequency = THETA ** (-(jnp.arange(half_width, dtype=jnp.float32) * 2.0 / head_size))
    angles = positions.astype(jnp.float32)[..., None] * frequency
    return (jnp.cos(angles), jnp.sin(angles))

def rotate(inputs, cosine, sine_table):
    half_width = inputs.shape[-1] // 2
    first_half, second_half = (inputs[..., :half_width], inputs[..., half_width:])
    return jnp.concatenate([first_half * cosine - second_half * sine_table, second_half * cosine + first_half * sine_table], axis=-1)

def allowed(seg_row):
    places = jnp.arange(seg_row.shape[0], dtype=jnp.int32)
    causal = (places[None, :] <= places[:, None]) & (places[:, None] - places[None, :] < WINDOW)
    return causal & (seg_row[:, None] == seg_row[None, :])

def layer_block(block_in, block_segs, attn_gain, w_query, w_key, w_value, w_out, mlp_gain, w_gate, w_up, w_down):
    seq_count = block_segs.shape[0]
    groups = HEADS // KV
    normed_one = low(scaled_norm(block_in, attn_gain))
    queries = low_back(matmul(normed_one, w_query)).reshape(seq_count, LEN, KV, groups, HD)
    keys_raw = low_back(matmul(normed_one, w_key)).reshape(seq_count, LEN, KV, HD)
    values_raw = low_back(matmul(normed_one, w_value)).reshape(seq_count, LEN, KV, HD)
    cosine, sine_table = rope_tables(doc_positions(block_segs), HD)
    q_rot = low(rotate(queries, cosine[:, :, None, None, :], sine_table[:, :, None, None, :]))
    k_rot = low(rotate(keys_raw, cosine[:, :, None, :], sine_table[:, :, None, :]))
    v_low = low(values_raw)

    def attend(packed):
        q_seq, k_seq, v_seq, seg_seq = packed
        scores = low_back(jnp.einsum('qkgd,skd->kgqs', q_seq, k_seq, precision=lax.Precision.HIGHEST) * HD ** (-0.5))
        scores = jnp.where(allowed(seg_seq), scores, NEG)
        row_top = lax.optimization_barrier(jnp.max(scores, axis=-1, keepdims=True))
        exp_scores = jnp.exp(scores - row_top)
        soft_probs = exp_scores / lax.optimization_barrier(jnp.sum(exp_scores, axis=-1, keepdims=True))
        return jnp.einsum('kgqs,skd->qkgd', low(soft_probs), v_seq, precision=lax.Precision.HIGHEST)
    mixed_heads = lax.map(jax.checkpoint(attend), (q_rot, k_rot, v_low, block_segs))
    mixed_heads = low(low_back(mixed_heads.reshape(seq_count * LEN, HEADS * HD)))
    residual = block_in + low_back(matmul(mixed_heads, w_out))
    normed_two = low(scaled_norm(residual, mlp_gain))
    gate_part = low_back(matmul(normed_two, w_gate))
    up_part = low_back(matmul(normed_two, w_up))
    hidden = low(jax.nn.silu(gate_part) * up_part)
    return residual + matmul(hidden, w_down)

def reference(tokens, segments, attn_gain, w_query, w_key, w_value, w_out, mlp_gain, w_gate, w_up, w_down, out_grad):
    per_block = math.gcd(NSEQ, 4)
    blocks = NSEQ // per_block
    block_segs = segments.reshape(blocks, per_block, LEN)

    def forward(tokens_in, gain_one, query_w, key_w, value_w, out_w, gain_two, gate_w, up_w, down_w):

        def run_block(packed):
            return layer_block(packed[0], packed[1], gain_one, query_w, key_w, value_w, out_w, gain_two, gate_w, up_w, down_w)
        stacked = tokens_in.reshape(blocks, per_block * LEN, D)
        return lax.map(jax.checkpoint(run_block), (stacked, block_segs)).reshape(TOKENS, D)
    result, pullback = jax.vjp(forward, tokens.astype(jnp.float32), attn_gain.astype(jnp.float32), w_query.astype(jnp.float32), w_key.astype(jnp.float32), w_value.astype(jnp.float32), w_out.astype(jnp.float32), mlp_gain.astype(jnp.float32), w_gate.astype(jnp.float32), w_up.astype(jnp.float32), w_down.astype(jnp.float32))
    valid_rows = (segments.reshape(TOKENS) >= 0).astype(jnp.float32)
    gradients = pullback(out_grad.astype(jnp.float32) * valid_rows[:, None])
    return (result.astype(jnp.bfloat16), gradients[0], gradients[1], gradients[2], gradients[3], gradients[4], gradients[5], gradients[6], gradients[7], gradients[8], gradients[9])
```

```python
import functools

import jax
import jax.numpy as jnp
from jax import lax
from jax.experimental import pallas as pl
from jax.experimental.pallas import tpu as pltpu
from jax.sharding import PartitionSpec as P

HD = 80
LANES = 128
WINDOW = 4096
EPS = 1e-05
THETA = 10000.0
NEG = -1e30
LOG2E = 1.4426950408889634
BLK = 256
BF = jnp.bfloat16
F32 = jnp.float32


def turn(x, c, s):
    return x * c + pltpu.roll(x, LANES // 2, 1) * s


def turn_back(x, c, s):
    return x * c - pltpu.roll(x, LANES // 2, 1) * s


def allowed(start, first_row, rows, first_col, cols):
    row = first_row + lax.broadcasted_iota(jnp.int32, (rows, cols), 0)
    col = first_col + lax.broadcasted_iota(jnp.int32, (rows, cols), 1)
    return (col >= start) & (col <= row) & (row - col < WINDOW)


def nt(a, b):
    return lax.dot_general(a, b, (((1,), (1,)), ((), ())), preferred_element_type=F32)


def nn(a, b):
    return lax.dot_general(a, b, (((1,), (0,)), ((), ())), preferred_element_type=F32)


def tn(a, b):
    return lax.dot_general(a, b, (((0,), (0,)), ((), ())), preferred_element_type=F32)


def fwd_kernel(groups, scale, lo_ref, q_ref, k_ref, v_ref, c_ref, s_ref, start_ref,
               o_ref, qr_ref, kr_ref, vb_ref, lse_ref):
    length = q_ref.shape[0]
    c, s = c_ref[...], s_ref[...]
    kr_ref[...] = turn(k_ref[...], c, s).astype(BF)
    vb_ref[...] = v_ref[...].astype(BF)
    for g in range(groups):
        lanes = slice(g * LANES, (g + 1) * LANES)
        qr_ref[:, lanes] = turn(q_ref[:, lanes], c, s).astype(BF)
    for i in range(length // BLK):
        rows = slice(i * BLK, (i + 1) * BLK)
        for j in range(i + 1):
            cols = slice(j * BLK, (i + 1) * BLK)
            width = (i + 1 - j) * BLK

            @pl.when(lo_ref[i] == j)
            def _():
                ok = allowed(start_ref[rows, :], i * BLK, BLK, j * BLK, width)
                for g in range(groups):
                    lanes = slice(g * LANES, (g + 1) * LANES)
                    scores = nt(qr_ref[rows, lanes], kr_ref[cols, :]) * (scale * LOG2E)
                    scores = jnp.where(ok, scores, NEG)
                    top = jnp.max(scores, axis=1, keepdims=True)
                    e = jnp.exp2(scores - top)
                    total = jnp.sum(e, axis=1, keepdims=True)
                    mixed = nn(e.astype(BF), vb_ref[cols, :])
                    o_ref[rows, lanes] = (mixed / total).astype(BF)
                    lse_ref[rows, g:g + 1] = top + jnp.log2(total)


def bwd_kernel(groups, scale, lo_ref, qr_ref, kr_ref, vb_ref, do_ref, c_ref, s_ref, start_ref, lse_ref,
               dq_ref, dk_ref, dv_ref, dk_acc, dv_acc):
    length = qr_ref.shape[0]
    dk_acc[...] = jnp.zeros_like(dk_acc)
    dv_acc[...] = jnp.zeros_like(dv_acc)
    for i in range(length // BLK):
        rows = slice(i * BLK, (i + 1) * BLK)
        for j in range(i + 1):
            cols = slice(j * BLK, (i + 1) * BLK)
            width = (i + 1 - j) * BLK

            @pl.when(lo_ref[i] == j)
            def _():
                ok = allowed(start_ref[rows, :], i * BLK, BLK, j * BLK, width)
                for g in range(groups):
                    lanes = slice(g * LANES, (g + 1) * LANES)
                    q, do = qr_ref[rows, lanes], do_ref[rows, lanes]
                    k, v = kr_ref[cols, :], vb_ref[cols, :]
                    scores = nt(q, k) * (scale * LOG2E)
                    p = jnp.exp2(jnp.where(ok, scores, NEG) - lse_ref[rows, g:g + 1])
                    pd = p * nt(do, v)
                    ds = (pd - p * jnp.sum(pd, axis=1, keepdims=True)).astype(BF)
                    dq = nn(ds, k) * scale
                    dq_ref[rows, lanes] = turn_back(dq, c_ref[rows, :], s_ref[rows, :]).astype(BF)
                    dk_acc[cols, :] += tn(ds, q)
                    dv_acc[cols, :] += tn(p.astype(BF), do)
    dk_ref[...] = turn_back(dk_acc[...] * scale, c_ref[...], s_ref[...]).astype(BF)
    dv_ref[...] = dv_acc[...].astype(BF)


def attend(proj, tables, kv, groups):
    cos_t, sin_t, start, lo = tables
    rows = proj.shape[0]
    whole = lambda width: pl.BlockSpec((rows, width), lambda h, lo: (0, 0))
    at = lambda width, first: pl.BlockSpec((rows, width), lambda h, lo: (0, first + h))
    wide = groups * LANES
    out = lambda width: jax.ShapeDtypeStruct((rows, kv * width), BF)
    return pl.pallas_call(
        functools.partial(fwd_kernel, groups, HD ** -0.5),
        grid_spec=pltpu.PrefetchScalarGridSpec(
            num_scalar_prefetch=1,
            grid=(kv,),
            in_specs=[at(wide, 0), at(LANES, kv * groups), at(LANES, kv * groups + kv),
                      whole(LANES), whole(LANES), whole(1)],
            out_specs=[at(wide, 0), at(wide, 0), at(LANES, 0), at(LANES, 0),
                       pl.BlockSpec((None, rows, groups), lambda h, lo: (h, 0, 0))],
        ),
        out_shape=[out(wide), out(wide), out(LANES), out(LANES),
                   jax.ShapeDtypeStruct((kv, rows, groups), F32)],
        compiler_params=pltpu.CompilerParams(vmem_limit_bytes=48 * 2 ** 20),
        cost_estimate=pl.CostEstimate(flops=int(4 * kv * groups * rows * rows * LANES * 0.6),
                                      bytes_accessed=rows * kv * (groups + 1) * LANES * 10, transcendentals=0),
        name="attend",
    )(lo, proj, proj, proj, cos_t, sin_t, start)


def attend_back(qr, kr, vb, d_o, tables, lse, kv, groups):
    cos_t, sin_t, start, lo = tables
    rows = qr.shape[0]
    whole = lambda width: pl.BlockSpec((rows, width), lambda h, lo: (0, 0))
    at = lambda width: pl.BlockSpec((rows, width), lambda h, lo: (0, h))
    wide = groups * LANES
    out = lambda width: jax.ShapeDtypeStruct((rows, kv * width), BF)
    return pl.pallas_call(
        functools.partial(bwd_kernel, groups, HD ** -0.5),
        grid_spec=pltpu.PrefetchScalarGridSpec(
            num_scalar_prefetch=1,
            grid=(kv,),
            in_specs=[at(wide), at(LANES), at(LANES), at(wide), whole(LANES), whole(LANES), whole(1),
                      pl.BlockSpec((None, rows, groups), lambda h, lo: (h, 0, 0))],
            out_specs=[at(wide), at(LANES), at(LANES)],
            scratch_shapes=[pltpu.VMEM((rows, LANES), F32)] * 2,
        ),
        out_shape=[out(wide), out(LANES), out(LANES)],
        compiler_params=pltpu.CompilerParams(vmem_limit_bytes=48 * 2 ** 20),
        cost_estimate=pl.CostEstimate(flops=int(10 * kv * groups * rows * rows * LANES * 0.6),
                                      bytes_accessed=rows * kv * (groups + 1) * LANES * 10, transcendentals=0),
        name="attend_back",
    )(lo, qr, kr, vb, d_o, cos_t, sin_t, start, lse)


def doc_starts(seg_row):
    places = jnp.arange(seg_row.shape[0], dtype=jnp.int32)
    previous = jnp.concatenate([seg_row[:1] - 1, seg_row[:-1]])
    return lax.cummax(jnp.where(seg_row != previous, places, 0), axis=0)


def head_tables(positions):
    half = HD // 2
    freq = THETA ** (-(jnp.arange(half, dtype=F32) * 2.0 / HD))
    angles = positions.astype(F32)[:, None] * freq
    cosine, sine = jnp.cos(angles), jnp.sin(angles)
    gap = jnp.zeros((positions.shape[0], LANES // 2 - half), F32)
    return (jnp.concatenate([cosine, gap, cosine, gap], axis=1),
            jnp.concatenate([-sine, gap, sine, gap], axis=1))


def spread_matrix(heads):
    row = jnp.arange(heads * HD)
    feature = row % HD
    lane = (row // HD) * LANES + feature + jnp.where(feature >= HD // 2, LANES // 2 - HD // 2, 0)
    return (lane[:, None] == jnp.arange(heads * LANES)[None, :]).astype(BF)


def dot(a, b, out=BF):
    return jnp.dot(a, b, preferred_element_type=F32).astype(out)


def dot_t(a, b, out=BF):
    return lax.dot_general(a, b, (((0,), (0,)), ((), ())), preferred_element_type=F32).astype(out)


def dot_nt(a, b, out=BF):
    return lax.dot_general(a, b, (((1,), (1,)), ((), ())), preferred_element_type=F32).astype(out)


def inverse_rms(v):
    return lax.rsqrt(jnp.mean(v * v, axis=-1, keepdims=True) + EPS)


def norm_back(v, inv, gain, grad):
    scaled = grad * gain
    return inv * scaled - v * (inv * inv * inv * jnp.mean(scaled * v, axis=-1, keepdims=True))


def swap(v, bit):
    return lax.ppermute(v, "tensor", [(i, i ^ bit) for i in range(lax.axis_size("tensor"))])


def groups_of(size):
    return [[first + i for i in range(size)] for first in range(0, lax.axis_size("tensor"), size)]


def gather(mine, size):
    if size == 2:
        return [mine, swap(mine, 1)]
    if size == 4 and lax.axis_size("tensor") == 4:
        half = mine.shape[0] // 2
        from_x, from_y = swap(mine, 1), swap(mine, 2)
        return [mine, from_x, from_y, jnp.concatenate([swap(from_x[:half], 2), swap(from_y[half:], 1)])]
    blocks = lax.all_gather(mine, "tensor", axis=0, tiled=False, axis_index_groups=groups_of(size))
    at = lax.axis_index("tensor") % size
    return [lax.dynamic_index_in_dim(blocks, at ^ r, 0, keepdims=False) for r in range(size)]


def scatter(parts, size):
    if size == 2:
        return swap(parts[1], 1).astype(F32)
    if size == 4 and lax.axis_size("tensor") == 4:
        _, p_x, p_y, p_diag = parts
        half = p_x.shape[0] // 2
        add = lambda a, b: (a.astype(F32) + b.astype(F32)).astype(BF)
        for_y = swap(p_diag[:half], 1)
        for_x = swap(p_diag[half:], 2)
        a1, b1 = swap(p_x[:half], 1), swap(p_y[half:], 2)
        a2, b2 = swap(add(p_x[half:], for_x), 1), swap(add(p_y[:half], for_y), 2)
        low = a1.astype(F32) + b2.astype(F32)
        high = a2.astype(F32) + b1.astype(F32)
        return jnp.concatenate([low, high])
    at = lax.axis_index("tensor") % size
    blocks = jnp.stack([jnp.zeros_like(parts[1])] + list(parts[1:]))[jnp.arange(size) ^ at]
    summed = lax.psum_scatter(blocks, "tensor", scatter_dimension=0, tiled=False, axis_index_groups=groups_of(size))
    return summed.astype(F32)


def in_order(blocks):
    at = lax.axis_index("tensor") % len(blocks)
    if len(blocks) == 2:
        return by_place(at, *blocks)
    return jnp.stack(blocks)[jnp.arange(len(blocks)) ^ at].reshape(-1, *blocks[0].shape[1:])


def by_place(bit, mine, other):
    return jnp.where(bit == 0, jnp.concatenate([mine, other]), jnp.concatenate([other, mine]))


def body(tokens, segments, attn_gain, w_query, w_key, w_value, w_out, mlp_gain, w_gate, w_up, w_down, out_grad):
    q_width, k_width = w_query.shape[1], w_key.shape[1]
    heads, kv = q_width // HD, k_width // HD
    groups = heads // kv
    row_count, width = tokens.shape
    seq_count, length = segments.shape
    ff = w_gate.shape[1]
    place, places = lax.axis_index("tensor"), lax.axis_size("tensor")
    group = places // seq_count
    core = lax.axis_index("dp") % 2

    token_blocks = gather(tokens, group)
    dy_blocks = gather(out_grad, places)
    qkv_shard = jnp.concatenate(
        [w_query, w_key, w_value, attn_gain[:, None], mlp_gain[:, None]], axis=1)
    qkv_all = lax.all_gather(qkv_shard, "dp", axis=0, tiled=True)
    qkv_w = qkv_all[:, :q_width + 2 * k_width]
    gain_one = qkv_all[:, q_width + 2 * k_width].astype(F32)
    gain_two = qkv_all[:, q_width + 2 * k_width + 1].astype(F32)
    out_w = lax.all_gather(w_out, "dp", axis=1, tiled=True)
    gu_w = lax.all_gather(jnp.concatenate([w_gate, w_up], axis=1), "dp", axis=0, tiled=True)
    down_w = lax.all_gather(w_down, "dp", axis=1, tiled=True)

    def swap_shared(v, bit):
        half = v.shape[0] // 2
        got = swap(lax.dynamic_slice_in_dim(v, core * half, half, 0), bit)
        pair = lax.ppermute(got, "dp", [(i, i ^ 1) for i in range(lax.axis_size("dp"))])
        return by_place(core, got, pair)

    others = [group * m for m in range(1, seq_count)]
    qkv_ws = [qkv_w] + [swap_shared(qkv_w, bits) for bits in others]
    out_ws = [out_w] + [swap_shared(out_w, bits) for bits in others]

    seg_row = lax.dynamic_index_in_dim(segments, place // group, 0, keepdims=False)
    start = doc_starts(seg_row)
    cos_t, sin_t = head_tables(jnp.arange(length, dtype=jnp.int32) - start)
    tables = (cos_t, sin_t, start[:, None], start[::BLK] // BLK)

    spread_q, spread_k = spread_matrix(heads), spread_matrix(kv)

    def pad_heads(w):
        return jnp.concatenate([
            dot(w[:, :q_width], spread_q), dot(w[:, q_width:q_width + k_width], spread_k),
            dot(w[:, q_width + k_width:], spread_k)], axis=1)

    x_own = tokens.astype(F32)
    inv_own = inverse_rms(x_own)
    x_pair = in_order(token_blocks).astype(F32)
    inv_pair = inverse_rms(x_pair)
    n1 = (x_pair * inv_pair * gain_one).astype(BF)
    kept = []
    for w in qkv_ws:
        proj = dot(n1, pad_heads(w), F32)
        o, qr, kr, vb, lse = attend(proj, tables, kv, groups)
        kept.append((dot_nt(o, spread_q), qr, kr, vb, lse))
    o_flat = jnp.concatenate([k[0] for k in kept], axis=1)
    out_both = jnp.concatenate(out_ws, axis=0)

    def rows_of(v, bits):
        return lax.dynamic_slice_in_dim(v, ((place % group) ^ bits) * row_count, row_count, 0)

    branch = scatter([None] + [dot(rows_of(o_flat, bits), out_both) for bits in range(1, group)], group)
    h = x_own + dot(rows_of(o_flat, 0), out_both, F32) + branch

    inv_h = inverse_rms(h)
    n2 = (h * inv_h * gain_two).astype(BF)
    n2s = gather(n2, places)
    segs = segments.reshape(-1)

    def masked(v, bits):
        own = lax.dynamic_slice_in_dim(segs, (place ^ bits) * row_count, row_count, 0)
        return v * (own >= 0).astype(BF)[:, None]

    dys = [masked(block, bits) for bits, block in enumerate(dy_blocks)]
    hiddens, gu_grads = [], []
    for n2_c, dy_c in zip(n2s, dys):
        gate_up = dot(n2_c, gu_w, F32)
        d_hidden = dot_nt(dy_c, down_w, F32)
        gate, up = gate_up[:, :ff], gate_up[:, ff:]
        sig = jax.nn.sigmoid(gate)
        act = gate * sig
        hiddens.append((act * up).astype(BF))
        gu_grads.append(jnp.concatenate(
            [(d_hidden * up * sig * (1.0 + gate * (1.0 - sig))).astype(BF), (d_hidden * act).astype(BF)], axis=1))
    d_n2 = scatter([None] + [dot_nt(g, gu_w) for g in gu_grads[1:]], places) + dot_nt(gu_grads[0], gu_w, F32)

    hidden_all, gu_grad_all = jnp.concatenate(hiddens), jnp.concatenate(gu_grads)
    n2_all, dy_all = jnp.concatenate(n2s), jnp.concatenate(dys)
    down_grad = lax.psum_scatter(dot_t(hidden_all, dy_all), "dp", scatter_dimension=1, tiled=True)
    gu_grad = lax.psum_scatter(dot_t(n2_all, gu_grad_all), "dp", scatter_dimension=0, tiled=True)
    mlp = scatter([None] + [dot(v, down_w) for v in hiddens[1:]], places) + dot(hiddens[0], down_w, F32)
    output = (h + mlp).astype(BF)

    gain_two_grad = jnp.sum(d_n2 * h * inv_h, axis=0)
    dh = dys[0].astype(F32) + norm_back(h, inv_h, gain_two, d_n2)

    dhb = dh.astype(BF)
    dhb_pair = in_order(gather(dhb, group))
    back, wgrads = [], []
    for (o, qr, kr, vb, lse), w, w_o in zip(kept[::-1], qkv_ws[::-1], out_ws[::-1]):
        d_o = dot(dot_nt(dhb_pair, w_o), spread_q)
        dq, dk, dv = attend_back(qr, kr, vb, d_o, tables, lse, kv, groups)
        d_proj = jnp.concatenate([dot_nt(dq, spread_q), dot_nt(dk, spread_k), dot_nt(dv, spread_k)], axis=1)
        back.append((d_proj, w))
        wgrads.append((dot_t(n1, d_proj), dot_t(o, dhb_pair)))

    def add_shares(shares):
        total = shares[-1].astype(F32)
        for bits, share in zip(others[::-1], shares):
            total += swap(share, bits).astype(F32)
        return total.astype(BF)

    qkv_grad = lax.psum_scatter(add_shares([g[0] for g in wgrads]), "dp", scatter_dimension=0, tiled=True).astype(F32)
    out_grad_w = lax.psum_scatter(add_shares([g[1] for g in wgrads]), "dp", scatter_dimension=1, tiled=True).astype(F32)

    d_n1_pair = sum(dot_nt(d, w, F32) for d, w in back)
    gain_one_grad = jnp.sum(d_n1_pair * x_pair * inv_pair, axis=0)
    d_n1 = rows_of(d_n1_pair, 0) + scatter(
        [None] + [rows_of(d_n1_pair, bits).astype(BF) for bits in range(1, group)], group)
    input_grad = dh + norm_back(x_own, inv_own, gain_one, d_n1)

    gains = lax.psum_scatter(jnp.stack([gain_one_grad, gain_two_grad], axis=1), ("dp", "tensor"),
                             scatter_dimension=0, tiled=True)
    return (
        output,
        input_grad,
        gains[:, 0],
        qkv_grad[:, :q_width],
        qkv_grad[:, q_width:q_width + k_width],
        qkv_grad[:, q_width + k_width:],
        out_grad_w,
        gains[:, 1],
        gu_grad[:, :ff].astype(F32),
        gu_grad[:, ff:].astype(F32),
        down_grad.astype(F32),
    )


def solution(mesh):
    rows, weight_in, weight_out = P(("dp", "tensor"), None), P("dp", "tensor"), P("tensor", "dp")
    in_specs = (rows, P("dp", None), P("dp"), weight_in, weight_in, weight_in, weight_out, P("dp"),
                weight_in, weight_in, weight_out, rows)
    gain = P(("dp", "tensor"))
    out_specs = (rows, rows, gain, weight_in, weight_in, weight_in, weight_out, gain, weight_in, weight_in, weight_out)
    return jax.shard_map(body, mesh=mesh, in_specs=in_specs, out_specs=out_specs, check_vma=False)
```

```python
import functools

import jax
import jax.numpy as jnp
from jax import lax
from jax.experimental import pallas as pl
from jax.experimental.pallas import tpu as pltpu
from jax.sharding import PartitionSpec as P

HD = 80
LANES = 128
WINDOW = 4096
EPS = 1e-05
THETA = 10000.0
NEG = -1e30
LOG2E = 1.4426950408889634
BLK = 256
BF = jnp.bfloat16
F32 = jnp.float32


def turn(x, c, s):
    return x * c + pltpu.roll(x, LANES // 2, 1) * s


def turn_back(x, c, s):
    return x * c - pltpu.roll(x, LANES // 2, 1) * s


def allowed(start, first_row, rows, first_col, cols):
    row = first_row + lax.broadcasted_iota(jnp.int32, (rows, cols), 0)
    col = first_col + lax.broadcasted_iota(jnp.int32, (rows, cols), 1)
    return (col >= start) & (col <= row) & (row - col < WINDOW)


def nt(a, b):
    return lax.dot_general(a, b, (((1,), (1,)), ((), ())), preferred_element_type=F32)


def nn(a, b):
    return lax.dot_general(a, b, (((1,), (0,)), ((), ())), preferred_element_type=F32)


def tn(a, b):
    return lax.dot_general(a, b, (((0,), (0,)), ((), ())), preferred_element_type=F32)


def fwd_kernel(groups, scale, lo_ref, qr_ref, kr_ref, vb_ref, start_ref, o_ref, lse_ref):
    length = qr_ref.shape[0]
    for i in range(length // BLK):
        rows = slice(i * BLK, (i + 1) * BLK)
        for j in range(i + 1):
            cols = slice(j * BLK, (i + 1) * BLK)
            width = (i + 1 - j) * BLK

            @pl.when(lo_ref[i] == j)
            def _():
                ok = allowed(start_ref[rows, :], i * BLK, BLK, j * BLK, width)
                for g in range(groups):
                    lanes = slice(g * LANES, (g + 1) * LANES)
                    scores = nt(qr_ref[rows, lanes], kr_ref[cols, :]) * (scale * LOG2E)
                    scores = jnp.where(ok, scores, NEG)
                    top = jnp.max(scores, axis=1, keepdims=True)
                    e = jnp.exp2(scores - top)
                    total = jnp.sum(e, axis=1, keepdims=True)
                    mixed = nn(e.astype(BF), vb_ref[cols, :])
                    o_ref[rows, lanes] = (mixed / total).astype(BF)
                    lse_ref[rows, g:g + 1] = top + jnp.log2(total)


def bwd_kernel(groups, scale, lo_ref, qr_ref, kr_ref, vb_ref, do_ref, c_ref, s_ref, start_ref, lse_ref,
               dq_ref, dk_ref, dv_ref, dk_acc, dv_acc):
    length = qr_ref.shape[0]
    dk_acc[...] = jnp.zeros_like(dk_acc)
    dv_acc[...] = jnp.zeros_like(dv_acc)
    for i in range(length // BLK):
        rows = slice(i * BLK, (i + 1) * BLK)
        for j in range(i + 1):
            cols = slice(j * BLK, (i + 1) * BLK)
            width = (i + 1 - j) * BLK

            @pl.when(lo_ref[i] == j)
            def _():
                ok = allowed(start_ref[rows, :], i * BLK, BLK, j * BLK, width)
                for g in range(groups):
                    lanes = slice(g * LANES, (g + 1) * LANES)
                    q, do = qr_ref[rows, lanes], do_ref[rows, lanes]
                    k, v = kr_ref[cols, :], vb_ref[cols, :]
                    scores = nt(q, k) * (scale * LOG2E)
                    p = jnp.exp2(jnp.where(ok, scores, NEG) - lse_ref[rows, g:g + 1])
                    pd = p * nt(do, v)
                    ds = (pd - p * jnp.sum(pd, axis=1, keepdims=True)).astype(BF)
                    dq = nn(ds, k) * scale
                    dq_ref[rows, lanes] = turn_back(dq, c_ref[rows, :], s_ref[rows, :]).astype(BF)
                    dk_acc[cols, :] += tn(ds, q)
                    dv_acc[cols, :] += tn(p.astype(BF), do)
    dk_ref[...] = turn_back(dk_acc[...] * scale, c_ref[...], s_ref[...]).astype(BF)
    dv_ref[...] = dv_acc[...].astype(BF)


def attend(proj, tables, kv, groups):
    start, lo = tables[2:]
    rows = proj.shape[0]
    at = lambda width, first: pl.BlockSpec((rows, width), lambda h, lo: (0, first + h))
    wide = groups * LANES
    return pl.pallas_call(
        functools.partial(fwd_kernel, groups, HD ** -0.5),
        grid_spec=pltpu.PrefetchScalarGridSpec(
            num_scalar_prefetch=1,
            grid=(kv,),
            in_specs=[at(wide, 0), at(LANES, kv * groups), at(LANES, kv * groups + kv),
                      pl.BlockSpec((rows, 1), lambda h, lo: (0, 0))],
            out_specs=[at(wide, 0), pl.BlockSpec((None, rows, groups), lambda h, lo: (h, 0, 0))],
        ),
        out_shape=[jax.ShapeDtypeStruct((rows, kv * wide), BF), jax.ShapeDtypeStruct((kv, rows, groups), F32)],
        compiler_params=pltpu.CompilerParams(vmem_limit_bytes=48 * 2 ** 20),
        cost_estimate=cost(4 * kv * groups * rows * rows * LANES), name="attend",
    )(lo, proj, proj, proj, start)


def attend_back(proj, d_o, tables, lse, kv, groups):
    cos_t, sin_t, start, lo = tables
    rows = proj.shape[0]
    whole = lambda width: pl.BlockSpec((rows, width), lambda h, lo: (0, 0))
    at = lambda width, first=0: pl.BlockSpec((rows, width), lambda h, lo: (0, first + h))
    wide = groups * LANES
    out = lambda width: jax.ShapeDtypeStruct((rows, kv * width), BF)
    return pl.pallas_call(
        functools.partial(bwd_kernel, groups, HD ** -0.5),
        grid_spec=pltpu.PrefetchScalarGridSpec(
            num_scalar_prefetch=1,
            grid=(kv,),
            in_specs=[at(wide), at(LANES, kv * groups), at(LANES, kv * groups + kv), at(wide), whole(LANES), whole(LANES), whole(1),
                      pl.BlockSpec((None, rows, groups), lambda h, lo: (h, 0, 0))],
            out_specs=[at(wide), at(LANES), at(LANES)],
            scratch_shapes=[pltpu.VMEM((rows, LANES), F32)] * 2,
        ),
        out_shape=[out(wide), out(LANES), out(LANES)],
        compiler_params=pltpu.CompilerParams(vmem_limit_bytes=48 * 2 ** 20),
        cost_estimate=cost(10 * kv * groups * rows * rows * LANES),
        name="attend_back",
    )(lo, proj, proj, proj, d_o, cos_t, sin_t, start, lse)


COLS = 256


def cost(flops):
    return pl.CostEstimate(flops=flops, bytes_accessed=0, transcendentals=0)


def params():
    return pltpu.CompilerParams(vmem_limit_bytes=56 * 2 ** 20)


def project_kernel(heads, kv, n1_ref, w_ref, eq_ref, ek_ref, c_ref, s_ref, out_ref):
    c, s = c_ref[...], s_ref[...]
    q_width = heads * HD
    step = pl.program_id(0)

    def go(w, spread, turned, width):
        padded = nn(w, spread).astype(BF)
        proj = nn(n1_ref[...], padded)
        for h in range(width):
            lanes = slice(h * LANES, (h + 1) * LANES)
            head = proj[:, lanes]
            out_ref[:, lanes] = (turn(head, c, s) if h < turned else head).astype(BF)

    per = 2 * kv

    @pl.when(step < heads // per)
    def _():
        go(w_ref[:, :q_width], eq_ref[...], per, per)

    @pl.when(step == heads // per)
    def _():
        go(w_ref[:, q_width:], ek_ref[...], kv, per)


def project(n1, w, tables, heads, kv):
    cos_t, sin_t = tables[:2]
    rows, d = n1.shape
    per = 2 * kv
    steps = heads // per + 1
    whole = lambda shape: pl.BlockSpec(shape, lambda i: (0, 0))
    e_k = spread_matrix(2 * kv)
    return pl.pallas_call(
        functools.partial(project_kernel, heads, kv),
        grid=(steps,),
        in_specs=[whole((rows, d)), whole(w.shape),
                  pl.BlockSpec((heads * HD, per * LANES), lambda i: (0, jnp.minimum(i, heads // per - 1))),
                  whole(e_k.shape), whole(cos_t.shape), whole(sin_t.shape)],
        out_specs=pl.BlockSpec((rows, per * LANES), lambda i: (0, i)),
        out_shape=jax.ShapeDtypeStruct((rows, steps * per * LANES), BF),
        compiler_params=params(), cost_estimate=cost(2 * rows * d * steps * per * LANES), name="project",
    )(n1, w, spread_matrix(heads), e_k, cos_t, sin_t)


def gate_up_kernel(sizes, *refs):
    n2_refs, (wg_ref, wu_ref), outs = refs[:-3 * len(sizes) - 2], refs[-3 * len(sizes) - 2:-3 * len(sizes)], refs[-3 * len(sizes):]
    n2_refs = list(n2_refs)
    for i, pieces in enumerate(sizes):
        at = 0
        for rows in pieces:
            a = n2_refs.pop(0)[...]
            gate, up = nn(a, wg_ref[...]), nn(a, wu_ref[...])
            here = slice(at, at + rows)
            outs[3 * i][here, :] = gate.astype(BF)
            outs[3 * i + 1][here, :] = up.astype(BF)
            outs[3 * i + 2][here, :] = (gate / (1.0 + jnp.exp(-gate)) * up).astype(BF)
            at += rows


def gate_up(blocks, w_gate, w_up):
    sizes = [[p.shape[0] for p in pieces] for pieces in blocks]
    flat = [p for pieces in blocks for p in pieces]
    d, ff = w_gate.shape
    tile = lambda size: pl.BlockSpec((size, COLS), lambda i: (0, i))
    outs = pl.pallas_call(
        functools.partial(gate_up_kernel, sizes),
        grid=(pl.cdiv(ff, COLS),),
        in_specs=[pl.BlockSpec(p.shape, lambda i: (0, 0)) for p in flat] + [tile(d)] * 2,
        out_specs=[tile(sum(pieces)) for pieces in sizes for _ in range(3)],
        out_shape=[jax.ShapeDtypeStruct((sum(pieces), ff), BF) for pieces in sizes for _ in range(3)],
        compiler_params=params(), cost_estimate=cost(4 * sum(map(sum, sizes)) * d * ff), name="gate_up",
    )(*flat, w_gate, w_up)
    return [outs[3 * i:3 * i + 3] for i in range(len(blocks))]


def gate_up_back_kernel(ff, dy_ref, g_ref, u_ref, wg_ref, wu_ref, wd_ref, dg_ref, du_ref, *p_refs_acc):
    *p_refs, acc = p_refs_acc
    step, last = pl.program_id(0), pl.num_programs(0) - 1
    d_hidden = nn(dy_ref[...], wd_ref[...])
    gate, up = g_ref[...].astype(F32), u_ref[...].astype(F32)
    sig = 1.0 / (1.0 + jnp.exp(-gate))
    act = gate * sig
    d_gate = (d_hidden * up * (sig + act * (1.0 - sig))).astype(BF)
    d_up = (d_hidden * act).astype(BF)
    dg_ref[...] = d_gate
    du_ref[...] = d_up

    @pl.when(step == 0)
    def _():
        acc[...] = jnp.zeros_like(acc)

    @pl.when(step < last)
    def _():
        acc[...] += nt(d_gate, wg_ref[...]) + nt(d_up, wu_ref[...])

    @pl.when(step == last)
    def _():
        def inside(v):
            col = last * COLS + lax.broadcasted_iota(jnp.int32, v.shape, 1)
            return jnp.where(col < ff, v, jnp.zeros_like(v))

        total = acc[...] + nt(inside(d_gate), inside(wg_ref[...])) + nt(inside(d_up), inside(wu_ref[...]))
        size = total.shape[0] // len(p_refs)
        for i, p_ref in enumerate(p_refs):
            p_ref[...] = total[i * size:(i + 1) * size].astype(p_ref.dtype)


def gate_up_back(dy, gate, up, w_gate, w_up, w_down_t, out, parts):
    (rows, d), ff = dy.shape, w_gate.shape[1]
    tile = lambda size: pl.BlockSpec((size, COLS), lambda i: (0, i))
    whole = pl.BlockSpec((rows, d), lambda i: (0, 0))
    return pl.pallas_call(
        functools.partial(gate_up_back_kernel, ff),
        grid=(pl.cdiv(ff, COLS),),
        in_specs=[whole, tile(rows), tile(rows), tile(d), tile(d), tile(d)],
        out_specs=[tile(rows)] * 2 + [pl.BlockSpec((rows // parts, d), lambda i: (0, 0))] * parts,
        out_shape=[jax.ShapeDtypeStruct((rows, ff), BF)] * 2 + [jax.ShapeDtypeStruct((rows // parts, d), out)] * parts,
        scratch_shapes=[pltpu.VMEM((rows, d), F32)],
        compiler_params=params(), cost_estimate=cost(6 * rows * d * ff), name="gate_up_back",
    )(dy, gate, up, w_gate, w_up, w_down_t)


def down_kernel(h_ref, w_ref, *out_refs):
    out = nt(h_ref[...], w_ref[...])
    size = out.shape[0] // len(out_refs)
    for i, out_ref in enumerate(out_refs):
        out_ref[...] = out[i * size:(i + 1) * size].astype(out_ref.dtype)


def down(hidden, w_down_t, parts):
    (rows, ff), d = hidden.shape, w_down_t.shape[0]
    size = 512
    return pl.pallas_call(
        down_kernel,
        grid=(pl.cdiv(d, size),),
        in_specs=[pl.BlockSpec((rows, ff), lambda i: (0, 0)), pl.BlockSpec((size, ff), lambda i: (i, 0))],
        out_specs=[pl.BlockSpec((rows // parts, size), lambda i: (0, i))] * parts,
        out_shape=[jax.ShapeDtypeStruct((rows // parts, d), BF)] * parts,
        compiler_params=params(), cost_estimate=cost(2 * rows * d * ff), name="down",
    )(hidden, w_down_t)


def wgrad_kernel(n, lists, *refs):
    a_refs, b_refs = refs[:n], list(refs[n:n + sum(map(len, lists))])
    outs, a_t = refs[n + len(b_refs):-1], refs[-1]

    @pl.when(pl.program_id(0) == 0)
    def _():
        at = 0
        for a_ref in a_refs:
            a_t[:, at:at + a_ref.shape[0]] = a_ref[...].T
            at += a_ref.shape[0]

    for j, sizes in enumerate(lists):
        total, at = None, 0
        for rows in sizes:
            part = nn(a_t[:, at:at + rows], b_refs.pop(0)[...])
            total = part if total is None else total + part
            at += rows
        outs[j][...] = total.astype(BF)


def wgrad(a_blocks, *b_lists):
    d, ff = a_blocks[0].shape[1], b_lists[0][0].shape[1]
    total = sum(a.shape[0] for a in a_blocks)
    lists = [[b.shape[0] for b in bs] for bs in b_lists]
    tile = lambda size: pl.BlockSpec((size, COLS), lambda i: (0, i))
    return pl.pallas_call(
        functools.partial(wgrad_kernel, len(a_blocks), lists),
        grid=(pl.cdiv(ff, COLS),),
        in_specs=[pl.BlockSpec(a.shape, lambda i: (0, 0), pipeline_mode=pl.Buffered(1)) for a in a_blocks]
        + [tile(b.shape[0]) for bs in b_lists for b in bs],
        out_specs=[tile(d)] * len(b_lists),
        out_shape=[jax.ShapeDtypeStruct((d, ff), BF)] * len(b_lists),
        scratch_shapes=[pltpu.VMEM((d, total), BF)],
        compiler_params=params(), cost_estimate=cost(2 * total * d * ff * len(b_lists)), name="wgrad",
    )(*a_blocks, *[b for bs in b_lists for b in bs])


def doc_starts(seg_row):
    places = jnp.arange(seg_row.shape[0], dtype=jnp.int32)
    previous = jnp.concatenate([seg_row[:1] - 1, seg_row[:-1]])
    return lax.cummax(jnp.where(seg_row != previous, places, 0), axis=0)


def head_tables(positions):
    half = HD // 2
    freq = THETA ** (-(jnp.arange(half, dtype=F32) * 2.0 / HD))
    angles = positions.astype(F32)[:, None] * freq
    cosine, sine = jnp.cos(angles), jnp.sin(angles)
    gap = jnp.zeros((positions.shape[0], LANES // 2 - half), F32)
    return (jnp.concatenate([cosine, gap, cosine, gap], axis=1),
            jnp.concatenate([-sine, gap, sine, gap], axis=1))


def spread_matrix(heads):
    row = jnp.arange(heads * HD)
    feature = row % HD
    lane = (row // HD) * LANES + feature + jnp.where(feature >= HD // 2, LANES // 2 - HD // 2, 0)
    return (lane[:, None] == jnp.arange(heads * LANES)[None, :]).astype(BF)


def dot(a, b, out=BF):
    return jnp.dot(a, b, preferred_element_type=F32).astype(out)


def dot_t(a, b, out=BF):
    return lax.dot_general(a, b, (((0,), (0,)), ((), ())), preferred_element_type=F32).astype(out)


def dot_nt(a, b, out=BF):
    return lax.dot_general(a, b, (((1,), (1,)), ((), ())), preferred_element_type=F32).astype(out)


def inverse_rms(v):
    return lax.rsqrt(jnp.mean(v * v, axis=-1, keepdims=True) + EPS)


def norm_back(v, inv, gain, grad):
    scaled = grad * gain
    return inv * scaled - v * (inv * inv * inv * jnp.mean(scaled * v, axis=-1, keepdims=True))


def swap(v, bit):
    return lax.ppermute(v, "tensor", [(i, i ^ bit) for i in range(lax.axis_size("tensor"))])


def groups_of(size):
    return [[first + i for i in range(size)] for first in range(0, lax.axis_size("tensor"), size)]


def after(v, *done):
    return lax.optimization_barrier((v, *done))[0]


def square(size):
    return size == 4 == lax.axis_size("tensor")


def gather(mine, size):
    if size == 2:
        return [[mine], [swap(mine, 1)]]
    if square(size):
        half = mine.shape[0] // 2
        from_x, from_y = swap(mine, 1), swap(mine, 2)
        return [[mine], [from_x], [from_y], [swap(from_x[:half], 2), swap(from_y[half:], 1)]]
    blocks = lax.all_gather(mine, "tensor", axis=0, tiled=False, axis_index_groups=groups_of(size))
    at = lax.axis_index("tensor") % size
    return [[lax.dynamic_index_in_dim(blocks, at ^ r, 0, keepdims=False)] for r in range(size)]


def scatter(parts, size):
    if size == 2:
        got = swap(jnp.concatenate(parts[1]), 1)
        return got.astype(F32), parts[1]
    if square(size):
        _, (x_low, x_high), (y_low, y_high), (d_low, d_high) = parts
        add = lambda a, b: (a.astype(F32) + b.astype(F32)).astype(BF)
        for_y, for_x = swap(d_low, 1), swap(d_high, 2)
        a1, b1 = swap(x_low, 1), swap(y_high, 2)
        x_high, y_low = add(x_high, for_x), add(y_low, for_y)
        a2, b2 = swap(x_high, 1), swap(y_low, 2)
        low = a1.astype(F32) + b2.astype(F32)
        high = a2.astype(F32) + b1.astype(F32)
        return jnp.concatenate([low, high]), [x_high, y_low]
    at = lax.axis_index("tensor") % size
    whole = [jnp.concatenate(p) for p in parts[1:]]
    blocks = jnp.stack([jnp.zeros_like(whole[0])] + whole)[jnp.arange(size) ^ at]
    summed = lax.psum_scatter(blocks, "tensor", scatter_dimension=0, tiled=False, axis_index_groups=groups_of(size))
    return summed.astype(F32), whole


def scatter_rows(v):
    for axis in ("dp", "tensor"):
        size, at = lax.axis_size(axis), lax.axis_index(axis)
        assert size & (size - 1) == 0
        while size > 1:
            size //= 2
            bit = (at // size) % 2
            low, high = jnp.split(v, 2)
            theirs = lax.ppermute(jnp.where(bit == 0, high, low), axis,
                                  [(i, i ^ size) for i in range(lax.axis_size(axis))])
            v = jnp.where(bit == 0, low, high) + theirs
    return v


def in_order(blocks):
    blocks = [pieces[0] for pieces in blocks]
    at = lax.axis_index("tensor") % len(blocks)
    if len(blocks) == 2:
        return by_place(at, *blocks)
    return jnp.stack(blocks)[jnp.arange(len(blocks)) ^ at].reshape(-1, *blocks[0].shape[1:])


def by_place(bit, mine, other):
    return jnp.where(bit == 0, jnp.concatenate([mine, other]), jnp.concatenate([other, mine]))


def body(tokens, segments, attn_gain, w_query, w_key, w_value, w_out, mlp_gain, w_gate, w_up, w_down, out_grad):
    q_width, k_width = w_query.shape[1], w_key.shape[1]
    heads, kv = q_width // HD, k_width // HD
    groups = heads // kv
    row_count, width = tokens.shape
    seq_count, length = segments.shape
    ff = w_gate.shape[1]
    place, places = lax.axis_index("tensor"), lax.axis_size("tensor")
    group = places // seq_count
    core = lax.axis_index("dp") % 2

    token_blocks = gather(tokens, group)
    if square(places):
        dy_y = swap(out_grad, 2)
    qkv_shard = jnp.concatenate(
        [w_query, w_key, w_value, attn_gain[:, None], mlp_gain[:, None]], axis=1)
    qkv_all = lax.all_gather(qkv_shard, "dp", axis=0, tiled=True)
    if square(places):
        qkv_all, token_blocks, dy_y, later = lax.optimization_barrier((qkv_all, token_blocks, dy_y, out_grad))
        dy_x = swap(later, 1)
        dy_blocks = [out_grad, dy_x, dy_y, swap(dy_x, 2)]
    else:
        dy_blocks = [pieces[0] for pieces in gather(out_grad, places)]
    qkv_w = qkv_all[:, :q_width + 2 * k_width]
    gain_one = qkv_all[:, q_width + 2 * k_width].astype(F32)
    gain_two = qkv_all[:, q_width + 2 * k_width + 1].astype(F32)
    out_w = lax.all_gather(after(w_out, qkv_all), "dp", axis=1, tiled=True)
    gate_w = lax.all_gather(after(w_gate, qkv_all), "dp", axis=0, tiled=True)
    up_w = lax.all_gather(after(w_up, qkv_all), "dp", axis=0, tiled=True)
    down_wt = lax.all_gather(after(w_down.T, out_w), "dp", axis=0, tiled=True)

    def swap_shared(v, bit):
        half = v.shape[0] // 2
        got = swap(lax.dynamic_slice_in_dim(v, core * half, half, 0), bit)
        pair = lax.ppermute(got, "dp", [(i, i ^ 1) for i in range(lax.axis_size("dp"))])
        return by_place(core, got, pair)

    others = [group * m for m in range(1, seq_count)]
    qkv_ws = [qkv_w] + [swap_shared(qkv_w, bits) for bits in others]
    out_ws = [out_w] + [swap_shared(out_w, bits) for bits in others]

    def share(part, bits):
        half = part.shape[0] // 2
        theirs = lax.dynamic_slice_in_dim(part, (1 - core) * half, half, 0)
        theirs = lax.ppermute(theirs, "dp", [(i, i ^ 1) for i in range(lax.axis_size("dp"))])
        mine = lax.dynamic_slice_in_dim(part, core * half, half, 0)
        return swap((mine.astype(F32) + theirs.astype(F32)).astype(BF), bits)

    seg_row = lax.dynamic_index_in_dim(segments, place // group, 0, keepdims=False)
    start = doc_starts(seg_row)
    cos_t, sin_t = head_tables(jnp.arange(length, dtype=jnp.int32) - start)
    tables = (cos_t, sin_t, start[:, None], start[::BLK] // BLK)

    spread_q, spread_k = spread_matrix(heads), spread_matrix(kv)

    x_own = tokens.astype(F32)
    inv_own = inverse_rms(x_own)
    x_pair = in_order(token_blocks).astype(F32)
    inv_pair = inverse_rms(x_pair)
    n1 = (x_pair * inv_pair * gain_one).astype(BF)
    kept = []
    for w in qkv_ws:
        if kept:
            w = after(w, kept[0][0])
        proj = project(n1, w, tables, heads, kv)
        o, lse = attend(proj, tables, kv, groups)
        kept.append((dot_nt(o, spread_q), proj, lse))
    o_flat = jnp.concatenate([k[0] for k in kept], axis=1)
    out_both = jnp.concatenate(out_ws, axis=0)

    def rows_of(v, bits):
        return lax.dynamic_slice_in_dim(v, ((place % group) ^ bits) * row_count, row_count, 0)

    branch, _ = scatter([None] + [[dot(rows_of(o_flat, bits), out_both)] for bits in range(1, group)], group)
    branch, dy_blocks = lax.optimization_barrier((branch, dy_blocks))
    h = x_own + dot(rows_of(o_flat, 0), out_both, F32) + branch

    inv_h = inverse_rms(h)
    n2 = (h * inv_h * gain_two).astype(BF)
    n2s = gather(after(n2, gate_w, up_w), places)
    segs = segments.reshape(-1)

    def masked(v, bits):
        own = lax.dynamic_slice_in_dim(segs, (place ^ bits) * row_count, row_count, 0)
        return v * (own >= 0).astype(BF)[:, None]

    dys = [masked(block, bits) for bits, block in enumerate(dy_blocks)]
    ups = gate_up(n2s[:1], gate_w, up_w)
    ups += gate_up(after(n2s[1:places - 1], ups[0]), gate_w, up_w)
    ups += gate_up(after(n2s[places - 1:], ups[1], down_wt), gate_w, up_w)
    n2_pieces = [p for pieces in n2s for p in pieces]
    hiddens = [u[2] for u in ups]
    down_part, = wgrad(dys, hiddens)
    down_grad = lax.psum_scatter(down_part, "dp", scatter_dimension=0, tiled=True)
    backs, last = [None] * places, down_part
    for r in reversed(range(places)):
        backs[r] = gate_up_back(after(dys[r], last), ups[r][0], ups[r][1], gate_w, up_w, down_wt,
                                *((BF, 2) if r else (F32, 1)))
        last = backs[r][2]
    d_n2, sent = scatter([v[2:] for v in backs], places)
    d_n2 += backs[0][2]
    gate_part, up_part = wgrad(after(n2_pieces, last, sent), [v[0] for v in backs], [v[1] for v in backs])
    gate_grad = lax.psum_scatter(gate_part, "dp", scatter_dimension=0, tiled=True)
    up_grad = lax.psum_scatter(up_part, "dp", scatter_dimension=0, tiled=True)

    gain_two_grad = jnp.sum(d_n2 * h * inv_h, axis=0)
    dh = dys[0].astype(F32) + norm_back(h, inv_h, gain_two, d_n2)

    dhb = dh.astype(BF)
    hiddens = after(hiddens, dhb)
    mlp_parts = [down(v, down_wt, 2 if r else 1) for r, v in enumerate(hiddens)]
    dhb_pair = in_order(after(gather(dhb, group), mlp_parts, down_grad))
    output = (h + scatter(after(mlp_parts, dhb_pair), places)[0] + mlp_parts[0][0].astype(F32)).astype(BF)
    back, shares = [], []
    for index in reversed(range(len(kept))):
        (o, proj, lse), w, w_o = kept[index], qkv_ws[index], out_ws[index]
        out_part = dot_t(dhb_pair, o)
        d_o = dot(dot_nt(dhb_pair, w_o), spread_q)
        dq, dk, dv = attend_back(proj, d_o, tables, lse, kv, groups)
        d_proj = jnp.concatenate([dot_nt(dq, spread_q), dot_nt(dk, spread_k), dot_nt(dv, spread_k)], axis=1)
        qkv_part = dot_t(n1, d_proj)
        if index:
            shares.append((share(qkv_part, others[index - 1]), share(out_part, others[index - 1])))
            dhb_pair = after(dhb_pair, qkv_part, out_part)
        back.append((d_proj, w))

    def with_shares(mine, got):
        half = mine.shape[0] // 2
        rows = lax.dynamic_slice_in_dim(mine, core * half, half, 0).astype(F32) + sum(v.astype(F32) for v in got)
        return lax.dynamic_update_slice_in_dim(mine, rows.astype(BF), core * half, 0)

    back, output, gate_grad, up_grad = lax.optimization_barrier((back, output, gate_grad, up_grad))
    out_grad_w = lax.psum_scatter(with_shares(out_part, [v[1] for v in shares]), "dp", scatter_dimension=0, tiled=True)
    qkv_grad = lax.psum_scatter(with_shares(qkv_part, [v[0] for v in shares]), "dp", scatter_dimension=0, tiled=True)
    out_grad_w, qkv_grad = out_grad_w.T.astype(F32), qkv_grad.astype(F32)
    d_n1_pair = sum(dot_nt(d, w, F32) for d, w in back)
    gain_one_grad = jnp.sum(d_n1_pair * x_pair * inv_pair, axis=0)
    d_n1 = rows_of(d_n1_pair, 0) + scatter(
        [None] + [[rows_of(d_n1_pair, bits).astype(BF)] for bits in range(1, group)], group)[0]
    input_grad = dh + norm_back(x_own, inv_own, gain_one, d_n1)

    gains = scatter_rows(jnp.concatenate(
        [v.reshape(lax.axis_size("dp") * places, -1) for v in (gain_one_grad, gain_two_grad)], axis=1))[0]
    return (
        output,
        input_grad,
        gains[:gains.shape[0] // 2],
        qkv_grad[:, :q_width],
        qkv_grad[:, q_width:q_width + k_width],
        qkv_grad[:, q_width + k_width:],
        out_grad_w,
        gains[gains.shape[0] // 2:],
        gate_grad.astype(F32),
        up_grad.astype(F32),
        down_grad.T.astype(F32),
    )


def solution(mesh):
    rows, weight_in, weight_out = P(("dp", "tensor"), None), P("dp", "tensor"), P("tensor", "dp")
    in_specs = (rows, P("dp", None), P("dp"), weight_in, weight_in, weight_in, weight_out, P("dp"),
                weight_in, weight_in, weight_out, rows)
    gain = P(("dp", "tensor"))
    out_specs = (rows, rows, gain, weight_in, weight_in, weight_in, weight_out, gain, weight_in, weight_in, weight_out)
    return jax.shard_map(body, mesh=mesh, in_specs=in_specs, out_specs=out_specs, check_vma=False)
```

```python
import functools

import jax
import jax.numpy as jnp
from jax import lax
from jax.experimental import pallas as pl
from jax.experimental.pallas import tpu as pltpu
from jax.sharding import PartitionSpec as P

HD = 80
LANES = 128
WINDOW = 4096
EPS = 1e-05
THETA = 10000.0
NEG = -1e30
LOG2E = 1.4426950408889634
BLK = 256
BF = jnp.bfloat16
F32 = jnp.float32


def turn(x, c, s):
    return x * c + pltpu.roll(x, LANES // 2, 1) * s


def turn_back(x, c, s):
    return x * c - pltpu.roll(x, LANES // 2, 1) * s


def allowed(start, first_row, rows, first_col, cols):
    row = first_row + lax.broadcasted_iota(jnp.int32, (rows, cols), 0)
    col = first_col + lax.broadcasted_iota(jnp.int32, (rows, cols), 1)
    return (col >= start) & (col <= row) & (row - col < WINDOW)


def nt(a, b):
    return lax.dot_general(a, b, (((1,), (1,)), ((), ())), preferred_element_type=F32)


def nn(a, b):
    return lax.dot_general(a, b, (((1,), (0,)), ((), ())), preferred_element_type=F32)


def tn(a, b):
    return lax.dot_general(a, b, (((0,), (0,)), ((), ())), preferred_element_type=F32)


def fwd_kernel(groups, scale, lo_ref, qr_ref, kr_ref, vb_ref, start_ref, o_ref, lse_ref):
    length = qr_ref.shape[0]
    for i in range(length // BLK):
        rows = slice(i * BLK, (i + 1) * BLK)
        for j in range(i + 1):
            cols = slice(j * BLK, (i + 1) * BLK)
            width = (i + 1 - j) * BLK

            @pl.when(lo_ref[i] == j)
            def _():
                ok = allowed(start_ref[rows, :], i * BLK, BLK, j * BLK, width)
                for g in range(groups):
                    lanes = slice(g * LANES, (g + 1) * LANES)
                    scores = nt(qr_ref[rows, lanes], kr_ref[cols, :]) * (scale * LOG2E)
                    scores = jnp.where(ok, scores, NEG)
                    top = jnp.max(scores, axis=1, keepdims=True)
                    e = jnp.exp2(scores - top)
                    total = jnp.sum(e, axis=1, keepdims=True)
                    mixed = nn(e.astype(BF), vb_ref[cols, :])
                    o_ref[rows, lanes] = (mixed / total).astype(BF)
                    lse_ref[rows, g:g + 1] = top + jnp.log2(total)


def bwd_kernel(groups, scale, lo_ref, qr_ref, kr_ref, vb_ref, do_ref, c_ref, s_ref, start_ref, lse_ref,
               dq_ref, dk_ref, dv_ref, dk_acc, dv_acc):
    length = qr_ref.shape[0]
    dk_acc[...] = jnp.zeros_like(dk_acc)
    dv_acc[...] = jnp.zeros_like(dv_acc)
    for i in range(length // BLK):
        rows = slice(i * BLK, (i + 1) * BLK)
        for j in range(i + 1):
            cols = slice(j * BLK, (i + 1) * BLK)
            width = (i + 1 - j) * BLK

            @pl.when(lo_ref[i] == j)
            def _():
                ok = allowed(start_ref[rows, :], i * BLK, BLK, j * BLK, width)
                for g in range(groups):
                    lanes = slice(g * LANES, (g + 1) * LANES)
                    q, do = qr_ref[rows, lanes], do_ref[rows, lanes]
                    k, v = kr_ref[cols, :], vb_ref[cols, :]
                    scores = nt(q, k) * (scale * LOG2E)
                    p = jnp.exp2(jnp.where(ok, scores, NEG) - lse_ref[rows, g:g + 1])
                    pd = p * nt(do, v)
                    ds = (pd - p * jnp.sum(pd, axis=1, keepdims=True)).astype(BF)
                    dq = nn(ds, k) * scale
                    dq_ref[rows, lanes] = turn_back(dq, c_ref[rows, :], s_ref[rows, :]).astype(BF)
                    dk_acc[cols, :] += tn(ds, q)
                    dv_acc[cols, :] += tn(p.astype(BF), do)
    dk_ref[...] = turn_back(dk_acc[...] * scale, c_ref[...], s_ref[...]).astype(BF)
    dv_ref[...] = dv_acc[...].astype(BF)


def attend(proj, tables, kv, groups):
    start, lo = tables[2:]
    rows = proj.shape[0]
    at = lambda width, first: pl.BlockSpec((rows, width), lambda h, lo: (0, first + h))
    wide = groups * LANES
    return pl.pallas_call(
        functools.partial(fwd_kernel, groups, HD ** -0.5),
        grid_spec=pltpu.PrefetchScalarGridSpec(
            num_scalar_prefetch=1,
            grid=(kv,),
            in_specs=[at(wide, 0), at(LANES, kv * groups), at(LANES, kv * groups + kv),
                      pl.BlockSpec((rows, 1), lambda h, lo: (0, 0))],
            out_specs=[at(wide, 0), pl.BlockSpec((None, rows, groups), lambda h, lo: (h, 0, 0))],
        ),
        out_shape=[jax.ShapeDtypeStruct((rows, kv * wide), BF), jax.ShapeDtypeStruct((kv, rows, groups), F32)],
        compiler_params=pltpu.CompilerParams(vmem_limit_bytes=48 * 2 ** 20),
        cost_estimate=cost(kv * groups * rows * rows * LANES), name="attend",
    )(lo, proj, proj, proj, start)


def attend_back(proj, d_o, tables, lse, kv, groups):
    cos_t, sin_t, start, lo = tables
    rows = proj.shape[0]
    whole = lambda width: pl.BlockSpec((rows, width), lambda h, lo: (0, 0))
    at = lambda width, first=0: pl.BlockSpec((rows, width), lambda h, lo: (0, first + h))
    wide = groups * LANES
    out = lambda width: jax.ShapeDtypeStruct((rows, kv * width), BF)
    return pl.pallas_call(
        functools.partial(bwd_kernel, groups, HD ** -0.5),
        grid_spec=pltpu.PrefetchScalarGridSpec(
            num_scalar_prefetch=1,
            grid=(kv,),
            in_specs=[at(wide), at(LANES, kv * groups), at(LANES, kv * groups + kv), at(wide), whole(LANES), whole(LANES), whole(1),
                      pl.BlockSpec((None, rows, groups), lambda h, lo: (h, 0, 0))],
            out_specs=[at(wide), at(LANES), at(LANES)],
            scratch_shapes=[pltpu.VMEM((rows, LANES), F32)] * 2,
        ),
        out_shape=[out(wide), out(LANES), out(LANES)],
        compiler_params=pltpu.CompilerParams(vmem_limit_bytes=48 * 2 ** 20),
        cost_estimate=cost(10 * kv * groups * rows * rows * LANES),
        name="attend_back",
    )(lo, proj, proj, proj, d_o, cos_t, sin_t, start, lse)


COLS = 256
FINISH_COST = 52 * 10 ** 9


def cost(flops):
    return pl.CostEstimate(flops=flops, bytes_accessed=0, transcendentals=0)


def params():
    return pltpu.CompilerParams(vmem_limit_bytes=56 * 2 ** 20)


def project_kernel(heads, kv, parts, at_ref, n1_ref, eq_ref, ek_ref, c_ref, s_ref, *refs):
    w_refs, out_ref = refs[:parts], refs[parts]
    q_width = heads * HD
    step = pl.program_id(0)

    def go(columns, spread, turned):
        proj = None
        for i, w_ref in enumerate(w_refs):
            depth = w_ref.shape[0]
            a = n1_ref[...] if parts == 1 else n1_ref[:, pl.ds(pl.multiple_of(at_ref[i] * depth, depth), depth)]
            part = nn(a, nn(w_ref[:, columns], spread).astype(BF))
            proj = part if proj is None else proj + part
        for h in range(proj.shape[1] // LANES):
            lanes = slice(h * LANES, (h + 1) * LANES)
            head = proj[:, lanes]
            out_ref[:, lanes] = (turn(head, c_ref[...], s_ref[...]) if h < turned else head).astype(BF)

    @pl.when(step < heads // (2 * kv))
    def _():
        go(slice(0, q_width), eq_ref[...], 2 * kv)

    @pl.when(step == heads // (2 * kv))
    def _():
        go(slice(q_width, w_refs[0].shape[1]), ek_ref[...], kv)


def project(n1, w_parts, at, tables, heads, kv):
    cos_t, sin_t = tables[:2]
    rows, d = n1.shape
    per = 2 * kv
    steps = heads // per + 1
    whole = lambda shape: pl.BlockSpec(shape, lambda i, at: (0, 0))
    e_k = jnp.pad(spread_matrix(2 * kv), ((0, w_parts[0].shape[1] - (heads + 2 * kv) * HD), (0, 0)))
    return pl.pallas_call(
        functools.partial(project_kernel, heads, kv, len(w_parts)),
        grid_spec=pltpu.PrefetchScalarGridSpec(
            num_scalar_prefetch=1,
            grid=(steps,),
            in_specs=[whole((rows, d)),
                      pl.BlockSpec((heads * HD, per * LANES), lambda i, at: (0, jnp.minimum(i, heads // per - 1))),
                      whole(e_k.shape), whole(cos_t.shape), whole(sin_t.shape)] + [whole(w.shape) for w in w_parts],
            out_specs=pl.BlockSpec((rows, per * LANES), lambda i, at: (0, i)),
        ),
        out_shape=jax.ShapeDtypeStruct((rows, steps * per * LANES), BF),
        compiler_params=params(), cost_estimate=cost(rows * d * steps * per * LANES // 2), name="project",
    )(at, n1, spread_matrix(heads), e_k, cos_t, sin_t, *w_parts)


def heads_back_kernel(d_ref, w_ref, e_ref, out_ref):
    out_ref[...] = nn(nn(d_ref[...], w_ref[...]).astype(BF), e_ref[...]).astype(BF)


def heads_back(grad, w_t, heads):
    (rows, d), size = grad.shape, 256
    e = spread_matrix(heads)
    return pl.pallas_call(
        heads_back_kernel,
        grid=(rows // size,),
        in_specs=[pl.BlockSpec((size, d), lambda i: (i, 0)), pl.BlockSpec(w_t.shape, lambda i: (0, 0)),
                  pl.BlockSpec(e.shape, lambda i: (0, 0))],
        out_specs=pl.BlockSpec((size, heads * LANES), lambda i: (i, 0)),
        out_shape=jax.ShapeDtypeStruct((rows, heads * LANES), BF),
        compiler_params=params(), cost_estimate=cost(2 * rows * heads * HD * (d + heads * LANES)), name="heads_back",
    )(grad, w_t, e)


def gate_up_kernel(sizes, *refs):
    n2_refs, (wg_ref, wu_ref), outs = refs[:-3 * len(sizes) - 2], refs[-3 * len(sizes) - 2:-3 * len(sizes)], refs[-3 * len(sizes):]
    n2_refs = list(n2_refs)
    for i, pieces in enumerate(sizes):
        at = 0
        for rows in pieces:
            a = n2_refs.pop(0)[...]
            gate, up = nn(a, wg_ref[...]), nn(a, wu_ref[...])
            here = slice(at, at + rows)
            outs[3 * i][here, :] = gate.astype(BF)
            outs[3 * i + 1][here, :] = up.astype(BF)
            outs[3 * i + 2][here, :] = (gate / (1.0 + jnp.exp(-gate)) * up).astype(BF)
            at += rows


def gate_up(blocks, w_gate, w_up):
    sizes = [[p.shape[0] for p in pieces] for pieces in blocks]
    flat = [p for pieces in blocks for p in pieces]
    d, ff = w_gate.shape
    tile = lambda size: pl.BlockSpec((size, COLS), lambda i: (0, i))
    outs = pl.pallas_call(
        functools.partial(gate_up_kernel, sizes),
        grid=(pl.cdiv(ff, COLS),),
        in_specs=[pl.BlockSpec(p.shape, lambda i: (0, 0)) for p in flat] + [tile(d)] * 2,
        out_specs=[tile(sum(pieces)) for pieces in sizes for _ in range(3)],
        out_shape=[jax.ShapeDtypeStruct((sum(pieces), ff), BF) for pieces in sizes for _ in range(3)],
        compiler_params=params(), cost_estimate=cost(4 * sum(map(sum, sizes)) * d * ff), name="gate_up",
    )(*flat, w_gate, w_up)
    return [outs[3 * i:3 * i + 3] for i in range(len(blocks))]


def gate_up_back_kernel(ff, n, parts, *refs):
    blocks, (wg_ref, wu_ref, wd_ref), refs = refs[:3 * n], refs[3 * n:3 * n + 3], refs[3 * n + 3:]
    d_refs, p_refs, accs = refs[:2 * n], refs[2 * n:-n], refs[-n:]
    step, last = pl.program_id(0), pl.num_programs(0) - 1
    for i in range(n):
        dy_ref, g_ref, u_ref = blocks[3 * i:3 * i + 3]
        d_hidden = nn(dy_ref[...], wd_ref[...])
        gate, up = g_ref[...].astype(F32), u_ref[...].astype(F32)
        sig = 1.0 / (1.0 + jnp.exp(-gate))
        act = gate * sig
        d_refs[2 * i][...] = (d_hidden * up * (sig + act * (1.0 - sig))).astype(BF)
        d_refs[2 * i + 1][...] = (d_hidden * act).astype(BF)

    @pl.when(step == 0)
    def _():
        for i in range(n):
            accs[i][...] = nt(d_refs[2 * i][...], wg_ref[...]) + nt(d_refs[2 * i + 1][...], wu_ref[...])

    @pl.when((step > 0) & (step < last))
    def _():
        for i in range(n):
            accs[i][...] += nt(d_refs[2 * i][...], wg_ref[...]) + nt(d_refs[2 * i + 1][...], wu_ref[...])

    @pl.when(step == last)
    def _():
        def inside(v):
            col = last * COLS + lax.broadcasted_iota(jnp.int32, v.shape, 1)
            return jnp.where(col < ff, v, jnp.zeros_like(v))

        w_g, w_u = inside(wg_ref[...]), inside(wu_ref[...])
        for i in range(n):
            total = accs[i][...] + nt(inside(d_refs[2 * i][...]), w_g) + nt(inside(d_refs[2 * i + 1][...]), w_u)
            size = total.shape[0] // parts
            for j in range(parts):
                p_refs[parts * i + j][...] = total[j * size:(j + 1) * size].astype(BF)


def gate_up_back(blocks, w_gate, w_up, w_down_t, parts):
    n, (rows, d), ff = len(blocks), blocks[0][0].shape, w_gate.shape[1]
    assert pl.cdiv(ff, COLS) > 1
    tile = lambda size: pl.BlockSpec((size, COLS), lambda i: (0, i))
    whole = pl.BlockSpec((rows, d), lambda i: (0, 0), pipeline_mode=pl.Buffered(1))
    piece = pl.BlockSpec((rows // parts, d), lambda i: (0, 0))
    outs = pl.pallas_call(
        functools.partial(gate_up_back_kernel, ff, n, parts),
        grid=(pl.cdiv(ff, COLS),),
        in_specs=[whole, tile(rows), tile(rows)] * n + [tile(d)] * 3,
        out_specs=[tile(rows)] * (2 * n) + [piece] * (parts * n),
        out_shape=[jax.ShapeDtypeStruct((rows, ff), BF)] * (2 * n)
        + [jax.ShapeDtypeStruct((rows // parts, d), BF)] * (parts * n),
        scratch_shapes=[pltpu.VMEM((rows, d), F32)] * n,
        compiler_params=pltpu.CompilerParams(vmem_limit_bytes=58 * 2 ** 20),
        cost_estimate=cost(6 * n * rows * d * ff), name="gate_up_back",
    )(*[v for block in blocks for v in block], w_gate, w_up, w_down_t)
    return [(*outs[2 * i:2 * i + 2], outs[2 * n + parts * i:2 * n + parts * (i + 1)]) for i in range(n)]


def down_kernel(h_ref, w_ref, *out_refs):
    out = nt(h_ref[...], w_ref[...])
    size = out.shape[0] // len(out_refs)
    for i, out_ref in enumerate(out_refs):
        out_ref[...] = out[i * size:(i + 1) * size].astype(out_ref.dtype)


def down(hidden, w_down_t, parts):
    (rows, ff), d = hidden.shape, w_down_t.shape[0]
    size = 512
    return pl.pallas_call(
        down_kernel,
        grid=(pl.cdiv(d, size),),
        in_specs=[pl.BlockSpec((rows, ff), lambda i: (0, 0)), pl.BlockSpec((size, ff), lambda i: (i, 0))],
        out_specs=[pl.BlockSpec((rows // parts, size), lambda i: (0, i))] * parts,
        out_shape=[jax.ShapeDtypeStruct((rows // parts, d), BF)] * parts,
        compiler_params=params(), cost_estimate=cost(2 * rows * d * ff), name="down",
    )(hidden, w_down_t)


def wgrad_kernel(n, lists, tiles, *refs):
    a_refs, b_refs, (out, a_t) = refs[:n], list(refs[n:-2]), refs[-2:]
    step = pl.program_id(0)

    @pl.when(step == 0)
    def _():
        at = 0
        for a_ref in a_refs:
            a_t[:, at:at + a_ref.shape[0]] = a_ref[...].T
            at += a_ref.shape[0]

    for j, sizes in enumerate(lists):
        bs = [b_refs.pop(0) for _ in sizes]

        @pl.when(step // tiles == j)
        def _():
            total, at = None, 0
            for rows, b_ref in zip(sizes, bs):
                part = nn(a_t[:, at:at + rows], b_ref[...])
                total = part if total is None else total + part
                at += rows
            out[...] = total.astype(BF)


def wgrad(a_blocks, *b_lists):
    d, ff = a_blocks[0].shape[1], b_lists[0][0].shape[1]
    total = sum(a.shape[0] for a in a_blocks)
    lists = [[b.shape[0] for b in bs] for bs in b_lists]
    tiles = pl.cdiv(ff, COLS)
    b_spec = lambda b, j: pl.BlockSpec((b.shape[0], COLS), lambda i: (0, jnp.clip(i - j * tiles, 0, tiles - 1)))
    width = ff if len(lists) == 1 else len(lists) * tiles * COLS
    return pl.pallas_call(
        functools.partial(wgrad_kernel, len(a_blocks), lists, tiles),
        grid=(len(lists) * tiles,),
        in_specs=[pl.BlockSpec(a.shape, lambda i: (0, 0), pipeline_mode=pl.Buffered(1)) for a in a_blocks]
        + [b_spec(b, j) for j, bs in enumerate(b_lists) for b in bs],
        out_specs=pl.BlockSpec((d, COLS), lambda i: (0, i)),
        out_shape=jax.ShapeDtypeStruct((d, width), BF),
        scratch_shapes=[pltpu.VMEM((d, total), BF)],
        compiler_params=params(), cost_estimate=cost(total * d * ff * len(b_lists) // 4), name="wgrad",
    )(*a_blocks, *[b for bs in b_lists for b in bs])


def finish_kernel(eps, x_ref, gain_ref, own_ref, got_ref, dh_ref, out_ref):
    x = x_ref[...].astype(F32)
    inv = lax.rsqrt(jnp.mean(x * x, axis=1, keepdims=True) + eps)
    scaled = (own_ref[...] + got_ref[...].astype(F32)) * gain_ref[...]
    out_ref[...] = dh_ref[...] + inv * scaled - x * (inv * inv * inv * jnp.mean(scaled * x, axis=1, keepdims=True))


def finish(x, gain, own, got, dh):
    rows, d = x.shape
    size = min(128, rows)
    at = pl.BlockSpec((size, d), lambda i: (i, 0))
    return pl.pallas_call(
        functools.partial(finish_kernel, EPS),
        grid=(rows // size,),
        in_specs=[at, pl.BlockSpec((1, d), lambda i: (0, 0)), at, at, at],
        out_specs=at,
        out_shape=jax.ShapeDtypeStruct((rows, d), F32),
        compiler_params=params(), cost_estimate=cost(FINISH_COST), name="finish",
    )(x, gain[None, :], own, got, dh)


def doc_starts(seg_row):
    places = jnp.arange(seg_row.shape[0], dtype=jnp.int32)
    previous = jnp.concatenate([seg_row[:1] - 1, seg_row[:-1]])
    return lax.cummax(jnp.where(seg_row != previous, places, 0), axis=0)


def head_tables(positions):
    half = HD // 2
    freq = THETA ** (-(jnp.arange(half, dtype=F32) * 2.0 / HD))
    angles = positions.astype(F32)[:, None] * freq
    cosine, sine = jnp.cos(angles), jnp.sin(angles)
    gap = jnp.zeros((positions.shape[0], LANES // 2 - half), F32)
    return (jnp.concatenate([cosine, gap, cosine, gap], axis=1),
            jnp.concatenate([-sine, gap, sine, gap], axis=1))


def spread_matrix(heads):
    row = jnp.arange(heads * HD)
    feature = row % HD
    lane = (row // HD) * LANES + feature + jnp.where(feature >= HD // 2, LANES // 2 - HD // 2, 0)
    return (lane[:, None] == jnp.arange(heads * LANES)[None, :]).astype(BF)


def dot(a, b, out=BF):
    return jnp.dot(a, b, preferred_element_type=F32).astype(out)


def dot_t(a, b, out=BF):
    return lax.dot_general(a, b, (((0,), (0,)), ((), ())), preferred_element_type=F32).astype(out)


def dot_nt(a, b, out=BF):
    return lax.dot_general(a, b, (((1,), (1,)), ((), ())), preferred_element_type=F32).astype(out)


def inverse_rms(v):
    return lax.rsqrt(jnp.mean(v * v, axis=-1, keepdims=True) + EPS)


def norm_back(v, inv, gain, grad):
    scaled = grad * gain
    return inv * scaled - v * (inv * inv * inv * jnp.mean(scaled * v, axis=-1, keepdims=True))


def swap(v, bit):
    return lax.ppermute(v, "tensor", [(i, i ^ bit) for i in range(lax.axis_size("tensor"))])


def groups_of(size):
    return [[first + i for i in range(size)] for first in range(0, lax.axis_size("tensor"), size)]


def after(v, *done):
    return lax.optimization_barrier((v, *done))[0]


def square(size):
    return size == 4 == lax.axis_size("tensor")


def gather(mine, size):
    if size == 2:
        return [[mine], [swap(mine, 1)]]
    if square(size):
        half = mine.shape[0] // 2
        from_x, from_y = swap(mine, 1), swap(mine, 2)
        return [[mine], [from_x], [from_y], [swap(from_x[:half], 2), swap(from_y[half:], 1)]]
    blocks = lax.all_gather(mine, "tensor", axis=0, tiled=False, axis_index_groups=groups_of(size))
    at = lax.axis_index("tensor") % size
    return [[lax.dynamic_index_in_dim(blocks, at ^ r, 0, keepdims=False)] for r in range(size)]


def scatter(parts, size):
    if size == 2:
        return [swap(jnp.concatenate(parts[1]), 1)], parts[1]
    if square(size):
        _, (x_low, x_high), (y_low, y_high), (d_low, d_high) = parts
        for_y, for_x = swap(d_low, 1), swap(d_high, 2)
        a1, b1 = swap(x_low, 1), swap(y_high, 2)
        x_high, y_low = plus(x_high, for_x), plus(y_low, for_y)
        a2, b2 = swap(x_high, 1), swap(y_low, 2)
        return [a1, b2, a2, b1], [x_high, y_low]
    at = lax.axis_index("tensor") % size
    whole = [jnp.concatenate(p) for p in parts[1:]]
    blocks = jnp.stack([jnp.zeros_like(whole[0])] + whole)[jnp.arange(size) ^ at]
    return [lax.psum_scatter(blocks, "tensor", scatter_dimension=0, tiled=False, axis_index_groups=groups_of(size))], whole


def plus(a, b):
    return (a.astype(F32) + b.astype(F32)).astype(BF)


def summed(got):
    got = [v.astype(F32) for v in got]
    return got[0] if len(got) == 1 else jnp.concatenate([got[0] + got[1], got[2] + got[3]])


def scatter_rows(v):
    for axis in ("dp", "tensor"):
        size, at = lax.axis_size(axis), lax.axis_index(axis)
        assert size & (size - 1) == 0
        while size > 1:
            size //= 2
            bit = (at // size) % 2
            low, high = jnp.split(v, 2)
            theirs = lax.ppermute(jnp.where(bit == 0, high, low), axis,
                                  [(i, i ^ size) for i in range(lax.axis_size(axis))])
            v = jnp.where(bit == 0, low, high) + theirs
    return v


def in_order(blocks):
    blocks = [pieces[0] for pieces in blocks]
    at = lax.axis_index("tensor") % len(blocks)
    if len(blocks) == 2:
        return by_place(at, *blocks)
    return jnp.stack(blocks)[jnp.arange(len(blocks)) ^ at].reshape(-1, *blocks[0].shape[1:])


def by_place(bit, mine, other):
    return jnp.where(bit == 0, jnp.concatenate([mine, other]), jnp.concatenate([other, mine]))


def body(tokens, segments, attn_gain, w_query, w_key, w_value, w_out, mlp_gain, w_gate, w_up, w_down, out_grad):
    q_width, k_width = w_query.shape[1], w_key.shape[1]
    heads, kv = q_width // HD, k_width // HD
    groups = heads // kv
    row_count, width = tokens.shape
    seq_count, length = segments.shape
    ff = w_gate.shape[1]
    place, places = lax.axis_index("tensor"), lax.axis_size("tensor")
    group = places // seq_count
    core = lax.axis_index("dp") % 2

    token_blocks = gather(tokens, group)
    if square(places):
        dy_y = swap(out_grad, 2)
    used = q_width + 2 * k_width
    spare = jnp.zeros((w_query.shape[0], -(used + 2) % LANES), BF)
    qkv_shard = jnp.concatenate(
        [w_query, w_key, w_value, attn_gain[:, None], mlp_gain[:, None], spare], axis=1)
    qkv_all = lax.all_gather(qkv_shard, "dp", axis=0, tiled=True)
    if square(places):
        qkv_all, token_blocks, dy_y, later = lax.optimization_barrier((qkv_all, token_blocks, dy_y, out_grad))
        dy_x = swap(later, 1)
    else:
        dy_x = None
    gain_one = qkv_all[:, used].astype(F32)
    gain_two = qkv_all[:, used + 1].astype(F32)
    out_wt = lax.all_gather(after(w_out.T, qkv_all), "dp", axis=0, tiled=True)
    gate_w = lax.all_gather(after(w_gate, qkv_all), "dp", axis=0, tiled=True)
    up_w = lax.all_gather(after(w_up, qkv_all), "dp", axis=0, tiled=True)
    down_wt = lax.all_gather(after(w_down.T, out_wt), "dp", axis=0, tiled=True)

    def core_half(v):
        half = v.shape[0] // 2
        return lax.dynamic_slice_in_dim(v, core * half, half, 0)

    def other_half(got):
        return lax.ppermute(got, "dp", [(i, i ^ 1) for i in range(lax.axis_size("dp"))])

    def joined(got, pair):
        both = jnp.broadcast_to(pair[None], (2, *pair.shape)).reshape(-1, pair.shape[1])
        return lax.dynamic_update_slice_in_dim(both, got, core * got.shape[0], 0)

    others = [group * m for m in range(1, seq_count)]
    out_sent = core_half(out_wt)
    qkv_halves = [swap(core_half(qkv_all), bits) for bits in others]
    out_halves = [swap(out_sent, bits) for bits in others]

    def chip_half(part):
        half = part.shape[0] // 2
        theirs = lax.dynamic_slice_in_dim(part, (1 - core) * half, half, 0)
        theirs = lax.ppermute(theirs, "dp", [(i, i ^ 1) for i in range(lax.axis_size("dp"))])
        mine = lax.dynamic_slice_in_dim(part, core * half, half, 0)
        return plus(mine, theirs)

    seg_row = lax.dynamic_index_in_dim(segments, place // group, 0, keepdims=False)
    start = doc_starts(seg_row)
    cos_t, sin_t = head_tables(jnp.arange(length, dtype=jnp.int32) - start)
    tables = (cos_t, sin_t, start[:, None], start[::BLK] // BLK)

    spread_q, spread_k = spread_matrix(heads), spread_matrix(kv)

    x_own = tokens.astype(F32)
    inv_own = inverse_rms(x_own)
    x_pair = in_order(token_blocks).astype(F32)
    inv_pair = inverse_rms(x_pair)
    n1 = (x_pair * inv_pair * gain_one).astype(BF)
    proj = project(n1, [qkv_all], jnp.zeros((1,), jnp.int32), tables, heads, kv)
    proj = after(proj, out_sent)
    o, lse = attend(proj, tables, kv, groups)
    kept, qkv_ws, out_wts = [(dot_nt(o, spread_q), proj, lse)], [qkv_all], [out_wt]
    for qkv_got, out_got in zip(qkv_halves, out_halves):
        qkv_got = after(qkv_got, o)
        parts = [qkv_got, other_half(qkv_got)]
        proj = project(n1, parts, jnp.stack([core, 1 - core]).astype(jnp.int32), tables, heads, kv)
        o, lse = attend(proj, tables, kv, groups)
        out_got = after(out_got, o)
        out_wts.append(joined(out_got, other_half(out_got)))
        parts, dy_x = lax.optimization_barrier((parts, dy_x, o))[:2]
        qkv_ws.append(joined(*parts))
        kept.append((dot_nt(o, spread_q), proj, lse))
    if square(places):
        dy_blocks = [out_grad, dy_x, dy_y, swap(dy_x, 2)]
    else:
        dy_blocks = [pieces[0] for pieces in gather(out_grad, places)]
    o_flat = jnp.concatenate([k[0] for k in kept], axis=1)
    out_both = jnp.concatenate(out_wts, axis=1)

    def rows_of(v, bits):
        return lax.dynamic_slice_in_dim(v, ((place % group) ^ bits) * row_count, row_count, 0)

    branch, _ = scatter([None] + [[dot_nt(rows_of(o_flat, bits), out_both)] for bits in range(1, group)], group)
    segs = segments.reshape(-1)

    def masked(v, bits):
        own = lax.dynamic_slice_in_dim(segs, (place ^ bits) * row_count, row_count, 0)
        return v * (own >= 0).astype(BF)[:, None]

    dys = [masked(block, bits) for bits, block in enumerate(dy_blocks)]
    branch, dys = lax.optimization_barrier((branch, dys))
    h = x_own + dot_nt(rows_of(o_flat, 0), out_both, F32) + summed(branch)

    inv_h = inverse_rms(h)
    n2 = (h * inv_h * gain_two).astype(BF)
    n2s = gather(after(n2, gate_w, up_w), places)
    first, qkv_ws = lax.optimization_barrier((n2s[:1], qkv_ws))
    ups = gate_up(first, gate_w, up_w)
    ups += gate_up(after(n2s[1:places - 1], ups[0]), gate_w, up_w)
    ups += gate_up(after(n2s[places - 1:], ups[1], down_wt), gate_w, up_w)
    n2_pieces = [p for pieces in n2s for p in pieces]
    hiddens = [u[2] for u in ups]
    down_part = wgrad(dys, hiddens)
    down_grad = lax.psum_scatter(down_part, "dp", scatter_dimension=0, tiled=True)
    back_blocks = [(dys[r], *ups[r][:2]) for r in range(places)]
    far = gate_up_back(after(back_blocks[places - 1:], down_part), gate_w, up_w, down_wt, 2)
    near = []
    for first in range(0, places - 1, 3):
        near += gate_up_back(after(back_blocks[first:min(first + 3, places - 1)], far), gate_w, up_w, down_wt, 2)
    backs = near + far
    got, sent = scatter([v[2] for v in backs], places)
    mlp_parts = [down(v, down_wt, 1)[0] for v in after(hiddens[1:], near)]
    n2_late = after(n2_pieces, near, sent, got[:1], got[-1:], mlp_parts[:2])
    gate_part = wgrad(n2_late, [v[0] for v in backs])
    gate_grad = lax.psum_scatter(gate_part, "dp", scatter_dimension=0, tiled=True)
    up_part = wgrad(after(n2_late, gate_part, got), [v[1] for v in backs])
    up_grad = lax.psum_scatter(up_part, "dp", scatter_dimension=0, tiled=True)
    got = after(got, up_part)
    d_n2 = summed(got) + jnp.concatenate(backs[0][2]).astype(F32)
    gain_two_grad = jnp.sum(d_n2 * h * inv_h, axis=0)
    dh = dys[0].astype(F32) + norm_back(h, inv_h, gain_two, d_n2)
    dhb = dh.astype(BF)
    late_hiddens, late_parts = after((hiddens[:1], mlp_parts[2:]), dhb)
    mlp_parts = [down(late_hiddens[0], down_wt, 1)[0], *mlp_parts[:2], *late_parts]

    dhb_blocks, mlp_parts, down_grad = lax.optimization_barrier((gather(dhb, group), mlp_parts, down_grad))
    dhb_pair = in_order(dhb_blocks)
    out_halves = [chip_half(dot_t(dhb_pair, k[0])) for k in kept[1:]]
    dhb_pair, mlp_parts = lax.optimization_barrier((dhb_pair, mlp_parts, out_halves))[:2]
    out_shares = [swap(v, bits) for v, bits in zip(out_halves, others)]
    if square(places):
        mlp_x = [swap(mlp_parts[3], 1), swap(mlp_parts[1], 1)]
    else:
        mlp_got = scatter([[v] for v in mlp_parts], places)[0]
    d_projs, qkv_shares = [], []
    for index in reversed(range(len(kept))):
        o, proj, lse = kept[index]
        d_o = heads_back(dhb_pair, out_wts[index], heads)
        dq, dk, dv = attend_back(proj, d_o, tables, lse, kv, groups)
        if not index and square(places):
            dq, far_got = lax.optimization_barrier((dq, mlp_x[0]))
        spare = jnp.zeros((dq.shape[0], qkv_all.shape[1] - used), BF)
        d_proj = jnp.concatenate([dot_nt(dq, spread_q), dot_nt(dk, spread_k), dot_nt(dv, spread_k), spare], axis=1)
        d_projs.insert(0, d_proj)
        if index:
            half = chip_half(dot_t(n1, d_proj))
            qkv_shares.append(swap(half, others[index - 1]))
            dhb_pair = after(dhb_pair, half)

    def with_shares(mine, got):
        half = mine.shape[0] // 2
        rows = lax.dynamic_slice_in_dim(mine, core * half, half, 0).astype(F32) + sum(v.astype(F32) for v in got)
        return lax.dynamic_update_slice_in_dim(mine, rows.astype(BF), core * half, 0)

    out_part = dot_t(after(dhb_pair, d_projs[0]), kept[0][0])
    out_grad_w = lax.psum_scatter(with_shares(out_part, out_shares), "dp", scatter_dimension=0, tiled=True)
    d_all, w_all = jnp.concatenate(d_projs, axis=1), jnp.concatenate(qkv_ws, axis=1)
    d_n1_parts = [dot_nt(rows_of(d_all, bits), w_all) for bits in range(1, group)]
    d_n1_got, sent = scatter([None] + [[v] for v in d_n1_parts], group)
    d_n1_own = dot_nt(rows_of(d_all, 0), w_all, F32)
    gain_one_grad = jnp.sum(d_n1_own * x_own * inv_own, axis=0) + sum(
        jnp.sum(v.astype(F32) * token_blocks[bits][0].astype(F32) * rows_of(inv_pair, bits), axis=0)
        for bits, v in zip(range(1, group), d_n1_parts))
    if square(places):
        last_sum = plus(mlp_parts[2], far_got)
        mlp_got = [mlp_x[1], swap(last_sum, 2)]
        n1_late = after(n1, sent, mlp_x[1], last_sum, gain_one_grad)
    else:
        n1_late = after(n1, sent, gain_one_grad)
    qkv_part = dot_t(n1_late, d_projs[0])

    qkv_grad = lax.psum_scatter(with_shares(qkv_part, qkv_shares), "dp", scatter_dimension=0, tiled=True)
    gains = scatter_rows(jnp.concatenate(
        [v.reshape(lax.axis_size("dp") * places, -1) for v in (gain_one_grad, gain_two_grad)], axis=1))[0]
    d_n1_got, mlp_got, gains = lax.optimization_barrier((d_n1_got, mlp_got, gains))
    output = (h + sum(v.astype(F32) for v in mlp_got) + mlp_parts[0].astype(F32)).astype(BF)
    input_grad = finish(tokens, gain_one, d_n1_own, summed(d_n1_got) if len(d_n1_got) > 1 else d_n1_got[0], dh)
    gate_grad, up_grad, out_grad_w, qkv_grad = after((gate_grad, up_grad, out_grad_w, qkv_grad), input_grad)
    out_grad_w, qkv_grad = out_grad_w.T.astype(F32), qkv_grad.astype(F32)

    return (
        output,
        input_grad,
        gains[:gains.shape[0] // 2],
        qkv_grad[:, :q_width],
        qkv_grad[:, q_width:q_width + k_width],
        qkv_grad[:, q_width + k_width:used],
        out_grad_w,
        gains[gains.shape[0] // 2:],
        gate_grad.astype(F32),
        up_grad.astype(F32),
        down_grad.T.astype(F32),
    )


def solution(mesh):
    rows, weight_in, weight_out = P(("dp", "tensor"), None), P("dp", "tensor"), P("tensor", "dp")
    in_specs = (rows, P("dp", None), P("dp"), weight_in, weight_in, weight_in, weight_out, P("dp"),
                weight_in, weight_in, weight_out, rows)
    gain = P(("dp", "tensor"))
    out_specs = (rows, rows, gain, weight_in, weight_in, weight_in, weight_out, gain, weight_in, weight_in, weight_out)
    return jax.shard_map(body, mesh=mesh, in_specs=in_specs, out_specs=out_specs, check_vma=False)
```

```python
import functools

import jax
import jax.numpy as jnp
from jax import lax
from jax.experimental import pallas as pl
from jax.experimental.pallas import tpu as pltpu
from jax.sharding import PartitionSpec as P

HD = 80
LANES = 128
WINDOW = 4096
EPS = 1e-05
THETA = 10000.0
NEG = -1e30
LOG2E = 1.4426950408889634
BLK = 256
HEADS_AT_ONCE = 1
BF = jnp.bfloat16
F32 = jnp.float32


def turn(x, c, s):
    return x * c + pltpu.roll(x, LANES // 2, 1) * s


def turn_back(x, c, s):
    return x * c - pltpu.roll(x, LANES // 2, 1) * s


def allowed(start, first_row, rows, first_col, cols):
    row = first_row + lax.broadcasted_iota(jnp.int32, (rows, cols), 0)
    col = first_col + lax.broadcasted_iota(jnp.int32, (rows, cols), 1)
    return (col >= start) & (col <= row) & (row - col < WINDOW)


def nt(a, b):
    return lax.dot_general(a, b, (((1,), (1,)), ((), ())), preferred_element_type=F32)


def nn(a, b):
    return lax.dot_general(a, b, (((1,), (0,)), ((), ())), preferred_element_type=F32)


def tn(a, b):
    return lax.dot_general(a, b, (((0,), (0,)), ((), ())), preferred_element_type=F32)


def fwd_kernel(groups, scale, lo_ref, qr_ref, kr_ref, vb_ref, start_ref, o_ref, lse_ref):
    length = qr_ref.shape[0]
    for i in range(length // BLK):
        rows = slice(i * BLK, (i + 1) * BLK)
        for j in range(i + 1):
            cols = slice(j * BLK, (i + 1) * BLK)
            width = (i + 1 - j) * BLK

            @pl.when(lo_ref[i] == j)
            def _():
                ok = allowed(start_ref[rows, :], i * BLK, BLK, j * BLK, width)

                @pl.loop(0, groups, unroll=HEADS_AT_ONCE)
                def _(g):
                    lanes = pl.ds(pl.multiple_of(g * LANES, LANES), LANES)
                    scores = nt(qr_ref[rows, lanes], kr_ref[cols, :]) * (scale * LOG2E)
                    scores = jnp.where(ok, scores, NEG)
                    top = jnp.max(scores, axis=1, keepdims=True)
                    e = jnp.exp2(scores - top)
                    total = jnp.sum(e, axis=1, keepdims=True)
                    mixed = nn(e.astype(BF), vb_ref[cols, :])
                    o_ref[rows, lanes] = (mixed / total).astype(BF)
                    lse = lse_ref[rows, :]
                    here = lax.broadcasted_iota(jnp.int32, lse.shape, 1) == g
                    lse_ref[rows, :] = jnp.where(here, top + jnp.log2(total), lse)


def bwd_kernel(groups, scale, lo_ref, qr_ref, kr_ref, vb_ref, do_ref, c_ref, s_ref, start_ref, lse_ref,
               dq_ref, dk_ref, dv_ref, dk_acc, dv_acc):
    length = qr_ref.shape[0]
    dk_acc[...] = jnp.zeros_like(dk_acc)
    dv_acc[...] = jnp.zeros_like(dv_acc)
    for i in range(length // BLK):
        rows = slice(i * BLK, (i + 1) * BLK)
        for j in range(i + 1):
            cols = slice(j * BLK, (i + 1) * BLK)
            width = (i + 1 - j) * BLK

            @pl.when(lo_ref[i] == j)
            def _():
                ok = allowed(start_ref[rows, :], i * BLK, BLK, j * BLK, width)

                @pl.loop(0, groups, unroll=HEADS_AT_ONCE)
                def _(g):
                    lanes = pl.ds(pl.multiple_of(g * LANES, LANES), LANES)
                    lse = lse_ref[rows, :]
                    here = lax.broadcasted_iota(jnp.int32, lse.shape, 1) == g
                    lse = jnp.sum(jnp.where(here, lse, 0.0), axis=1, keepdims=True)
                    q, do = qr_ref[rows, lanes], do_ref[rows, lanes]
                    k, v = kr_ref[cols, :], vb_ref[cols, :]
                    scores = nt(q, k) * (scale * LOG2E)
                    p = jnp.exp2(jnp.where(ok, scores, NEG) - lse)
                    pd = p * nt(do, v)
                    ds = (pd - p * jnp.sum(pd, axis=1, keepdims=True)).astype(BF)
                    dq = nn(ds, k) * scale
                    dq_ref[rows, lanes] = turn_back(dq, c_ref[rows, :], s_ref[rows, :]).astype(BF)
                    dk_acc[cols, :] += tn(ds, q)
                    dv_acc[cols, :] += tn(p.astype(BF), do)
    dk_ref[...] = turn_back(dk_acc[...] * scale, c_ref[...], s_ref[...]).astype(BF)
    dv_ref[...] = dv_acc[...].astype(BF)


def attend(proj, tables, kv, groups):
    start, lo = tables[2:]
    rows = proj.shape[0]
    at = lambda width, first: pl.BlockSpec((rows, width), lambda h, lo: (0, first + h))
    wide = groups * LANES
    return pl.pallas_call(
        functools.partial(fwd_kernel, groups, HD ** -0.5),
        grid_spec=pltpu.PrefetchScalarGridSpec(
            num_scalar_prefetch=1,
            grid=(kv,),
            in_specs=[at(wide, 0), at(LANES, kv * groups), at(LANES, kv * groups + kv),
                      pl.BlockSpec((rows, 1), lambda h, lo: (0, 0))],
            out_specs=[at(wide, 0), pl.BlockSpec((None, rows, groups), lambda h, lo: (h, 0, 0))],
        ),
        out_shape=[jax.ShapeDtypeStruct((rows, kv * wide), BF), jax.ShapeDtypeStruct((kv, rows, groups), F32)],
        compiler_params=pltpu.CompilerParams(vmem_limit_bytes=48 * 2 ** 20),
        cost_estimate=cost(kv * groups * rows * rows * LANES), name="attend",
    )(lo, proj, proj, proj, start)


def attend_back(proj, d_o, tables, lse, kv, groups):
    cos_t, sin_t, start, lo = tables
    rows = proj.shape[0]
    whole = lambda width: pl.BlockSpec((rows, width), lambda h, lo: (0, 0))
    at = lambda width, first=0: pl.BlockSpec((rows, width), lambda h, lo: (0, first + h))
    wide = groups * LANES
    out = lambda width: jax.ShapeDtypeStruct((rows, kv * width), BF)
    return pl.pallas_call(
        functools.partial(bwd_kernel, groups, HD ** -0.5),
        grid_spec=pltpu.PrefetchScalarGridSpec(
            num_scalar_prefetch=1,
            grid=(kv,),
            in_specs=[at(wide), at(LANES, kv * groups), at(LANES, kv * groups + kv), at(wide), whole(LANES), whole(LANES), whole(1),
                      pl.BlockSpec((None, rows, groups), lambda h, lo: (h, 0, 0))],
            out_specs=[at(wide), at(LANES), at(LANES)],
            scratch_shapes=[pltpu.VMEM((rows, LANES), F32)] * 2,
        ),
        out_shape=[out(wide), out(LANES), out(LANES)],
        compiler_params=pltpu.CompilerParams(vmem_limit_bytes=48 * 2 ** 20),
        cost_estimate=cost(4 * kv * groups * rows * rows * LANES),
        name="attend_back",
    )(lo, proj, proj, proj, d_o, cos_t, sin_t, start, lse)


COLS = 256
FINISH_COST = 52 * 10 ** 9


def cost(flops):
    return pl.CostEstimate(flops=flops, bytes_accessed=0, transcendentals=0)


def params():
    return pltpu.CompilerParams(vmem_limit_bytes=56 * 2 ** 20)


def project_kernel(heads, kv, parts, at_ref, n1_ref, eq_ref, ek_ref, c_ref, s_ref, *refs):
    w_refs, out_ref = refs[:parts], refs[parts]
    q_width = heads * HD
    step = pl.program_id(0)

    def go(columns, spread, turned):
        proj = None
        for i, w_ref in enumerate(w_refs):
            depth = w_ref.shape[0]
            a = n1_ref[...] if parts == 1 else n1_ref[:, pl.ds(pl.multiple_of(at_ref[i] * depth, depth), depth)]
            part = nn(a, nn(w_ref[:, columns], spread).astype(BF))
            proj = part if proj is None else proj + part
        for h in range(proj.shape[1] // LANES):
            lanes = slice(h * LANES, (h + 1) * LANES)
            head = proj[:, lanes]
            out_ref[:, lanes] = (turn(head, c_ref[...], s_ref[...]) if h < turned else head).astype(BF)

    @pl.when(step < heads // (2 * kv))
    def _():
        go(slice(0, q_width), eq_ref[...], 2 * kv)

    @pl.when(step == heads // (2 * kv))
    def _():
        go(slice(q_width, w_refs[0].shape[1]), ek_ref[...], kv)


def project(n1, w_parts, at, tables, heads, kv):
    cos_t, sin_t = tables[:2]
    rows, d = n1.shape
    per = 2 * kv
    steps = heads // per + 1
    whole = lambda shape: pl.BlockSpec(shape, lambda i, at: (0, 0))
    e_k = jnp.pad(spread_matrix(2 * kv), ((0, w_parts[0].shape[1] - (heads + 2 * kv) * HD), (0, 0)))
    return pl.pallas_call(
        functools.partial(project_kernel, heads, kv, len(w_parts)),
        grid_spec=pltpu.PrefetchScalarGridSpec(
            num_scalar_prefetch=1,
            grid=(steps,),
            in_specs=[whole((rows, d)),
                      pl.BlockSpec((heads * HD, per * LANES), lambda i, at: (0, jnp.minimum(i, heads // per - 1))),
                      whole(e_k.shape), whole(cos_t.shape), whole(sin_t.shape)] + [whole(w.shape) for w in w_parts],
            out_specs=pl.BlockSpec((rows, per * LANES), lambda i, at: (0, i)),
        ),
        out_shape=jax.ShapeDtypeStruct((rows, steps * per * LANES), BF),
        compiler_params=params(), cost_estimate=cost(rows * d * steps * per * LANES // 2), name="project",
    )(at, n1, spread_matrix(heads), e_k, cos_t, sin_t, *w_parts)


def heads_back_kernel(d_ref, w_ref, e_ref, out_ref):
    out_ref[...] = nn(nn(d_ref[...], w_ref[...]).astype(BF), e_ref[...]).astype(BF)


def heads_back(grad, w_t, heads):
    (rows, d), size = grad.shape, 256
    e = spread_matrix(heads)
    return pl.pallas_call(
        heads_back_kernel,
        grid=(rows // size,),
        in_specs=[pl.BlockSpec((size, d), lambda i: (i, 0)), pl.BlockSpec(w_t.shape, lambda i: (0, 0)),
                  pl.BlockSpec(e.shape, lambda i: (0, 0))],
        out_specs=pl.BlockSpec((size, heads * LANES), lambda i: (i, 0)),
        out_shape=jax.ShapeDtypeStruct((rows, heads * LANES), BF),
        compiler_params=params(), cost_estimate=cost(2 * rows * heads * HD * (d + heads * LANES)), name="heads_back",
    )(grad, w_t, e)


def gate_up_kernel(sizes, *refs):
    n2_refs, (wg_ref, wu_ref), outs = refs[:-3 * len(sizes) - 2], refs[-3 * len(sizes) - 2:-3 * len(sizes)], refs[-3 * len(sizes):]
    n2_refs = list(n2_refs)
    for i, pieces in enumerate(sizes):
        at = 0
        for rows in pieces:
            a = n2_refs.pop(0)[...]
            gate, up = nn(a, wg_ref[...]), nn(a, wu_ref[...])
            here = slice(at, at + rows)
            outs[3 * i][here, :] = gate.astype(BF)
            outs[3 * i + 1][here, :] = up.astype(BF)
            outs[3 * i + 2][here, :] = (gate / (1.0 + jnp.exp(-gate)) * up).astype(BF)
            at += rows


def gate_up(blocks, w_gate, w_up):
    sizes = [[p.shape[0] for p in pieces] for pieces in blocks]
    flat = [p for pieces in blocks for p in pieces]
    d, ff = w_gate.shape
    tile = lambda size: pl.BlockSpec((size, COLS), lambda i: (0, i))
    outs = pl.pallas_call(
        functools.partial(gate_up_kernel, sizes),
        grid=(pl.cdiv(ff, COLS),),
        in_specs=[pl.BlockSpec(p.shape, lambda i: (0, 0)) for p in flat] + [tile(d)] * 2,
        out_specs=[tile(sum(pieces)) for pieces in sizes for _ in range(3)],
        out_shape=[jax.ShapeDtypeStruct((sum(pieces), ff), BF) for pieces in sizes for _ in range(3)],
        compiler_params=params(), cost_estimate=cost(4 * sum(map(sum, sizes)) * d * ff), name="gate_up",
    )(*flat, w_gate, w_up)
    return [outs[3 * i:3 * i + 3] for i in range(len(blocks))]


def gate_up_back_kernel(ff, n, parts, *refs):
    blocks, (wg_ref, wu_ref, wd_ref), refs = refs[:3 * n], refs[3 * n:3 * n + 3], refs[3 * n + 3:]
    d_refs, p_refs, accs = refs[:2 * n], refs[2 * n:-n], refs[-n:]
    step, last = pl.program_id(0), pl.num_programs(0) - 1
    for i in range(n):
        dy_ref, g_ref, u_ref = blocks[3 * i:3 * i + 3]
        d_hidden = nn(dy_ref[...], wd_ref[...])
        gate, up = g_ref[...].astype(F32), u_ref[...].astype(F32)
        sig = 1.0 / (1.0 + jnp.exp(-gate))
        act = gate * sig
        d_refs[2 * i][...] = (d_hidden * up * (sig + act * (1.0 - sig))).astype(BF)
        d_refs[2 * i + 1][...] = (d_hidden * act).astype(BF)

    @pl.when(step == 0)
    def _():
        for i in range(n):
            accs[i][...] = nt(d_refs[2 * i][...], wg_ref[...]) + nt(d_refs[2 * i + 1][...], wu_ref[...])

    @pl.when((step > 0) & (step < last))
    def _():
        for i in range(n):
            accs[i][...] += nt(d_refs[2 * i][...], wg_ref[...]) + nt(d_refs[2 * i + 1][...], wu_ref[...])

    @pl.when(step == last)
    def _():
        def inside(v):
            col = last * COLS + lax.broadcasted_iota(jnp.int32, v.shape, 1)
            return jnp.where(col < ff, v, jnp.zeros_like(v))

        w_g, w_u = inside(wg_ref[...]), inside(wu_ref[...])
        for i in range(n):
            total = accs[i][...] + nt(inside(d_refs[2 * i][...]), w_g) + nt(inside(d_refs[2 * i + 1][...]), w_u)
            size = total.shape[0] // parts
            for j in range(parts):
                p_refs[parts * i + j][...] = total[j * size:(j + 1) * size].astype(BF)


def gate_up_back(blocks, w_gate, w_up, w_down_t, parts):
    n, (rows, d), ff = len(blocks), blocks[0][0].shape, w_gate.shape[1]
    assert pl.cdiv(ff, COLS) > 1
    tile = lambda size: pl.BlockSpec((size, COLS), lambda i: (0, i))
    whole = pl.BlockSpec((rows, d), lambda i: (0, 0), pipeline_mode=pl.Buffered(1))
    piece = pl.BlockSpec((rows // parts, d), lambda i: (0, 0))
    outs = pl.pallas_call(
        functools.partial(gate_up_back_kernel, ff, n, parts),
        grid=(pl.cdiv(ff, COLS),),
        in_specs=[whole, tile(rows), tile(rows)] * n + [tile(d)] * 3,
        out_specs=[tile(rows)] * (2 * n) + [piece] * (parts * n),
        out_shape=[jax.ShapeDtypeStruct((rows, ff), BF)] * (2 * n)
        + [jax.ShapeDtypeStruct((rows // parts, d), BF)] * (parts * n),
        scratch_shapes=[pltpu.VMEM((rows, d), F32)] * n,
        compiler_params=pltpu.CompilerParams(vmem_limit_bytes=58 * 2 ** 20),
        cost_estimate=cost(6 * n * rows * d * ff), name="gate_up_back",
    )(*[v for block in blocks for v in block], w_gate, w_up, w_down_t)
    return [(*outs[2 * i:2 * i + 2], outs[2 * n + parts * i:2 * n + parts * (i + 1)]) for i in range(n)]


def down_kernel(h_ref, w_ref, *out_refs):
    out = nt(h_ref[...], w_ref[...])
    size = out.shape[0] // len(out_refs)
    for i, out_ref in enumerate(out_refs):
        out_ref[...] = out[i * size:(i + 1) * size].astype(out_ref.dtype)


def down(hidden, w_down_t, parts):
    (rows, ff), d = hidden.shape, w_down_t.shape[0]
    size = 512
    return pl.pallas_call(
        down_kernel,
        grid=(pl.cdiv(d, size),),
        in_specs=[pl.BlockSpec((rows, ff), lambda i: (0, 0)), pl.BlockSpec((size, ff), lambda i: (i, 0))],
        out_specs=[pl.BlockSpec((rows // parts, size), lambda i: (0, i))] * parts,
        out_shape=[jax.ShapeDtypeStruct((rows // parts, d), BF)] * parts,
        compiler_params=params(), cost_estimate=cost(2 * rows * d * ff), name="down",
    )(hidden, w_down_t)


def wgrad_kernel(n, lists, tiles, *refs):
    a_refs, b_refs, (out, a_t) = refs[:n], list(refs[n:-2]), refs[-2:]
    step = pl.program_id(0)

    @pl.when(step == 0)
    def _():
        at = 0
        for a_ref in a_refs:
            a_t[:, at:at + a_ref.shape[0]] = a_ref[...].T
            at += a_ref.shape[0]

    for j, sizes in enumerate(lists):
        bs = [b_refs.pop(0) for _ in sizes]

        @pl.when(step // tiles == j)
        def _():
            total, at = None, 0
            for rows, b_ref in zip(sizes, bs):
                part = nn(a_t[:, at:at + rows], b_ref[...])
                total = part if total is None else total + part
                at += rows
            out[...] = total.astype(BF)


def wgrad(a_blocks, *b_lists):
    d, ff = a_blocks[0].shape[1], b_lists[0][0].shape[1]
    total = sum(a.shape[0] for a in a_blocks)
    lists = [[b.shape[0] for b in bs] for bs in b_lists]
    tiles = pl.cdiv(ff, COLS)
    b_spec = lambda b, j: pl.BlockSpec((b.shape[0], COLS), lambda i: (0, jnp.clip(i - j * tiles, 0, tiles - 1)))
    width = ff if len(lists) == 1 else len(lists) * tiles * COLS
    return pl.pallas_call(
        functools.partial(wgrad_kernel, len(a_blocks), lists, tiles),
        grid=(len(lists) * tiles,),
        in_specs=[pl.BlockSpec(a.shape, lambda i: (0, 0), pipeline_mode=pl.Buffered(1)) for a in a_blocks]
        + [b_spec(b, j) for j, bs in enumerate(b_lists) for b in bs],
        out_specs=pl.BlockSpec((d, COLS), lambda i: (0, i)),
        out_shape=jax.ShapeDtypeStruct((d, width), BF),
        scratch_shapes=[pltpu.VMEM((d, total), BF)],
        compiler_params=params(), cost_estimate=cost(total * d * ff * len(b_lists) // 4), name="wgrad",
    )(*a_blocks, *[b for bs in b_lists for b in bs])


def finish_kernel(eps, x_ref, gain_ref, own_ref, got_ref, dh_ref, out_ref):
    x = x_ref[...].astype(F32)
    inv = lax.rsqrt(jnp.mean(x * x, axis=1, keepdims=True) + eps)
    scaled = (own_ref[...] + got_ref[...].astype(F32)) * gain_ref[...]
    out_ref[...] = dh_ref[...] + inv * scaled - x * (inv * inv * inv * jnp.mean(scaled * x, axis=1, keepdims=True))


def finish(x, gain, own, got, dh):
    rows, d = x.shape
    size = min(128, rows)
    at = pl.BlockSpec((size, d), lambda i: (i, 0))
    return pl.pallas_call(
        functools.partial(finish_kernel, EPS),
        grid=(rows // size,),
        in_specs=[at, pl.BlockSpec((1, d), lambda i: (0, 0)), at, at, at],
        out_specs=at,
        out_shape=jax.ShapeDtypeStruct((rows, d), F32),
        compiler_params=params(), cost_estimate=cost(FINISH_COST), name="finish",
    )(x, gain[None, :], own, got, dh)


def doc_starts(seg_row):
    places = jnp.arange(seg_row.shape[0], dtype=jnp.int32)
    previous = jnp.concatenate([seg_row[:1] - 1, seg_row[:-1]])
    return lax.cummax(jnp.where(seg_row != previous, places, 0), axis=0)


def head_tables(positions):
    half = HD // 2
    freq = THETA ** (-(jnp.arange(half, dtype=F32) * 2.0 / HD))
    angles = positions.astype(F32)[:, None] * freq
    cosine, sine = jnp.cos(angles), jnp.sin(angles)
    gap = jnp.zeros((positions.shape[0], LANES // 2 - half), F32)
    return (jnp.concatenate([cosine, gap, cosine, gap], axis=1),
            jnp.concatenate([-sine, gap, sine, gap], axis=1))


def spread_matrix(heads):
    row = jnp.arange(heads * HD)
    feature = row % HD
    lane = (row // HD) * LANES + feature + jnp.where(feature >= HD // 2, LANES // 2 - HD // 2, 0)
    return (lane[:, None] == jnp.arange(heads * LANES)[None, :]).astype(BF)


def dot(a, b, out=BF):
    return jnp.dot(a, b, preferred_element_type=F32).astype(out)


def dot_t(a, b, out=BF):
    return lax.dot_general(a, b, (((0,), (0,)), ((), ())), preferred_element_type=F32).astype(out)


def dot_nt(a, b, out=BF):
    return lax.dot_general(a, b, (((1,), (1,)), ((), ())), preferred_element_type=F32).astype(out)


def inverse_rms(v):
    return lax.rsqrt(jnp.mean(v * v, axis=-1, keepdims=True) + EPS)


def norm_back(v, inv, gain, grad):
    scaled = grad * gain
    return inv * scaled - v * (inv * inv * inv * jnp.mean(scaled * v, axis=-1, keepdims=True))


def swap(v, bit):
    return lax.ppermute(v, "tensor", [(i, i ^ bit) for i in range(lax.axis_size("tensor"))])


def groups_of(size):
    return [[first + i for i in range(size)] for first in range(0, lax.axis_size("tensor"), size)]


def after(v, *done):
    return lax.optimization_barrier((v, *done))[0]


def square(size):
    return size == 4 == lax.axis_size("tensor")


def gather(mine, size):
    if size == 2:
        return [[mine], [swap(mine, 1)]]
    if square(size):
        half = mine.shape[0] // 2
        from_x, from_y = swap(mine, 1), swap(mine, 2)
        return [[mine], [from_x], [from_y], [swap(from_x[:half], 2), swap(from_y[half:], 1)]]
    blocks = lax.all_gather(mine, "tensor", axis=0, tiled=False, axis_index_groups=groups_of(size))
    at = lax.axis_index("tensor") % size
    return [[lax.dynamic_index_in_dim(blocks, at ^ r, 0, keepdims=False)] for r in range(size)]


def scatter(parts, size):
    if size == 2:
        return [swap(jnp.concatenate(parts[1]), 1)], parts[1]
    if square(size):
        _, (x_low, x_high), (y_low, y_high), (d_low, d_high) = parts
        for_y, for_x = swap(d_low, 1), swap(d_high, 2)
        a1, b1 = swap(x_low, 1), swap(y_high, 2)
        x_high, y_low = plus(x_high, for_x), plus(y_low, for_y)
        a2, b2 = swap(x_high, 1), swap(y_low, 2)
        return [a1, b2, a2, b1], [x_high, y_low]
    at = lax.axis_index("tensor") % size
    whole = [jnp.concatenate(p) for p in parts[1:]]
    blocks = jnp.stack([jnp.zeros_like(whole[0])] + whole)[jnp.arange(size) ^ at]
    return [lax.psum_scatter(blocks, "tensor", scatter_dimension=0, tiled=False, axis_index_groups=groups_of(size))], whole


def plus(a, b):
    return (a.astype(F32) + b.astype(F32)).astype(BF)


def summed(got):
    got = [v.astype(F32) for v in got]
    return got[0] if len(got) == 1 else jnp.concatenate([got[0] + got[1], got[2] + got[3]])


def scatter_rows(v):
    for axis in ("dp", "tensor"):
        size, at = lax.axis_size(axis), lax.axis_index(axis)
        assert size & (size - 1) == 0
        while size > 1:
            size //= 2
            bit = (at // size) % 2
            low, high = jnp.split(v, 2)
            theirs = lax.ppermute(jnp.where(bit == 0, high, low), axis,
                                  [(i, i ^ size) for i in range(lax.axis_size(axis))])
            v = jnp.where(bit == 0, low, high) + theirs
    return v


def in_order(blocks):
    blocks = [pieces[0] for pieces in blocks]
    at = lax.axis_index("tensor") % len(blocks)
    if len(blocks) == 2:
        return by_place(at, *blocks)
    return jnp.stack(blocks)[jnp.arange(len(blocks)) ^ at].reshape(-1, *blocks[0].shape[1:])


def by_place(bit, mine, other):
    return jnp.where(bit == 0, jnp.concatenate([mine, other]), jnp.concatenate([other, mine]))


def body(tokens, segments, attn_gain, w_query, w_key, w_value, w_out, mlp_gain, w_gate, w_up, w_down, out_grad):
    q_width, k_width = w_query.shape[1], w_key.shape[1]
    heads, kv = q_width // HD, k_width // HD
    groups = heads // kv
    row_count, width = tokens.shape
    seq_count, length = segments.shape
    ff = w_gate.shape[1]
    place, places = lax.axis_index("tensor"), lax.axis_size("tensor")
    group = places // seq_count
    core = lax.axis_index("dp") % 2

    token_blocks = gather(tokens, group)
    if square(places):
        dy_y = swap(out_grad, 2)
    used = q_width + 2 * k_width
    spare = jnp.zeros((w_query.shape[0], -(used + 2) % LANES), BF)
    qkv_shard = jnp.concatenate(
        [w_query, w_key, w_value, attn_gain[:, None], mlp_gain[:, None], spare], axis=1)
    qkv_all = lax.all_gather(qkv_shard, "dp", axis=0, tiled=True)
    if square(places):
        qkv_all, token_blocks, dy_y, later = lax.optimization_barrier((qkv_all, token_blocks, dy_y, out_grad))
        dy_x = swap(later, 1)
    else:
        dy_x = None
    gain_one = qkv_all[:, used].astype(F32)
    gain_two = qkv_all[:, used + 1].astype(F32)
    out_wt = lax.all_gather(after(w_out.T, qkv_all), "dp", axis=0, tiled=True)
    gate_w = lax.all_gather(after(w_gate, qkv_all), "dp", axis=0, tiled=True)
    up_w = lax.all_gather(after(w_up, qkv_all), "dp", axis=0, tiled=True)
    down_wt = lax.all_gather(after(w_down.T, out_wt), "dp", axis=0, tiled=True)

    def core_half(v):
        half = v.shape[0] // 2
        return lax.dynamic_slice_in_dim(v, core * half, half, 0)

    def other_half(got):
        return lax.ppermute(got, "dp", [(i, i ^ 1) for i in range(lax.axis_size("dp"))])

    def joined(got, pair):
        both = jnp.broadcast_to(pair[None], (2, *pair.shape)).reshape(-1, pair.shape[1])
        return lax.dynamic_update_slice_in_dim(both, got, core * got.shape[0], 0)

    others = [group * m for m in range(1, seq_count)]
    out_sent = core_half(out_wt)
    qkv_halves = [swap(core_half(qkv_all), bits) for bits in others]
    out_halves = [swap(out_sent, bits) for bits in others]

    def chip_half(part):
        half = part.shape[0] // 2
        theirs = lax.dynamic_slice_in_dim(part, (1 - core) * half, half, 0)
        theirs = lax.ppermute(theirs, "dp", [(i, i ^ 1) for i in range(lax.axis_size("dp"))])
        mine = lax.dynamic_slice_in_dim(part, core * half, half, 0)
        return plus(mine, theirs)

    seg_row = lax.dynamic_index_in_dim(segments, place // group, 0, keepdims=False)
    start = doc_starts(seg_row)
    cos_t, sin_t = head_tables(jnp.arange(length, dtype=jnp.int32) - start)
    tables = (cos_t, sin_t, start[:, None], start[::BLK] // BLK)

    spread_q, spread_k = spread_matrix(heads), spread_matrix(kv)

    x_own = tokens.astype(F32)
    inv_own = inverse_rms(x_own)
    x_pair = in_order(token_blocks).astype(F32)
    inv_pair = inverse_rms(x_pair)
    n1 = (x_pair * inv_pair * gain_one).astype(BF)
    proj = project(n1, [qkv_all], jnp.zeros((1,), jnp.int32), tables, heads, kv)
    proj = after(proj, out_sent)
    o, lse = attend(proj, tables, kv, groups)
    kept, qkv_ws, out_wts = [(dot_nt(o, spread_q), proj, lse)], [qkv_all], [out_wt]
    for qkv_got, out_got in zip(qkv_halves, out_halves):
        qkv_got, dy_x = lax.optimization_barrier((qkv_got, dy_x, o))[:2]
        parts = [qkv_got, other_half(qkv_got)]
        proj = project(n1, parts, jnp.stack([core, 1 - core]).astype(jnp.int32), tables, heads, kv)
        o, lse = attend(proj, tables, kv, groups)
        out_got = after(out_got, o)
        out_wts.append(joined(out_got, other_half(out_got)))
        qkv_ws.append(joined(*after(parts, o)))
        kept.append((dot_nt(o, spread_q), proj, lse))
    if square(places):
        dy_blocks = [out_grad, dy_x, dy_y, swap(dy_x, 2)]
    else:
        dy_blocks = [pieces[0] for pieces in gather(out_grad, places)]
    o_flat = jnp.concatenate([k[0] for k in kept], axis=1)
    out_both = jnp.concatenate(out_wts, axis=1)

    def rows_of(v, bits):
        return lax.dynamic_slice_in_dim(v, ((place % group) ^ bits) * row_count, row_count, 0)

    branch, _ = scatter([None] + [[dot_nt(rows_of(o_flat, bits), out_both)] for bits in range(1, group)], group)
    segs = segments.reshape(-1)

    def masked(v, bits):
        own = lax.dynamic_slice_in_dim(segs, (place ^ bits) * row_count, row_count, 0)
        return v * (own >= 0).astype(BF)[:, None]

    dys = [masked(block, bits) for bits, block in enumerate(dy_blocks)]
    branch, dys = lax.optimization_barrier((branch, dys))
    h = x_own + dot_nt(rows_of(o_flat, 0), out_both, F32) + summed(branch)

    inv_h = inverse_rms(h)
    n2 = (h * inv_h * gain_two).astype(BF)
    n2s = gather(after(n2, gate_w), places)
    first, qkv_ws = lax.optimization_barrier((n2s[:1], qkv_ws))
    ups = gate_up(first, gate_w, up_w)
    ups += gate_up(after(n2s[1:places - 1], ups[0]), gate_w, up_w)
    ups += gate_up(after(n2s[places - 1:], ups[1], down_wt), gate_w, up_w)
    n2_pieces = [p for pieces in n2s for p in pieces]
    hiddens = [u[2] for u in ups]
    down_part = wgrad(dys, hiddens)
    down_grad = lax.psum_scatter(down_part, "dp", scatter_dimension=0, tiled=True)
    back_blocks = [(dys[r], *ups[r][:2]) for r in range(places)]
    far = gate_up_back(after(back_blocks[places - 1:], down_part), gate_w, up_w, down_wt, 2)
    near = []
    for first in range(0, places - 1, 3):
        near += gate_up_back(after(back_blocks[first:min(first + 3, places - 1)], far), gate_w, up_w, down_wt, 2)
    backs = near + far
    got, sent = scatter([v[2] for v in backs], places)
    mlp_parts = [down(v, down_wt, 1)[0] for v in after(hiddens[1:], near)]
    n2_late = after(n2_pieces, near, sent, got[:1], got[-1:], mlp_parts[:2])
    gate_part = wgrad(n2_late, [v[0] for v in backs])
    gate_grad = lax.psum_scatter(gate_part, "dp", scatter_dimension=0, tiled=True)
    up_part = wgrad(after(n2_late, gate_part, got), [v[1] for v in backs])
    up_grad = lax.psum_scatter(up_part, "dp", scatter_dimension=0, tiled=True)
    got = after(got, up_part)
    d_n2 = summed(got) + jnp.concatenate(backs[0][2]).astype(F32)
    gain_two_grad = jnp.sum(d_n2 * h * inv_h, axis=0)
    dh = dys[0].astype(F32) + norm_back(h, inv_h, gain_two, d_n2)
    dhb = dh.astype(BF)
    late_hiddens, late_parts = after((hiddens[:1], mlp_parts[2:]), dhb)
    mlp_parts = [down(late_hiddens[0], down_wt, 1)[0], *mlp_parts[:2], *late_parts]

    dhb_blocks, mlp_parts, down_grad = lax.optimization_barrier((gather(dhb, group), mlp_parts, down_grad))
    dhb_pair = in_order(dhb_blocks)
    out_halves = [chip_half(dot_t(dhb_pair, k[0])) for k in kept[1:]]
    dhb_pair, mlp_parts = lax.optimization_barrier((dhb_pair, mlp_parts, out_halves))[:2]
    out_shares = [swap(v, bits) for v, bits in zip(out_halves, others)]
    if square(places):
        mlp_x = [swap(mlp_parts[3], 1), swap(mlp_parts[1], 1)]
    else:
        mlp_got = scatter([[v] for v in mlp_parts], places)[0]
    d_projs, qkv_shares = [], []
    for index in reversed(range(len(kept))):
        o, proj, lse = kept[index]
        d_o = heads_back(dhb_pair, out_wts[index], heads)
        dq, dk, dv = attend_back(proj, d_o, tables, lse, kv, groups)
        spare = jnp.zeros((dq.shape[0], qkv_all.shape[1] - used), BF)
        d_proj = jnp.concatenate([dot_nt(dq, spread_q), dot_nt(dk, spread_k), dot_nt(dv, spread_k), spare], axis=1)
        d_projs.insert(0, d_proj)
        last_dq = dq
        if index:
            part = dot_t(n1, d_proj)
            if square(places):
                part, far_got, out_shares = lax.optimization_barrier((part, mlp_x[0], out_shares))
            half = chip_half(part)
            qkv_shares.append(swap(half, others[index - 1]))
            dhb_pair = after(dhb_pair, half)

    def with_shares(mine, got):
        half = mine.shape[0] // 2
        rows = lax.dynamic_slice_in_dim(mine, core * half, half, 0).astype(F32) + sum(v.astype(F32) for v in got)
        return lax.dynamic_update_slice_in_dim(mine, rows.astype(BF), core * half, 0)

    out_part = dot_t(after(dhb_pair, last_dq), kept[0][0])
    out_grad_w = lax.psum_scatter(with_shares(out_part, out_shares), "dp", scatter_dimension=0, tiled=True)
    d_all, w_all = jnp.concatenate(d_projs, axis=1), jnp.concatenate(qkv_ws, axis=1)
    d_all, qkv_shares = lax.optimization_barrier((d_all, qkv_shares))
    d_n1_parts = [dot_nt(rows_of(d_all, bits), w_all) for bits in range(1, group)]
    d_n1_got, sent = scatter([None] + [[v] for v in d_n1_parts], group)
    d_n1_own = dot_nt(rows_of(d_all, 0), w_all, F32)
    gain_one_grad = jnp.sum(d_n1_own * x_own * inv_own, axis=0) + sum(
        jnp.sum(v.astype(F32) * token_blocks[bits][0].astype(F32) * rows_of(inv_pair, bits), axis=0)
        for bits, v in zip(range(1, group), d_n1_parts))
    if square(places):
        last_sum = plus(mlp_parts[2], far_got)
        mlp_got = [mlp_x[1], swap(last_sum, 2)]
        n1_late = after(n1, sent, mlp_x[1], last_sum, d_n1_own)
    else:
        n1_late = after(n1, sent, d_n1_own)
    qkv_part = dot_t(n1_late, d_projs[0])

    qkv_grad = lax.psum_scatter(with_shares(qkv_part, qkv_shares), "dp", scatter_dimension=0, tiled=True)
    d_n1_got, mlp_got = lax.optimization_barrier((d_n1_got, mlp_got))
    gain_one_grad, gain_two_grad = after((gain_one_grad, gain_two_grad), d_n1_got)
    gains = scatter_rows(jnp.concatenate(
        [v.reshape(lax.axis_size("dp") * places, -1) for v in (gain_one_grad, gain_two_grad)], axis=1))[0]
    output = (h + sum(v.astype(F32) for v in mlp_got) + mlp_parts[0].astype(F32)).astype(BF)
    input_grad = finish(tokens, gain_one, d_n1_own, summed(d_n1_got) if len(d_n1_got) > 1 else d_n1_got[0], dh)
    gate_grad, up_grad, out_grad_w, qkv_grad = after((gate_grad, up_grad, out_grad_w, qkv_grad), input_grad)
    out_grad_w, qkv_grad = out_grad_w.T.astype(F32), qkv_grad.astype(F32)

    return (
        output,
        input_grad,
        gains[:gains.shape[0] // 2],
        qkv_grad[:, :q_width],
        qkv_grad[:, q_width:q_width + k_width],
        qkv_grad[:, q_width + k_width:used],
        out_grad_w,
        gains[gains.shape[0] // 2:],
        gate_grad.astype(F32),
        up_grad.astype(F32),
        down_grad.T.astype(F32),
    )


def solution(mesh):
    rows, weight_in, weight_out = P(("dp", "tensor"), None), P("dp", "tensor"), P("tensor", "dp")
    in_specs = (rows, P("dp", None), P("dp"), weight_in, weight_in, weight_in, weight_out, P("dp"),
                weight_in, weight_in, weight_out, rows)
    gain = P(("dp", "tensor"))
    out_specs = (rows, rows, gain, weight_in, weight_in, weight_in, weight_out, gain, weight_in, weight_in, weight_out)
    return jax.shard_map(body, mesh=mesh, in_specs=in_specs, out_specs=out_specs, check_vma=False)
```

```python
import functools

import jax
import jax.numpy as jnp
from jax import lax
from jax.experimental import pallas as pl
from jax.experimental.pallas import tpu as pltpu
from jax.sharding import PartitionSpec as P

HD = 80
LANES = 128
WINDOW = 4096
EPS = 1e-05
THETA = 10000.0
NEG = -1e30
LOG2E = 1.4426950408889634
BLK = 256
HEADS_AT_ONCE = 1
BF = jnp.bfloat16
F32 = jnp.float32


def turn(x, c, s):
    return x * c + pltpu.roll(x, LANES // 2, 1) * s


def turn_back(x, c, s):
    return x * c - pltpu.roll(x, LANES // 2, 1) * s


def allowed(start, first_row, rows, first_col, cols):
    row = first_row + lax.broadcasted_iota(jnp.int32, (rows, cols), 0)
    col = first_col + lax.broadcasted_iota(jnp.int32, (rows, cols), 1)
    return (col >= start) & (col <= row) & (row - col < WINDOW)


def nt(a, b):
    return lax.dot_general(a, b, (((1,), (1,)), ((), ())), preferred_element_type=F32)


def nn(a, b):
    return lax.dot_general(a, b, (((1,), (0,)), ((), ())), preferred_element_type=F32)


def tn(a, b):
    return lax.dot_general(a, b, (((0,), (0,)), ((), ())), preferred_element_type=F32)


def fwd_kernel(groups, scale, lo_ref, qr_ref, kr_ref, vb_ref, start_ref, o_ref, lse_ref):
    length = qr_ref.shape[0]
    for i in range(length // BLK):
        rows = slice(i * BLK, (i + 1) * BLK)
        for j in range(i + 1):
            cols = slice(j * BLK, (i + 1) * BLK)
            width = (i + 1 - j) * BLK

            @pl.when(lo_ref[i] == j)
            def _():
                ok = allowed(start_ref[rows, :], i * BLK, BLK, j * BLK, width)

                @pl.loop(0, groups, unroll=HEADS_AT_ONCE)
                def _(g):
                    lanes = pl.ds(pl.multiple_of(g * LANES, LANES), LANES)
                    scores = nt(qr_ref[rows, lanes], kr_ref[cols, :]) * (scale * LOG2E)
                    scores = jnp.where(ok, scores, NEG)
                    top = jnp.max(scores, axis=1, keepdims=True)
                    e = jnp.exp2(scores - top)
                    total = jnp.sum(e, axis=1, keepdims=True)
                    mixed = nn(e.astype(BF), vb_ref[cols, :])
                    o_ref[rows, lanes] = (mixed / total).astype(BF)
                    lse = lse_ref[rows, :]
                    here = lax.broadcasted_iota(jnp.int32, lse.shape, 1) == g
                    lse_ref[rows, :] = jnp.where(here, top + jnp.log2(total), lse)


def bwd_kernel(groups, scale, lo_ref, qr_ref, kr_ref, vb_ref, do_ref, c_ref, s_ref, start_ref, lse_ref,
               dq_ref, dk_ref, dv_ref, dk_acc, dv_acc):
    length = qr_ref.shape[0]
    dk_acc[...] = jnp.zeros_like(dk_acc)
    dv_acc[...] = jnp.zeros_like(dv_acc)
    for i in range(length // BLK):
        rows = slice(i * BLK, (i + 1) * BLK)
        for j in range(i + 1):
            cols = slice(j * BLK, (i + 1) * BLK)
            width = (i + 1 - j) * BLK

            @pl.when(lo_ref[i] == j)
            def _():
                ok = allowed(start_ref[rows, :], i * BLK, BLK, j * BLK, width)

                @pl.loop(0, groups, unroll=HEADS_AT_ONCE)
                def _(g):
                    lanes = pl.ds(pl.multiple_of(g * LANES, LANES), LANES)
                    lse = lse_ref[rows, :]
                    here = lax.broadcasted_iota(jnp.int32, lse.shape, 1) == g
                    lse = jnp.sum(jnp.where(here, lse, 0.0), axis=1, keepdims=True)
                    q, do = qr_ref[rows, lanes], do_ref[rows, lanes]
                    k, v = kr_ref[cols, :], vb_ref[cols, :]
                    scores = nt(q, k) * (scale * LOG2E)
                    p = jnp.exp2(jnp.where(ok, scores, NEG) - lse)
                    pd = p * nt(do, v)
                    ds = (pd - p * jnp.sum(pd, axis=1, keepdims=True)).astype(BF)
                    dq = nn(ds, k) * scale
                    dq_ref[rows, lanes] = turn_back(dq, c_ref[rows, :], s_ref[rows, :]).astype(BF)
                    dk_acc[cols, :] += tn(ds, q)
                    dv_acc[cols, :] += tn(p.astype(BF), do)
    dk_ref[...] = turn_back(dk_acc[...] * scale, c_ref[...], s_ref[...]).astype(BF)
    dv_ref[...] = dv_acc[...].astype(BF)


def attend(proj, tables, kv, groups):
    start, lo = tables[2:]
    rows = proj.shape[0]
    at = lambda width, first: pl.BlockSpec((rows, width), lambda h, lo: (0, first + h))
    wide = groups * LANES
    return pl.pallas_call(
        functools.partial(fwd_kernel, groups, HD ** -0.5),
        grid_spec=pltpu.PrefetchScalarGridSpec(
            num_scalar_prefetch=1,
            grid=(kv,),
            in_specs=[at(wide, 0), at(LANES, kv * groups), at(LANES, kv * groups + kv),
                      pl.BlockSpec((rows, 1), lambda h, lo: (0, 0))],
            out_specs=[at(wide, 0), pl.BlockSpec((None, rows, groups), lambda h, lo: (h, 0, 0))],
        ),
        out_shape=[jax.ShapeDtypeStruct((rows, kv * wide), BF), jax.ShapeDtypeStruct((kv, rows, groups), F32)],
        compiler_params=pltpu.CompilerParams(vmem_limit_bytes=48 * 2 ** 20),
        cost_estimate=cost(kv * groups * rows * rows * LANES), name="attend",
    )(lo, proj, proj, proj, start)


def attend_back(proj, d_o, tables, lse, kv, groups):
    cos_t, sin_t, start, lo = tables
    rows = proj.shape[0]
    whole = lambda width: pl.BlockSpec((rows, width), lambda h, lo: (0, 0))
    at = lambda width, first=0: pl.BlockSpec((rows, width), lambda h, lo: (0, first + h))
    wide = groups * LANES
    out = lambda width: jax.ShapeDtypeStruct((rows, kv * width), BF)
    return pl.pallas_call(
        functools.partial(bwd_kernel, groups, HD ** -0.5),
        grid_spec=pltpu.PrefetchScalarGridSpec(
            num_scalar_prefetch=1,
            grid=(kv,),
            in_specs=[at(wide), at(LANES, kv * groups), at(LANES, kv * groups + kv), at(wide), whole(LANES), whole(LANES), whole(1),
                      pl.BlockSpec((None, rows, groups), lambda h, lo: (h, 0, 0))],
            out_specs=[at(wide), at(LANES), at(LANES)],
            scratch_shapes=[pltpu.VMEM((rows, LANES), F32)] * 2,
        ),
        out_shape=[out(wide), out(LANES), out(LANES)],
        compiler_params=pltpu.CompilerParams(vmem_limit_bytes=48 * 2 ** 20),
        cost_estimate=cost(4 * kv * groups * rows * rows * LANES),
        name="attend_back",
    )(lo, proj, proj, proj, d_o, cos_t, sin_t, start, lse)


COLS = 256
FINISH_COST = 52 * 10 ** 9


def cost(flops):
    return pl.CostEstimate(flops=flops, bytes_accessed=0, transcendentals=0)


def params():
    return pltpu.CompilerParams(vmem_limit_bytes=56 * 2 ** 20)


def project_kernel(heads, kv, parts, at_ref, n1_ref, eq_ref, ek_ref, c_ref, s_ref, *refs):
    w_refs, out_ref = refs[:parts], refs[parts]
    q_width = heads * HD
    step = pl.program_id(0)

    def go(columns, spread, turned):
        proj = None
        for i, w_ref in enumerate(w_refs):
            depth = w_ref.shape[0]
            a = n1_ref[...] if parts == 1 else n1_ref[:, pl.ds(pl.multiple_of(at_ref[i] * depth, depth), depth)]
            part = nn(a, nn(w_ref[:, columns], spread).astype(BF))
            proj = part if proj is None else proj + part
        for h in range(proj.shape[1] // LANES):
            lanes = slice(h * LANES, (h + 1) * LANES)
            head = proj[:, lanes]
            out_ref[:, lanes] = (turn(head, c_ref[...], s_ref[...]) if h < turned else head).astype(BF)

    @pl.when(step < heads // (2 * kv))
    def _():
        go(slice(0, q_width), eq_ref[...], 2 * kv)

    @pl.when(step == heads // (2 * kv))
    def _():
        go(slice(q_width, w_refs[0].shape[1]), ek_ref[...], kv)


def project(n1, w_parts, at, tables, heads, kv):
    cos_t, sin_t = tables[:2]
    rows, d = n1.shape
    per = 2 * kv
    steps = heads // per + 1
    whole = lambda shape: pl.BlockSpec(shape, lambda i, at: (0, 0))
    e_k = jnp.pad(spread_matrix(2 * kv), ((0, w_parts[0].shape[1] - (heads + 2 * kv) * HD), (0, 0)))
    return pl.pallas_call(
        functools.partial(project_kernel, heads, kv, len(w_parts)),
        grid_spec=pltpu.PrefetchScalarGridSpec(
            num_scalar_prefetch=1,
            grid=(steps,),
            in_specs=[whole((rows, d)),
                      pl.BlockSpec((heads * HD, per * LANES), lambda i, at: (0, jnp.minimum(i, heads // per - 1))),
                      whole(e_k.shape), whole(cos_t.shape), whole(sin_t.shape)] + [whole(w.shape) for w in w_parts],
            out_specs=pl.BlockSpec((rows, per * LANES), lambda i, at: (0, i)),
        ),
        out_shape=jax.ShapeDtypeStruct((rows, steps * per * LANES), BF),
        compiler_params=params(), cost_estimate=cost(rows * d * steps * per * LANES // 2), name="project",
    )(at, n1, spread_matrix(heads), e_k, cos_t, sin_t, *w_parts)


def heads_back_kernel(d_ref, w_ref, e_ref, out_ref):
    out_ref[...] = nn(nn(d_ref[...], w_ref[...]).astype(BF), e_ref[...]).astype(BF)


def heads_back(grad, w_t, heads):
    (rows, d), size = grad.shape, 256
    e = spread_matrix(heads)
    return pl.pallas_call(
        heads_back_kernel,
        grid=(rows // size,),
        in_specs=[pl.BlockSpec((size, d), lambda i: (i, 0)), pl.BlockSpec(w_t.shape, lambda i: (0, 0)),
                  pl.BlockSpec(e.shape, lambda i: (0, 0))],
        out_specs=pl.BlockSpec((size, heads * LANES), lambda i: (i, 0)),
        out_shape=jax.ShapeDtypeStruct((rows, heads * LANES), BF),
        compiler_params=params(), cost_estimate=cost(2 * rows * heads * HD * (d + heads * LANES)), name="heads_back",
    )(grad, w_t, e)


def gate_up_kernel(sizes, *refs):
    n2_refs, (wg_ref, wu_ref), outs = refs[:-3 * len(sizes) - 2], refs[-3 * len(sizes) - 2:-3 * len(sizes)], refs[-3 * len(sizes):]
    n2_refs = list(n2_refs)
    for i, pieces in enumerate(sizes):
        at = 0
        for rows in pieces:
            a = n2_refs.pop(0)[...]
            gate, up = nn(a, wg_ref[...]), nn(a, wu_ref[...])
            here = slice(at, at + rows)
            outs[3 * i][here, :] = gate.astype(BF)
            outs[3 * i + 1][here, :] = up.astype(BF)
            outs[3 * i + 2][here, :] = (gate / (1.0 + jnp.exp(-gate)) * up).astype(BF)
            at += rows


def gate_up(blocks, w_gate, w_up):
    sizes = [[p.shape[0] for p in pieces] for pieces in blocks]
    flat = [p for pieces in blocks for p in pieces]
    d, ff = w_gate.shape
    tile = lambda size: pl.BlockSpec((size, COLS), lambda i: (0, i))
    outs = pl.pallas_call(
        functools.partial(gate_up_kernel, sizes),
        grid=(pl.cdiv(ff, COLS),),
        in_specs=[pl.BlockSpec(p.shape, lambda i: (0, 0)) for p in flat] + [tile(d)] * 2,
        out_specs=[tile(sum(pieces)) for pieces in sizes for _ in range(3)],
        out_shape=[jax.ShapeDtypeStruct((sum(pieces), ff), BF) for pieces in sizes for _ in range(3)],
        compiler_params=params(), cost_estimate=cost(4 * sum(map(sum, sizes)) * d * ff), name="gate_up",
    )(*flat, w_gate, w_up)
    return [outs[3 * i:3 * i + 3] for i in range(len(blocks))]


def gate_up_back_kernel(ff, n, parts, *refs):
    blocks, (wg_ref, wu_ref, wd_ref), refs = refs[:3 * n], refs[3 * n:3 * n + 3], refs[3 * n + 3:]
    d_refs, p_refs, accs = refs[:2 * n], refs[2 * n:-n], refs[-n:]
    step, last = pl.program_id(0), pl.num_programs(0) - 1
    for i in range(n):
        dy_ref, g_ref, u_ref = blocks[3 * i:3 * i + 3]
        d_hidden = nn(dy_ref[...], wd_ref[...])
        gate, up = g_ref[...].astype(F32), u_ref[...].astype(F32)
        sig = 1.0 / (1.0 + jnp.exp(-gate))
        act = gate * sig
        d_refs[2 * i][...] = (d_hidden * up * (sig + act * (1.0 - sig))).astype(BF)
        d_refs[2 * i + 1][...] = (d_hidden * act).astype(BF)

    @pl.when(step == 0)
    def _():
        for i in range(n):
            accs[i][...] = nt(d_refs[2 * i][...], wg_ref[...]) + nt(d_refs[2 * i + 1][...], wu_ref[...])

    @pl.when((step > 0) & (step < last))
    def _():
        for i in range(n):
            accs[i][...] += nt(d_refs[2 * i][...], wg_ref[...]) + nt(d_refs[2 * i + 1][...], wu_ref[...])

    @pl.when(step == last)
    def _():
        def inside(v):
            col = last * COLS + lax.broadcasted_iota(jnp.int32, v.shape, 1)
            return jnp.where(col < ff, v, jnp.zeros_like(v))

        w_g, w_u = inside(wg_ref[...]), inside(wu_ref[...])
        for i in range(n):
            total = accs[i][...] + nt(inside(d_refs[2 * i][...]), w_g) + nt(inside(d_refs[2 * i + 1][...]), w_u)
            size = total.shape[0] // parts
            for j in range(parts):
                p_refs[parts * i + j][...] = total[j * size:(j + 1) * size].astype(BF)


def gate_up_back(blocks, w_gate, w_up, w_down_t, parts):
    n, (rows, d), ff = len(blocks), blocks[0][0].shape, w_gate.shape[1]
    assert pl.cdiv(ff, COLS) > 1
    tile = lambda size: pl.BlockSpec((size, COLS), lambda i: (0, i))
    whole = pl.BlockSpec((rows, d), lambda i: (0, 0), pipeline_mode=pl.Buffered(1))
    piece = pl.BlockSpec((rows // parts, d), lambda i: (0, 0))
    outs = pl.pallas_call(
        functools.partial(gate_up_back_kernel, ff, n, parts),
        grid=(pl.cdiv(ff, COLS),),
        in_specs=[whole, tile(rows), tile(rows)] * n + [tile(d)] * 3,
        out_specs=[tile(rows)] * (2 * n) + [piece] * (parts * n),
        out_shape=[jax.ShapeDtypeStruct((rows, ff), BF)] * (2 * n)
        + [jax.ShapeDtypeStruct((rows // parts, d), BF)] * (parts * n),
        scratch_shapes=[pltpu.VMEM((rows, d), F32)] * n,
        compiler_params=pltpu.CompilerParams(vmem_limit_bytes=58 * 2 ** 20),
        cost_estimate=cost(6 * n * rows * d * ff), name="gate_up_back",
    )(*[v for block in blocks for v in block], w_gate, w_up, w_down_t)
    return [(*outs[2 * i:2 * i + 2], outs[2 * n + parts * i:2 * n + parts * (i + 1)]) for i in range(n)]


def down_kernel(h_ref, w_ref, *out_refs):
    out = nt(h_ref[...], w_ref[...])
    size = out.shape[0] // len(out_refs)
    for i, out_ref in enumerate(out_refs):
        out_ref[...] = out[i * size:(i + 1) * size].astype(out_ref.dtype)


def down(hidden, w_down_t, parts):
    (rows, ff), d = hidden.shape, w_down_t.shape[0]
    size = 512
    return pl.pallas_call(
        down_kernel,
        grid=(pl.cdiv(d, size),),
        in_specs=[pl.BlockSpec((rows, ff), lambda i: (0, 0)), pl.BlockSpec((size, ff), lambda i: (i, 0))],
        out_specs=[pl.BlockSpec((rows // parts, size), lambda i: (0, i))] * parts,
        out_shape=[jax.ShapeDtypeStruct((rows // parts, d), BF)] * parts,
        compiler_params=params(), cost_estimate=cost(0), name="down",
    )(hidden, w_down_t)


def wgrad_kernel(n, lists, tiles, *refs):
    a_refs, b_refs, (out, a_t) = refs[:n], list(refs[n:-2]), refs[-2:]
    step = pl.program_id(0)

    @pl.when(step == 0)
    def _():
        at = 0
        for a_ref in a_refs:
            a_t[:, at:at + a_ref.shape[0]] = a_ref[...].T
            at += a_ref.shape[0]

    for j, sizes in enumerate(lists):
        bs = [b_refs.pop(0) for _ in sizes]

        @pl.when(step // tiles == j)
        def _():
            total, at = None, 0
            for rows, b_ref in zip(sizes, bs):
                part = nn(a_t[:, at:at + rows], b_ref[...])
                total = part if total is None else total + part
                at += rows
            out[...] = total.astype(BF)


def wgrad(a_blocks, *b_lists):
    d, ff = a_blocks[0].shape[1], b_lists[0][0].shape[1]
    total = sum(a.shape[0] for a in a_blocks)
    lists = [[b.shape[0] for b in bs] for bs in b_lists]
    tiles = pl.cdiv(ff, COLS)
    b_spec = lambda b, j: pl.BlockSpec((b.shape[0], COLS), lambda i: (0, jnp.clip(i - j * tiles, 0, tiles - 1)))
    width = ff if len(lists) == 1 else len(lists) * tiles * COLS
    return pl.pallas_call(
        functools.partial(wgrad_kernel, len(a_blocks), lists, tiles),
        grid=(len(lists) * tiles,),
        in_specs=[pl.BlockSpec(a.shape, lambda i: (0, 0), pipeline_mode=pl.Buffered(1)) for a in a_blocks]
        + [b_spec(b, j) for j, bs in enumerate(b_lists) for b in bs],
        out_specs=pl.BlockSpec((d, COLS), lambda i: (0, i)),
        out_shape=jax.ShapeDtypeStruct((d, width), BF),
        scratch_shapes=[pltpu.VMEM((d, total), BF)],
        compiler_params=params(), cost_estimate=cost(total * d * ff * len(b_lists) // 4), name="wgrad",
    )(*a_blocks, *[b for bs in b_lists for b in bs])


def finish_kernel(eps, x_ref, gain_ref, own_ref, got_ref, dh_ref, out_ref):
    x = x_ref[...].astype(F32)
    inv = lax.rsqrt(jnp.mean(x * x, axis=1, keepdims=True) + eps)
    scaled = (own_ref[...] + got_ref[...].astype(F32)) * gain_ref[...]
    out_ref[...] = dh_ref[...] + inv * scaled - x * (inv * inv * inv * jnp.mean(scaled * x, axis=1, keepdims=True))


def finish(x, gain, own, got, dh):
    rows, d = x.shape
    size = min(128, rows)
    at = pl.BlockSpec((size, d), lambda i: (i, 0))
    return pl.pallas_call(
        functools.partial(finish_kernel, EPS),
        grid=(rows // size,),
        in_specs=[at, pl.BlockSpec((1, d), lambda i: (0, 0)), at, at, at],
        out_specs=at,
        out_shape=jax.ShapeDtypeStruct((rows, d), F32),
        compiler_params=params(), cost_estimate=cost(FINISH_COST), name="finish",
    )(x, gain[None, :], own, got, dh)


def doc_starts(seg_row):
    places = jnp.arange(seg_row.shape[0], dtype=jnp.int32)
    previous = jnp.concatenate([seg_row[:1] - 1, seg_row[:-1]])
    return lax.cummax(jnp.where(seg_row != previous, places, 0), axis=0)


def head_tables(positions):
    half = HD // 2
    freq = THETA ** (-(jnp.arange(half, dtype=F32) * 2.0 / HD))
    angles = positions.astype(F32)[:, None] * freq
    cosine, sine = jnp.cos(angles), jnp.sin(angles)
    gap = jnp.zeros((positions.shape[0], LANES // 2 - half), F32)
    return (jnp.concatenate([cosine, gap, cosine, gap], axis=1),
            jnp.concatenate([-sine, gap, sine, gap], axis=1))


def spread_matrix(heads):
    row = jnp.arange(heads * HD)
    feature = row % HD
    lane = (row // HD) * LANES + feature + jnp.where(feature >= HD // 2, LANES // 2 - HD // 2, 0)
    return (lane[:, None] == jnp.arange(heads * LANES)[None, :]).astype(BF)


def dot(a, b, out=BF):
    return jnp.dot(a, b, preferred_element_type=F32).astype(out)


def dot_t(a, b, out=BF):
    return lax.dot_general(a, b, (((0,), (0,)), ((), ())), preferred_element_type=F32).astype(out)


def dot_nt(a, b, out=BF):
    return lax.dot_general(a, b, (((1,), (1,)), ((), ())), preferred_element_type=F32).astype(out)


def inverse_rms(v):
    return lax.rsqrt(jnp.mean(v * v, axis=-1, keepdims=True) + EPS)


def norm_back(v, inv, gain, grad):
    scaled = grad * gain
    return inv * scaled - v * (inv * inv * inv * jnp.mean(scaled * v, axis=-1, keepdims=True))


def swap(v, bit):
    return lax.ppermute(v, "tensor", [(i, i ^ bit) for i in range(lax.axis_size("tensor"))])


def groups_of(size):
    return [[first + i for i in range(size)] for first in range(0, lax.axis_size("tensor"), size)]


def after(v, *done):
    return lax.optimization_barrier((v, *done))[0]


def square(size):
    return size == 4 == lax.axis_size("tensor")


def gather(mine, size):
    if size == 2:
        return [[mine], [swap(mine, 1)]]
    if square(size):
        half = mine.shape[0] // 2
        from_x, from_y = swap(mine, 1), swap(mine, 2)
        return [[mine], [from_x], [from_y], [swap(from_x[:half], 2), swap(from_y[half:], 1)]]
    blocks = lax.all_gather(mine, "tensor", axis=0, tiled=False, axis_index_groups=groups_of(size))
    at = lax.axis_index("tensor") % size
    return [[lax.dynamic_index_in_dim(blocks, at ^ r, 0, keepdims=False)] for r in range(size)]


def scatter(parts, size):
    if size == 2:
        return [swap(jnp.concatenate(parts[1]), 1)], parts[1]
    if square(size):
        _, (x_low, x_high), (y_low, y_high), (d_low, d_high) = parts
        for_y, for_x = swap(d_low, 1), swap(d_high, 2)
        a1, b1 = swap(x_low, 1), swap(y_high, 2)
        x_high, y_low = plus(x_high, for_x), plus(y_low, for_y)
        a2, b2 = swap(x_high, 1), swap(y_low, 2)
        return [a1, b2, a2, b1], [x_high, y_low]
    at = lax.axis_index("tensor") % size
    whole = [jnp.concatenate(p) for p in parts[1:]]
    blocks = jnp.stack([jnp.zeros_like(whole[0])] + whole)[jnp.arange(size) ^ at]
    return [lax.psum_scatter(blocks, "tensor", scatter_dimension=0, tiled=False, axis_index_groups=groups_of(size))], whole


def plus(a, b):
    return (a.astype(F32) + b.astype(F32)).astype(BF)


def summed(got):
    got = [v.astype(F32) for v in got]
    return got[0] if len(got) == 1 else jnp.concatenate([got[0] + got[1], got[2] + got[3]])


def scatter_rows(v):
    for axis in ("dp", "tensor"):
        size, at = lax.axis_size(axis), lax.axis_index(axis)
        assert size & (size - 1) == 0
        while size > 1:
            size //= 2
            bit = (at // size) % 2
            low, high = jnp.split(v, 2)
            theirs = lax.ppermute(jnp.where(bit == 0, high, low), axis,
                                  [(i, i ^ size) for i in range(lax.axis_size(axis))])
            v = jnp.where(bit == 0, low, high) + theirs
    return v


def in_order(blocks):
    blocks = [pieces[0] for pieces in blocks]
    at = lax.axis_index("tensor") % len(blocks)
    if len(blocks) == 2:
        return by_place(at, *blocks)
    return jnp.stack(blocks)[jnp.arange(len(blocks)) ^ at].reshape(-1, *blocks[0].shape[1:])


def by_place(bit, mine, other):
    return jnp.where(bit == 0, jnp.concatenate([mine, other]), jnp.concatenate([other, mine]))


def body(tokens, segments, attn_gain, w_query, w_key, w_value, w_out, mlp_gain, w_gate, w_up, w_down, out_grad):
    q_width, k_width = w_query.shape[1], w_key.shape[1]
    heads, kv = q_width // HD, k_width // HD
    groups = heads // kv
    row_count, width = tokens.shape
    seq_count, length = segments.shape
    ff = w_gate.shape[1]
    place, places = lax.axis_index("tensor"), lax.axis_size("tensor")
    group = places // seq_count
    core = lax.axis_index("dp") % 2

    token_blocks = gather(tokens, group)
    if square(places):
        dy_y = swap(out_grad, 2)
    used = q_width + 2 * k_width
    spare = jnp.zeros((w_query.shape[0], -(used + 2) % LANES), BF)
    qkv_shard = jnp.concatenate(
        [w_query, w_key, w_value, attn_gain[:, None], mlp_gain[:, None], spare], axis=1)
    qkv_all = lax.all_gather(qkv_shard, "dp", axis=0, tiled=True)
    if square(places):
        qkv_all, token_blocks, dy_y, later = lax.optimization_barrier((qkv_all, token_blocks, dy_y, out_grad))
        dy_x = swap(later, 1)
    else:
        dy_x = None
    gain_one = qkv_all[:, used].astype(F32)
    gain_two = qkv_all[:, used + 1].astype(F32)
    out_wt = lax.all_gather(after(w_out.T, qkv_all), "dp", axis=0, tiled=True)
    gate_w = lax.all_gather(after(w_gate, qkv_all), "dp", axis=0, tiled=True)
    up_w = lax.all_gather(after(w_up, qkv_all), "dp", axis=0, tiled=True)
    down_wt = lax.all_gather(after(w_down.T, out_wt), "dp", axis=0, tiled=True)

    def core_half(v):
        half = v.shape[0] // 2
        return lax.dynamic_slice_in_dim(v, core * half, half, 0)

    def other_half(got):
        return lax.ppermute(got, "dp", [(i, i ^ 1) for i in range(lax.axis_size("dp"))])

    def joined(got, pair):
        both = jnp.broadcast_to(pair[None], (2, *pair.shape)).reshape(-1, pair.shape[1])
        return lax.dynamic_update_slice_in_dim(both, got, core * got.shape[0], 0)

    others = [group * m for m in range(1, seq_count)]
    out_sent = core_half(out_wt)
    qkv_halves = [swap(core_half(qkv_all), bits) for bits in others]
    out_halves = [swap(out_sent, bits) for bits in others]

    def chip_half(part):
        half = part.shape[0] // 2
        theirs = lax.dynamic_slice_in_dim(part, (1 - core) * half, half, 0)
        theirs = lax.ppermute(theirs, "dp", [(i, i ^ 1) for i in range(lax.axis_size("dp"))])
        mine = lax.dynamic_slice_in_dim(part, core * half, half, 0)
        return plus(mine, theirs)

    seg_row = lax.dynamic_index_in_dim(segments, place // group, 0, keepdims=False)
    start = doc_starts(seg_row)
    cos_t, sin_t = head_tables(jnp.arange(length, dtype=jnp.int32) - start)
    tables = (cos_t, sin_t, start[:, None], start[::BLK] // BLK)

    spread_q, spread_k = spread_matrix(heads), spread_matrix(kv)

    x_own = tokens.astype(F32)
    inv_own = inverse_rms(x_own)
    x_pair = in_order(token_blocks).astype(F32)
    inv_pair = inverse_rms(x_pair)
    n1 = (x_pair * inv_pair * gain_one).astype(BF)
    proj = project(n1, [qkv_all], jnp.zeros((1,), jnp.int32), tables, heads, kv)
    proj = after(proj, out_sent)
    o, lse = attend(proj, tables, kv, groups)
    kept, qkv_ws, out_wts = [(dot_nt(o, spread_q), proj, lse)], [qkv_all], [out_wt]
    for qkv_got, out_got in zip(qkv_halves, out_halves):
        qkv_got, dy_x = lax.optimization_barrier((qkv_got, dy_x, o))[:2]
        parts = [qkv_got, other_half(qkv_got)]
        proj = project(n1, parts, jnp.stack([core, 1 - core]).astype(jnp.int32), tables, heads, kv)
        o, lse = attend(proj, tables, kv, groups)
        out_got = after(out_got, o)
        out_wts.append(joined(out_got, other_half(out_got)))
        qkv_ws.append(joined(*after(parts, o)))
        kept.append((dot_nt(o, spread_q), proj, lse))
    if square(places):
        dy_blocks = [out_grad, dy_x, dy_y, swap(dy_x, 2)]
    else:
        dy_blocks = [pieces[0] for pieces in gather(out_grad, places)]
    o_flat = jnp.concatenate([k[0] for k in kept], axis=1)
    out_both = jnp.concatenate(out_wts, axis=1)

    def rows_of(v, bits):
        return lax.dynamic_slice_in_dim(v, ((place % group) ^ bits) * row_count, row_count, 0)

    branch, _ = scatter([None] + [[dot_nt(rows_of(o_flat, bits), out_both)] for bits in range(1, group)], group)
    segs = segments.reshape(-1)

    def masked(v, bits):
        own = lax.dynamic_slice_in_dim(segs, (place ^ bits) * row_count, row_count, 0)
        return v * (own >= 0).astype(BF)[:, None]

    dys = [masked(block, bits) for bits, block in enumerate(dy_blocks)]
    branch, dys = lax.optimization_barrier((branch, dys))
    h = x_own + dot_nt(rows_of(o_flat, 0), out_both, F32) + summed(branch)

    inv_h = inverse_rms(h)
    n2 = (h * inv_h * gain_two).astype(BF)
    n2s = gather(after(n2, gate_w), places)
    first, qkv_ws = lax.optimization_barrier((n2s[:1], qkv_ws))
    ups = gate_up(first, gate_w, up_w)
    ups += gate_up(after(n2s[1:places - 1], ups[0]), gate_w, up_w)
    ups += gate_up(after(n2s[places - 1:], ups[1]), gate_w, up_w)
    n2_pieces = [p for pieces in n2s for p in pieces]
    hiddens = [u[2] for u in ups]
    down_part = wgrad(dys, hiddens)
    down_grad = lax.psum_scatter(down_part, "dp", scatter_dimension=0, tiled=True)
    back_blocks = [(dys[r], *ups[r][:2]) for r in range(places)]
    far = gate_up_back(after(back_blocks[places - 1:], down_part), gate_w, up_w, down_wt, 2)
    near = []
    for first in range(1, places - 1, 2):
        near += gate_up_back(after(back_blocks[first:min(first + 2, places - 1)], far), gate_w, up_w, down_wt, 2)
    got, sent = scatter([None, *(v[2] for v in near + far)], places)
    own = gate_up_back(after(back_blocks[:1], near, sent), gate_w, up_w, down_wt, 2)
    backs = own + near + far
    mlp_parts = [down(v, down_wt, 1)[0] for v in after(hiddens[1:], own)]
    n2_late, got = lax.optimization_barrier((n2_pieces, got, own, mlp_parts[:2]))[:2]
    gate_part = wgrad(n2_late, [v[0] for v in backs])
    gate_grad = lax.psum_scatter(gate_part, "dp", scatter_dimension=0, tiled=True)
    up_part = wgrad(after(n2_late, gate_part), [v[1] for v in backs])
    up_grad = lax.psum_scatter(up_part, "dp", scatter_dimension=0, tiled=True)
    got = after(got, up_part)
    d_n2 = summed(got) + jnp.concatenate(backs[0][2]).astype(F32)
    gain_two_grad = jnp.sum(d_n2 * h * inv_h, axis=0)
    dh = dys[0].astype(F32) + norm_back(h, inv_h, gain_two, d_n2)
    dhb = dh.astype(BF)
    late_hiddens, late_parts = after((hiddens[:1], mlp_parts[2:]), dhb)
    mlp_parts = [down(late_hiddens[0], down_wt, 1)[0], *mlp_parts[:2], *late_parts]

    dhb_blocks, mlp_parts, down_grad = lax.optimization_barrier((gather(dhb, group), mlp_parts, down_grad))
    dhb_pair = in_order(dhb_blocks)
    out_halves = [chip_half(dot_t(dhb_pair, k[0])) for k in kept[1:]]
    dhb_pair, mlp_parts = lax.optimization_barrier((dhb_pair, mlp_parts, out_halves))[:2]
    out_shares = [swap(v, bits) for v, bits in zip(out_halves, others)]
    if square(places):
        mlp_x = [swap(mlp_parts[3], 1), swap(mlp_parts[1], 1)]
    else:
        mlp_got = scatter([[v] for v in mlp_parts], places)[0]
    d_projs, qkv_shares = [], []
    for index in reversed(range(len(kept))):
        o, proj, lse = kept[index]
        d_o = heads_back(dhb_pair, out_wts[index], heads)
        dq, dk, dv = attend_back(proj, d_o, tables, lse, kv, groups)
        spare = jnp.zeros((dq.shape[0], qkv_all.shape[1] - used), BF)
        d_proj = jnp.concatenate([dot_nt(dq, spread_q), dot_nt(dk, spread_k), dot_nt(dv, spread_k), spare], axis=1)
        d_projs.insert(0, d_proj)
        last_dq = dq
        if index:
            part = dot_t(n1, d_proj)
            if square(places):
                part, far_got, out_shares = lax.optimization_barrier((part, mlp_x[0], out_shares))
            half = chip_half(part)
            qkv_shares.append(swap(half, others[index - 1]))
            dhb_pair = after(dhb_pair, half)

    def with_shares(mine, got):
        half = mine.shape[0] // 2
        rows = lax.dynamic_slice_in_dim(mine, core * half, half, 0).astype(F32) + sum(v.astype(F32) for v in got)
        return lax.dynamic_update_slice_in_dim(mine, rows.astype(BF), core * half, 0)

    out_part = dot_t(after(dhb_pair, last_dq), kept[0][0])
    out_grad_w = lax.psum_scatter(with_shares(out_part, out_shares), "dp", scatter_dimension=0, tiled=True)
    d_all, w_all = jnp.concatenate(d_projs, axis=1), jnp.concatenate(qkv_ws, axis=1)
    d_all, qkv_shares = lax.optimization_barrier((d_all, qkv_shares))
    d_n1_parts = [dot_nt(rows_of(d_all, bits), w_all) for bits in range(1, group)]
    d_n1_got, sent = scatter([None] + [[v] for v in d_n1_parts], group)
    d_n1_own = dot_nt(rows_of(d_all, 0), w_all, F32)
    gain_one_grad = jnp.sum(d_n1_own * x_own * inv_own, axis=0) + sum(
        jnp.sum(v.astype(F32) * token_blocks[bits][0].astype(F32) * rows_of(inv_pair, bits), axis=0)
        for bits, v in zip(range(1, group), d_n1_parts))
    if square(places):
        last_sum = plus(mlp_parts[2], far_got)
        mlp_got = [mlp_x[1], swap(last_sum, 2)]
        n1_late = after(n1, sent, mlp_x[1], last_sum, d_n1_own)
    else:
        n1_late = after(n1, sent, d_n1_own)
    qkv_part = dot_t(n1_late, d_projs[0])

    qkv_grad = lax.psum_scatter(with_shares(qkv_part, qkv_shares), "dp", scatter_dimension=0, tiled=True)
    d_n1_got, mlp_got = lax.optimization_barrier((d_n1_got, mlp_got))
    gain_one_grad, gain_two_grad = after((gain_one_grad, gain_two_grad), d_n1_got)
    gains = scatter_rows(jnp.concatenate(
        [v.reshape(lax.axis_size("dp") * places, -1) for v in (gain_one_grad, gain_two_grad)], axis=1))[0]
    output = (h + sum(v.astype(F32) for v in mlp_got) + mlp_parts[0].astype(F32)).astype(BF)
    input_grad = finish(tokens, gain_one, d_n1_own, summed(d_n1_got) if len(d_n1_got) > 1 else d_n1_got[0], dh)
    gate_grad, up_grad, out_grad_w, qkv_grad = after((gate_grad, up_grad, out_grad_w, qkv_grad), input_grad)
    out_grad_w, qkv_grad = out_grad_w.T.astype(F32), qkv_grad.astype(F32)

    return (
        output,
        input_grad,
        gains[:gains.shape[0] // 2],
        qkv_grad[:, :q_width],
        qkv_grad[:, q_width:q_width + k_width],
        qkv_grad[:, q_width + k_width:used],
        out_grad_w,
        gains[gains.shape[0] // 2:],
        gate_grad.astype(F32),
        up_grad.astype(F32),
        down_grad.T.astype(F32),
    )


def solution(mesh):
    rows, weight_in, weight_out = P(("dp", "tensor"), None), P("dp", "tensor"), P("tensor", "dp")
    in_specs = (rows, P("dp", None), P("dp"), weight_in, weight_in, weight_in, weight_out, P("dp"),
                weight_in, weight_in, weight_out, rows)
    gain = P(("dp", "tensor"))
    out_specs = (rows, rows, gain, weight_in, weight_in, weight_in, weight_out, gain, weight_in, weight_in, weight_out)
    return jax.shard_map(body, mesh=mesh, in_specs=in_specs, out_specs=out_specs, check_vma=False)
```

```python
import functools

import jax
import jax.numpy as jnp
from jax import lax
from jax.experimental import pallas as pl
from jax.experimental.pallas import tpu as pltpu
from jax.sharding import PartitionSpec as P

HD = 80
LANES = 128
WINDOW = 4096
EPS = 1e-05
THETA = 10000.0
NEG = -1e30
LOG2E = 1.4426950408889634
BLK = 256
HEADS_AT_ONCE = 1
BF = jnp.bfloat16
F32 = jnp.float32


def turn(x, c, s):
    return x * c + pltpu.roll(x, LANES // 2, 1) * s


def turn_back(x, c, s):
    return x * c - pltpu.roll(x, LANES // 2, 1) * s


def allowed(start, first_row, rows, first_col, cols):
    row = first_row + lax.broadcasted_iota(jnp.int32, (rows, cols), 0)
    col = first_col + lax.broadcasted_iota(jnp.int32, (rows, cols), 1)
    return (col >= start) & (col <= row) & (row - col < WINDOW)


def nt(a, b):
    return lax.dot_general(a, b, (((1,), (1,)), ((), ())), preferred_element_type=F32)


def nn(a, b):
    return lax.dot_general(a, b, (((1,), (0,)), ((), ())), preferred_element_type=F32)


def tn(a, b):
    return lax.dot_general(a, b, (((0,), (0,)), ((), ())), preferred_element_type=F32)


def fwd_kernel(groups, scale, lo_ref, qr_ref, kr_ref, vb_ref, start_ref, o_ref, lse_ref):
    length = qr_ref.shape[0]
    for i in range(length // BLK):
        rows = slice(i * BLK, (i + 1) * BLK)
        for j in range(i + 1):
            cols = slice(j * BLK, (i + 1) * BLK)
            width = (i + 1 - j) * BLK

            @pl.when(lo_ref[i] == j)
            def _():
                ok = allowed(start_ref[rows, :], i * BLK, BLK, j * BLK, width)

                @pl.loop(0, groups, unroll=HEADS_AT_ONCE)
                def _(g):
                    lanes = pl.ds(pl.multiple_of(g * LANES, LANES), LANES)
                    scores = nt(qr_ref[rows, lanes], kr_ref[cols, :]) * (scale * LOG2E)
                    scores = jnp.where(ok, scores, NEG)
                    top = jnp.max(scores, axis=1, keepdims=True)
                    e = jnp.exp2(scores - top)
                    total = jnp.sum(e, axis=1, keepdims=True)
                    mixed = nn(e.astype(BF), vb_ref[cols, :])
                    o_ref[rows, lanes] = (mixed / total).astype(BF)
                    lse = lse_ref[rows, :]
                    here = lax.broadcasted_iota(jnp.int32, lse.shape, 1) == g
                    lse_ref[rows, :] = jnp.where(here, top + jnp.log2(total), lse)


def bwd_kernel(groups, scale, lo_ref, qr_ref, kr_ref, vb_ref, do_ref, c_ref, s_ref, start_ref, lse_ref,
               dq_ref, dk_ref, dv_ref, dk_acc, dv_acc):
    length = qr_ref.shape[0]
    dk_acc[...] = jnp.zeros_like(dk_acc)
    dv_acc[...] = jnp.zeros_like(dv_acc)
    for i in range(length // BLK):
        rows = slice(i * BLK, (i + 1) * BLK)
        for j in range(i + 1):
            cols = slice(j * BLK, (i + 1) * BLK)
            width = (i + 1 - j) * BLK

            @pl.when(lo_ref[i] == j)
            def _():
                ok = allowed(start_ref[rows, :], i * BLK, BLK, j * BLK, width)

                @pl.loop(0, groups, unroll=HEADS_AT_ONCE)
                def _(g):
                    lanes = pl.ds(pl.multiple_of(g * LANES, LANES), LANES)
                    lse = lse_ref[rows, :]
                    here = lax.broadcasted_iota(jnp.int32, lse.shape, 1) == g
                    lse = jnp.sum(jnp.where(here, lse, 0.0), axis=1, keepdims=True)
                    q, do = qr_ref[rows, lanes], do_ref[rows, lanes]
                    k, v = kr_ref[cols, :], vb_ref[cols, :]
                    scores = nt(q, k) * (scale * LOG2E)
                    p = jnp.exp2(jnp.where(ok, scores, NEG) - lse)
                    pd = p * nt(do, v)
                    ds = (pd - p * jnp.sum(pd, axis=1, keepdims=True)).astype(BF)
                    dq = nn(ds, k) * scale
                    dq_ref[rows, lanes] = turn_back(dq, c_ref[rows, :], s_ref[rows, :]).astype(BF)
                    dk_acc[cols, :] += tn(ds, q)
                    dv_acc[cols, :] += tn(p.astype(BF), do)
    dk_ref[...] = turn_back(dk_acc[...] * scale, c_ref[...], s_ref[...]).astype(BF)
    dv_ref[...] = dv_acc[...].astype(BF)


def attend(proj, tables, kv, groups):
    start, lo = tables[2:]
    rows = proj.shape[0]
    at = lambda width, first: pl.BlockSpec((rows, width), lambda h, lo: (0, first + h))
    wide = groups * LANES
    return pl.pallas_call(
        functools.partial(fwd_kernel, groups, HD ** -0.5),
        grid_spec=pltpu.PrefetchScalarGridSpec(
            num_scalar_prefetch=1,
            grid=(kv,),
            in_specs=[at(wide, 0), at(LANES, kv * groups), at(LANES, kv * groups + kv),
                      pl.BlockSpec((rows, 1), lambda h, lo: (0, 0))],
            out_specs=[at(wide, 0), pl.BlockSpec((None, rows, groups), lambda h, lo: (h, 0, 0))],
        ),
        out_shape=[jax.ShapeDtypeStruct((rows, kv * wide), BF), jax.ShapeDtypeStruct((kv, rows, groups), F32)],
        compiler_params=pltpu.CompilerParams(vmem_limit_bytes=48 * 2 ** 20),
        cost_estimate=cost(kv * groups * rows * rows * LANES), name="attend",
    )(lo, proj, proj, proj, start)


def attend_back(proj, d_o, tables, lse, kv, groups):
    cos_t, sin_t, start, lo = tables
    rows = proj.shape[0]
    whole = lambda width: pl.BlockSpec((rows, width), lambda h, lo: (0, 0))
    at = lambda width, first=0: pl.BlockSpec((rows, width), lambda h, lo: (0, first + h))
    wide = groups * LANES
    out = lambda width: jax.ShapeDtypeStruct((rows, kv * width), BF)
    return pl.pallas_call(
        functools.partial(bwd_kernel, groups, HD ** -0.5),
        grid_spec=pltpu.PrefetchScalarGridSpec(
            num_scalar_prefetch=1,
            grid=(kv,),
            in_specs=[at(wide), at(LANES, kv * groups), at(LANES, kv * groups + kv), at(wide), whole(LANES), whole(LANES), whole(1),
                      pl.BlockSpec((None, rows, groups), lambda h, lo: (h, 0, 0))],
            out_specs=[at(wide), at(LANES), at(LANES)],
            scratch_shapes=[pltpu.VMEM((rows, LANES), F32)] * 2,
        ),
        out_shape=[out(wide), out(LANES), out(LANES)],
        compiler_params=pltpu.CompilerParams(vmem_limit_bytes=48 * 2 ** 20),
        cost_estimate=cost(4 * kv * groups * rows * rows * LANES),
        name="attend_back",
    )(lo, proj, proj, proj, d_o, cos_t, sin_t, start, lse)


COLS = 256
FINISH_COST = 52 * 10 ** 9


def cost(flops):
    return pl.CostEstimate(flops=flops, bytes_accessed=0, transcendentals=0)


def params():
    return pltpu.CompilerParams(vmem_limit_bytes=56 * 2 ** 20)


def project_kernel(heads, kv, parts, at_ref, n1_ref, eq_ref, ek_ref, c_ref, s_ref, *refs):
    w_refs, out_ref = refs[:parts], refs[parts]
    q_width = heads * HD
    step = pl.program_id(0)

    def go(columns, spread, turned):
        proj = None
        for i, w_ref in enumerate(w_refs):
            depth = w_ref.shape[0]
            a = n1_ref[...] if parts == 1 else n1_ref[:, pl.ds(pl.multiple_of(at_ref[i] * depth, depth), depth)]
            part = nn(a, nn(w_ref[:, columns], spread).astype(BF))
            proj = part if proj is None else proj + part
        for h in range(proj.shape[1] // LANES):
            lanes = slice(h * LANES, (h + 1) * LANES)
            head = proj[:, lanes]
            out_ref[:, lanes] = (turn(head, c_ref[...], s_ref[...]) if h < turned else head).astype(BF)

    @pl.when(step < heads // (2 * kv))
    def _():
        go(slice(0, q_width), eq_ref[...], 2 * kv)

    @pl.when(step == heads // (2 * kv))
    def _():
        go(slice(q_width, w_refs[0].shape[1]), ek_ref[...], kv)


def project(n1, w_parts, at, tables, heads, kv):
    cos_t, sin_t = tables[:2]
    rows, d = n1.shape
    per = 2 * kv
    steps = heads // per + 1
    whole = lambda shape: pl.BlockSpec(shape, lambda i, at: (0, 0))
    e_k = jnp.pad(spread_matrix(2 * kv), ((0, w_parts[0].shape[1] - (heads + 2 * kv) * HD), (0, 0)))
    return pl.pallas_call(
        functools.partial(project_kernel, heads, kv, len(w_parts)),
        grid_spec=pltpu.PrefetchScalarGridSpec(
            num_scalar_prefetch=1,
            grid=(steps,),
            in_specs=[whole((rows, d)),
                      pl.BlockSpec((heads * HD, per * LANES), lambda i, at: (0, jnp.minimum(i, heads // per - 1))),
                      whole(e_k.shape), whole(cos_t.shape), whole(sin_t.shape)] + [whole(w.shape) for w in w_parts],
            out_specs=pl.BlockSpec((rows, per * LANES), lambda i, at: (0, i)),
        ),
        out_shape=jax.ShapeDtypeStruct((rows, steps * per * LANES), BF),
        compiler_params=params(), cost_estimate=cost(rows * d * steps * per * LANES // 2), name="project",
    )(at, n1, spread_matrix(heads), e_k, cos_t, sin_t, *w_parts)


def heads_back_kernel(d_ref, w_ref, e_ref, out_ref):
    out_ref[...] = nn(nn(d_ref[...], w_ref[...]).astype(BF), e_ref[...]).astype(BF)


def heads_back(grad, w_t, heads):
    (rows, d), size = grad.shape, 256
    e = spread_matrix(heads)
    return pl.pallas_call(
        heads_back_kernel,
        grid=(rows // size,),
        in_specs=[pl.BlockSpec((size, d), lambda i: (i, 0)), pl.BlockSpec(w_t.shape, lambda i: (0, 0)),
                  pl.BlockSpec(e.shape, lambda i: (0, 0))],
        out_specs=pl.BlockSpec((size, heads * LANES), lambda i: (i, 0)),
        out_shape=jax.ShapeDtypeStruct((rows, heads * LANES), BF),
        compiler_params=params(), cost_estimate=cost(2 * rows * heads * HD * (d + heads * LANES)), name="heads_back",
    )(grad, w_t, e)


def gate_up_kernel(sizes, *refs):
    n2_refs, (wg_ref, wu_ref), outs = refs[:-3 * len(sizes) - 2], refs[-3 * len(sizes) - 2:-3 * len(sizes)], refs[-3 * len(sizes):]
    n2_refs = list(n2_refs)
    for i, pieces in enumerate(sizes):
        at = 0
        for rows in pieces:
            a = n2_refs.pop(0)[...]
            gate, up = nn(a, wg_ref[...]), nn(a, wu_ref[...])
            here = slice(at, at + rows)
            outs[3 * i][here, :] = gate.astype(BF)
            outs[3 * i + 1][here, :] = up.astype(BF)
            outs[3 * i + 2][here, :] = (gate / (1.0 + jnp.exp(-gate)) * up).astype(BF)
            at += rows


def gate_up(blocks, w_gate, w_up):
    sizes = [[p.shape[0] for p in pieces] for pieces in blocks]
    flat = [p for pieces in blocks for p in pieces]
    d, ff = w_gate.shape
    tile = lambda size: pl.BlockSpec((size, COLS), lambda i: (0, i))
    outs = pl.pallas_call(
        functools.partial(gate_up_kernel, sizes),
        grid=(pl.cdiv(ff, COLS),),
        in_specs=[pl.BlockSpec(p.shape, lambda i: (0, 0)) for p in flat] + [tile(d)] * 2,
        out_specs=[tile(sum(pieces)) for pieces in sizes for _ in range(3)],
        out_shape=[jax.ShapeDtypeStruct((sum(pieces), ff), BF) for pieces in sizes for _ in range(3)],
        compiler_params=params(), cost_estimate=cost(4 * sum(map(sum, sizes)) * d * ff), name="gate_up",
    )(*flat, w_gate, w_up)
    return [outs[3 * i:3 * i + 3] for i in range(len(blocks))]


def gate_up_back_kernel(ff, n, parts, *refs):
    blocks, (wg_ref, wu_ref, wd_ref), refs = refs[:3 * n], refs[3 * n:3 * n + 3], refs[3 * n + 3:]
    d_refs, p_refs, accs = refs[:2 * n], refs[2 * n:-n], refs[-n:]
    step, last = pl.program_id(0), pl.num_programs(0) - 1
    for i in range(n):
        dy_ref, g_ref, u_ref = blocks[3 * i:3 * i + 3]
        d_hidden = nn(dy_ref[...], wd_ref[...])
        gate, up = g_ref[...].astype(F32), u_ref[...].astype(F32)
        sig = 1.0 / (1.0 + jnp.exp(-gate))
        act = gate * sig
        d_refs[2 * i][...] = (d_hidden * up * (sig + act * (1.0 - sig))).astype(BF)
        d_refs[2 * i + 1][...] = (d_hidden * act).astype(BF)

    @pl.when(step == 0)
    def _():
        for i in range(n):
            accs[i][...] = nt(d_refs[2 * i][...], wg_ref[...]) + nt(d_refs[2 * i + 1][...], wu_ref[...])

    @pl.when((step > 0) & (step < last))
    def _():
        for i in range(n):
            accs[i][...] += nt(d_refs[2 * i][...], wg_ref[...]) + nt(d_refs[2 * i + 1][...], wu_ref[...])

    @pl.when(step == last)
    def _():
        def inside(v):
            col = last * COLS + lax.broadcasted_iota(jnp.int32, v.shape, 1)
            return jnp.where(col < ff, v, jnp.zeros_like(v))

        w_g, w_u = inside(wg_ref[...]), inside(wu_ref[...])
        for i in range(n):
            total = accs[i][...] + nt(inside(d_refs[2 * i][...]), w_g) + nt(inside(d_refs[2 * i + 1][...]), w_u)
            size = total.shape[0] // parts
            for j in range(parts):
                p_refs[parts * i + j][...] = total[j * size:(j + 1) * size].astype(BF)


def gate_up_back(blocks, w_gate, w_up, w_down_t, parts):
    n, (rows, d), ff = len(blocks), blocks[0][0].shape, w_gate.shape[1]
    assert pl.cdiv(ff, COLS) > 1
    tile = lambda size: pl.BlockSpec((size, COLS), lambda i: (0, i))
    whole = pl.BlockSpec((rows, d), lambda i: (0, 0), pipeline_mode=pl.Buffered(1))
    piece = pl.BlockSpec((rows // parts, d), lambda i: (0, 0))
    outs = pl.pallas_call(
        functools.partial(gate_up_back_kernel, ff, n, parts),
        grid=(pl.cdiv(ff, COLS),),
        in_specs=[whole, tile(rows), tile(rows)] * n + [tile(d)] * 3,
        out_specs=[tile(rows)] * (2 * n) + [piece] * (parts * n),
        out_shape=[jax.ShapeDtypeStruct((rows, ff), BF)] * (2 * n)
        + [jax.ShapeDtypeStruct((rows // parts, d), BF)] * (parts * n),
        scratch_shapes=[pltpu.VMEM((rows, d), F32)] * n,
        compiler_params=pltpu.CompilerParams(vmem_limit_bytes=58 * 2 ** 20),
        cost_estimate=cost(6 * n * rows * d * ff), name="gate_up_back",
    )(*[v for block in blocks for v in block], w_gate, w_up, w_down_t)
    return [(*outs[2 * i:2 * i + 2], outs[2 * n + parts * i:2 * n + parts * (i + 1)]) for i in range(n)]


def down_kernel(h_ref, w_ref, *out_refs):
    out = nt(h_ref[...], w_ref[...])
    size = out.shape[0] // len(out_refs)
    for i, out_ref in enumerate(out_refs):
        out_ref[...] = out[i * size:(i + 1) * size].astype(out_ref.dtype)


def down(hidden, w_down_t, parts):
    (rows, ff), d = hidden.shape, w_down_t.shape[0]
    size = 512
    return pl.pallas_call(
        down_kernel,
        grid=(pl.cdiv(d, size),),
        in_specs=[pl.BlockSpec((rows, ff), lambda i: (0, 0)), pl.BlockSpec((size, ff), lambda i: (i, 0))],
        out_specs=[pl.BlockSpec((rows // parts, size), lambda i: (0, i))] * parts,
        out_shape=[jax.ShapeDtypeStruct((rows // parts, d), BF)] * parts,
        compiler_params=params(), cost_estimate=cost(0), name="down",
    )(hidden, w_down_t)


def wgrad_kernel(n, lists, tiles, *refs):
    a_refs, b_refs, (out, a_t) = refs[:n], list(refs[n:-2]), refs[-2:]
    step = pl.program_id(0)

    @pl.when(step == 0)
    def _():
        at = 0
        for a_ref in a_refs:
            a_t[:, at:at + a_ref.shape[0]] = a_ref[...].T
            at += a_ref.shape[0]

    for j, sizes in enumerate(lists):
        bs = [b_refs.pop(0) for _ in sizes]

        @pl.when(step // tiles == j)
        def _():
            total, at = None, 0
            for rows, b_ref in zip(sizes, bs):
                part = nn(a_t[:, at:at + rows], b_ref[...])
                total = part if total is None else total + part
                at += rows
            out[...] = total.astype(BF)


def wgrad(a_blocks, *b_lists):
    d, ff = a_blocks[0].shape[1], b_lists[0][0].shape[1]
    total = sum(a.shape[0] for a in a_blocks)
    lists = [[b.shape[0] for b in bs] for bs in b_lists]
    tiles = pl.cdiv(ff, COLS)
    b_spec = lambda b, j: pl.BlockSpec((b.shape[0], COLS), lambda i: (0, jnp.clip(i - j * tiles, 0, tiles - 1)))
    width = ff if len(lists) == 1 else len(lists) * tiles * COLS
    return pl.pallas_call(
        functools.partial(wgrad_kernel, len(a_blocks), lists, tiles),
        grid=(len(lists) * tiles,),
        in_specs=[pl.BlockSpec(a.shape, lambda i: (0, 0), pipeline_mode=pl.Buffered(1)) for a in a_blocks]
        + [b_spec(b, j) for j, bs in enumerate(b_lists) for b in bs],
        out_specs=pl.BlockSpec((d, COLS), lambda i: (0, i)),
        out_shape=jax.ShapeDtypeStruct((d, width), BF),
        scratch_shapes=[pltpu.VMEM((d, total), BF)],
        compiler_params=params(), cost_estimate=cost(total * d * ff * len(b_lists) // 4), name="wgrad",
    )(*a_blocks, *[b for bs in b_lists for b in bs])


def finish_kernel(eps, x_ref, gain_ref, own_ref, got_ref, dh_ref, out_ref):
    x = x_ref[...].astype(F32)
    inv = lax.rsqrt(jnp.mean(x * x, axis=1, keepdims=True) + eps)
    scaled = (own_ref[...] + got_ref[...].astype(F32)) * gain_ref[...]
    out_ref[...] = dh_ref[...] + inv * scaled - x * (inv * inv * inv * jnp.mean(scaled * x, axis=1, keepdims=True))


def finish(x, gain, own, got, dh):
    rows, d = x.shape
    size = min(128, rows)
    at = pl.BlockSpec((size, d), lambda i: (i, 0))
    return pl.pallas_call(
        functools.partial(finish_kernel, EPS),
        grid=(rows // size,),
        in_specs=[at, pl.BlockSpec((1, d), lambda i: (0, 0)), at, at, at],
        out_specs=at,
        out_shape=jax.ShapeDtypeStruct((rows, d), F32),
        compiler_params=params(), cost_estimate=cost(FINISH_COST), name="finish",
    )(x, gain[None, :], own, got, dh)


def doc_starts(seg_row):
    places = jnp.arange(seg_row.shape[0], dtype=jnp.int32)
    previous = jnp.concatenate([seg_row[:1] - 1, seg_row[:-1]])
    return lax.cummax(jnp.where(seg_row != previous, places, 0), axis=0)


def head_tables(positions):
    half = HD // 2
    freq = THETA ** (-(jnp.arange(half, dtype=F32) * 2.0 / HD))
    angles = positions.astype(F32)[:, None] * freq
    cosine, sine = jnp.cos(angles), jnp.sin(angles)
    gap = jnp.zeros((positions.shape[0], LANES // 2 - half), F32)
    return (jnp.concatenate([cosine, gap, cosine, gap], axis=1),
            jnp.concatenate([-sine, gap, sine, gap], axis=1))


def spread_matrix(heads):
    row = jnp.arange(heads * HD)
    feature = row % HD
    lane = (row // HD) * LANES + feature + jnp.where(feature >= HD // 2, LANES // 2 - HD // 2, 0)
    return (lane[:, None] == jnp.arange(heads * LANES)[None, :]).astype(BF)


def dot(a, b, out=BF):
    return jnp.dot(a, b, preferred_element_type=F32).astype(out)


def dot_t(a, b, out=BF):
    return lax.dot_general(a, b, (((0,), (0,)), ((), ())), preferred_element_type=F32).astype(out)


def dot_nt(a, b, out=BF):
    return lax.dot_general(a, b, (((1,), (1,)), ((), ())), preferred_element_type=F32).astype(out)


def inverse_rms(v):
    return lax.rsqrt(jnp.mean(v * v, axis=-1, keepdims=True) + EPS)


def norm_back(v, inv, gain, grad):
    scaled = grad * gain
    return inv * scaled - v * (inv * inv * inv * jnp.mean(scaled * v, axis=-1, keepdims=True))


def swap(v, bit):
    return lax.ppermute(v, "tensor", [(i, i ^ bit) for i in range(lax.axis_size("tensor"))])


def groups_of(size):
    return [[first + i for i in range(size)] for first in range(0, lax.axis_size("tensor"), size)]


def after(v, *done):
    return lax.optimization_barrier((v, *done))[0]


def square(size):
    return size == 4 == lax.axis_size("tensor")


def gather(mine, size):
    if size == 2:
        return [[mine], [swap(mine, 1)]]
    if square(size):
        half = mine.shape[0] // 2
        from_x, from_y = swap(mine, 1), swap(mine, 2)
        return [[mine], [from_x], [from_y], [swap(from_x[:half], 2), swap(from_y[half:], 1)]]
    blocks = lax.all_gather(mine, "tensor", axis=0, tiled=False, axis_index_groups=groups_of(size))
    at = lax.axis_index("tensor") % size
    return [[lax.dynamic_index_in_dim(blocks, at ^ r, 0, keepdims=False)] for r in range(size)]


def scatter(parts, size):
    if size == 2:
        return [swap(jnp.concatenate(parts[1]), 1)], parts[1]
    if square(size):
        _, (x_low, x_high), (y_low, y_high), (d_low, d_high) = parts
        for_y, for_x = swap(d_low, 1), swap(d_high, 2)
        a1, b1 = swap(x_low, 1), swap(y_high, 2)
        x_high, y_low = plus(x_high, for_x), plus(y_low, for_y)
        a2, b2 = swap(x_high, 1), swap(y_low, 2)
        return [a1, b2, a2, b1], [x_high, y_low]
    at = lax.axis_index("tensor") % size
    whole = [jnp.concatenate(p) for p in parts[1:]]
    blocks = jnp.stack([jnp.zeros_like(whole[0])] + whole)[jnp.arange(size) ^ at]
    return [lax.psum_scatter(blocks, "tensor", scatter_dimension=0, tiled=False, axis_index_groups=groups_of(size))], whole


def plus(a, b):
    return (a.astype(F32) + b.astype(F32)).astype(BF)


def summed(got):
    got = [v.astype(F32) for v in got]
    return got[0] if len(got) == 1 else jnp.concatenate([got[0] + got[1], got[2] + got[3]])


def scatter_rows(v):
    for axis in ("dp", "tensor"):
        size, at = lax.axis_size(axis), lax.axis_index(axis)
        assert size & (size - 1) == 0
        while size > 1:
            size //= 2
            bit = (at // size) % 2
            low, high = jnp.split(v, 2)
            theirs = lax.ppermute(jnp.where(bit == 0, high, low), axis,
                                  [(i, i ^ size) for i in range(lax.axis_size(axis))])
            v = jnp.where(bit == 0, low, high) + theirs
    return v


def in_order(blocks):
    blocks = [pieces[0] for pieces in blocks]
    at = lax.axis_index("tensor") % len(blocks)
    if len(blocks) == 2:
        return by_place(at, *blocks)
    return jnp.stack(blocks)[jnp.arange(len(blocks)) ^ at].reshape(-1, *blocks[0].shape[1:])


def by_place(bit, mine, other):
    return jnp.where(bit == 0, jnp.concatenate([mine, other]), jnp.concatenate([other, mine]))


def body(tokens, segments, attn_gain, w_query, w_key, w_value, w_out, mlp_gain, w_gate, w_up, w_down, out_grad):
    q_width, k_width = w_query.shape[1], w_key.shape[1]
    heads, kv = q_width // HD, k_width // HD
    groups = heads // kv
    row_count, width = tokens.shape
    seq_count, length = segments.shape
    ff = w_gate.shape[1]
    place, places = lax.axis_index("tensor"), lax.axis_size("tensor")
    group = places // seq_count
    core = lax.axis_index("dp") % 2

    token_blocks = gather(tokens, group)
    if square(places):
        dy_y = swap(out_grad, 2)
    used = q_width + 2 * k_width
    spare = jnp.zeros((w_query.shape[0], -(used + 2) % LANES), BF)
    qkv_shard = jnp.concatenate(
        [w_query, w_key, w_value, attn_gain[:, None], mlp_gain[:, None], spare], axis=1)
    qkv_all = lax.all_gather(qkv_shard, "dp", axis=0, tiled=True)
    if square(places):
        qkv_all, token_blocks, dy_y, later = lax.optimization_barrier((qkv_all, token_blocks, dy_y, out_grad))
        dy_x = swap(later, 1)
    else:
        dy_x = None
    gain_one = qkv_all[:, used].astype(F32)
    gain_two = qkv_all[:, used + 1].astype(F32)
    out_wt = lax.all_gather(after(w_out.T, qkv_all), "dp", axis=0, tiled=True)
    gate_w = lax.all_gather(after(w_gate, qkv_all), "dp", axis=0, tiled=True)
    up_w = lax.all_gather(after(w_up, qkv_all), "dp", axis=0, tiled=True)
    down_wt = lax.all_gather(after(w_down.T, out_wt), "dp", axis=0, tiled=True)

    def core_half(v):
        half = v.shape[0] // 2
        return lax.dynamic_slice_in_dim(v, core * half, half, 0)

    def other_half(got):
        return lax.ppermute(got, "dp", [(i, i ^ 1) for i in range(lax.axis_size("dp"))])

    def joined(got, pair):
        both = jnp.broadcast_to(pair[None], (2, *pair.shape)).reshape(-1, pair.shape[1])
        return lax.dynamic_update_slice_in_dim(both, got, core * got.shape[0], 0)

    others = [group * m for m in range(1, seq_count)]
    out_sent = core_half(out_wt)
    qkv_halves = [swap(core_half(qkv_all), bits) for bits in others]
    out_halves = [swap(out_sent, bits) for bits in others]

    def chip_half(part):
        half = part.shape[0] // 2
        theirs = lax.dynamic_slice_in_dim(part, (1 - core) * half, half, 0)
        theirs = lax.ppermute(theirs, "dp", [(i, i ^ 1) for i in range(lax.axis_size("dp"))])
        mine = lax.dynamic_slice_in_dim(part, core * half, half, 0)
        return plus(mine, theirs)

    seg_row = lax.dynamic_index_in_dim(segments, place // group, 0, keepdims=False)
    start = doc_starts(seg_row)
    cos_t, sin_t = head_tables(jnp.arange(length, dtype=jnp.int32) - start)
    tables = (cos_t, sin_t, start[:, None], start[::BLK] // BLK)

    spread_q, spread_k = spread_matrix(heads), spread_matrix(kv)

    x_own = tokens.astype(F32)
    inv_own = inverse_rms(x_own)
    x_pair = in_order(token_blocks).astype(F32)
    inv_pair = inverse_rms(x_pair)
    n1 = (x_pair * inv_pair * gain_one).astype(BF)
    proj = project(n1, [qkv_all], jnp.zeros((1,), jnp.int32), tables, heads, kv)
    proj = after(proj, out_sent)
    o, lse = attend(proj, tables, kv, groups)
    kept, qkv_ws, out_wts = [(dot_nt(o, spread_q), proj, lse)], [qkv_all], [out_wt]
    for qkv_got, out_got in zip(qkv_halves, out_halves):
        qkv_got, dy_x = lax.optimization_barrier((qkv_got, dy_x, o))[:2]
        parts = [qkv_got, other_half(qkv_got)]
        proj = project(n1, parts, jnp.stack([core, 1 - core]).astype(jnp.int32), tables, heads, kv)
        o, lse = attend(proj, tables, kv, groups)
        out_got = after(out_got, o)
        out_wts.append(joined(out_got, other_half(out_got)))
        qkv_ws.append(joined(*after(parts, o)))
        kept.append((dot_nt(o, spread_q), proj, lse))
    if square(places):
        dy_blocks = [out_grad, dy_x, dy_y, swap(dy_x, 2)]
    else:
        dy_blocks = [pieces[0] for pieces in gather(out_grad, places)]
    o_flat = jnp.concatenate([k[0] for k in kept], axis=1)
    out_both = jnp.concatenate(out_wts, axis=1)

    def rows_of(v, bits):
        return lax.dynamic_slice_in_dim(v, ((place % group) ^ bits) * row_count, row_count, 0)

    branch, _ = scatter([None] + [[dot_nt(rows_of(o_flat, bits), out_both)] for bits in range(1, group)], group)
    segs = segments.reshape(-1)

    def masked(v, bits):
        own = lax.dynamic_slice_in_dim(segs, (place ^ bits) * row_count, row_count, 0)
        return v * (own >= 0).astype(BF)[:, None]

    dys = [masked(block, bits) for bits, block in enumerate(dy_blocks)]
    branch, dys = lax.optimization_barrier((branch, dys))
    h = x_own + dot_nt(rows_of(o_flat, 0), out_both, F32) + summed(branch)

    inv_h = inverse_rms(h)
    n2 = (h * inv_h * gain_two).astype(BF)
    n2s = gather(after(n2, gate_w), places)
    first, qkv_ws = lax.optimization_barrier((n2s[:1], qkv_ws))
    ups = gate_up(first, gate_w, up_w)
    ups += gate_up(after(n2s[1:places - 1], ups[0]), gate_w, up_w)
    ups += gate_up(after(n2s[places - 1:], ups[1]), gate_w, up_w)
    n2_pieces = [p for pieces in n2s for p in pieces]
    hiddens = [u[2] for u in ups]
    down_part = wgrad(dys, hiddens)
    down_grad = lax.psum_scatter(down_part, "dp", scatter_dimension=0, tiled=True)
    back_blocks = [(dys[r], *ups[r][:2]) for r in range(places)]
    far = gate_up_back(after(back_blocks[places - 1:], down_part), gate_w, up_w, down_wt, 2)
    near = []
    for first in range(1, places - 1, 2):
        near += gate_up_back(after(back_blocks[first:min(first + 2, places - 1)], far), gate_w, up_w, down_wt, 2)
    got, sent = scatter([None, *(v[2] for v in near + far)], places)
    own = gate_up_back(after(back_blocks[:1], near, sent), gate_w, up_w, down_wt, 2)
    backs = own + near + far
    mlp_parts = [down(v, down_wt, 1)[0] for v in after(hiddens[1:], own)]
    n2_late, got = lax.optimization_barrier((n2_pieces, got, own, mlp_parts[:2]))[:2]
    gu_part = wgrad(n2_late, [v[0] for v in backs], [v[1] for v in backs])
    gu_grad = lax.psum_scatter(gu_part, "dp", scatter_dimension=0, tiled=True)
    got = after(got, gu_part)
    d_n2 = summed(got) + jnp.concatenate(backs[0][2]).astype(F32)
    gain_two_grad = jnp.sum(d_n2 * h * inv_h, axis=0)
    dh = dys[0].astype(F32) + norm_back(h, inv_h, gain_two, d_n2)
    dhb = dh.astype(BF)
    late_hiddens, late_parts = after((hiddens[:1], mlp_parts[2:]), dhb)
    mlp_parts = [down(late_hiddens[0], down_wt, 1)[0], *mlp_parts[:2], *late_parts]

    dhb_blocks, mlp_parts, down_grad = lax.optimization_barrier((gather(dhb, group), mlp_parts, down_grad))
    dhb_pair = in_order(dhb_blocks)
    out_halves = [chip_half(dot_t(dhb_pair, k[0])) for k in kept[1:]]
    dhb_pair, mlp_parts = lax.optimization_barrier((dhb_pair, mlp_parts, out_halves))[:2]
    out_shares = [swap(v, bits) for v, bits in zip(out_halves, others)]
    if square(places):
        mlp_x = [swap(mlp_parts[3], 1), swap(mlp_parts[1], 1)]
    else:
        mlp_got = scatter([[v] for v in mlp_parts], places)[0]
    d_projs, qkv_shares = [], []
    for index in reversed(range(len(kept))):
        o, proj, lse = kept[index]
        d_o = heads_back(dhb_pair, out_wts[index], heads)
        dq, dk, dv = attend_back(proj, d_o, tables, lse, kv, groups)
        spare = jnp.zeros((dq.shape[0], qkv_all.shape[1] - used), BF)
        d_proj = jnp.concatenate([dot_nt(dq, spread_q), dot_nt(dk, spread_k), dot_nt(dv, spread_k), spare], axis=1)
        d_projs.insert(0, d_proj)
        last_dq = dq
        if index:
            part = dot_t(n1, d_proj)
            if square(places):
                part, far_got, out_shares = lax.optimization_barrier((part, mlp_x[0], out_shares))
            half = chip_half(part)
            qkv_shares.append(swap(half, others[index - 1]))
            dhb_pair = after(dhb_pair, half)

    def with_shares(mine, got):
        half = mine.shape[0] // 2
        rows = lax.dynamic_slice_in_dim(mine, core * half, half, 0).astype(F32) + sum(v.astype(F32) for v in got)
        return lax.dynamic_update_slice_in_dim(mine, rows.astype(BF), core * half, 0)

    out_part = dot_t(after(dhb_pair, last_dq), kept[0][0])
    out_grad_w = lax.psum_scatter(with_shares(out_part, out_shares), "dp", scatter_dimension=0, tiled=True)
    d_all, w_all = jnp.concatenate(d_projs, axis=1), jnp.concatenate(qkv_ws, axis=1)
    d_all, qkv_shares = lax.optimization_barrier((d_all, qkv_shares))
    d_n1_parts = [dot_nt(rows_of(d_all, bits), w_all) for bits in range(1, group)]
    d_n1_got, sent = scatter([None] + [[v] for v in d_n1_parts], group)
    d_n1_own = dot_nt(rows_of(d_all, 0), w_all, F32)
    gain_one_grad = jnp.sum(d_n1_own * x_own * inv_own, axis=0) + sum(
        jnp.sum(v.astype(F32) * token_blocks[bits][0].astype(F32) * rows_of(inv_pair, bits), axis=0)
        for bits, v in zip(range(1, group), d_n1_parts))
    if square(places):
        last_sum = plus(mlp_parts[2], far_got)
        mlp_got = [mlp_x[1], swap(last_sum, 2)]
        n1_late = after(n1, sent, mlp_x[1], last_sum, d_n1_own)
    else:
        n1_late = after(n1, sent, d_n1_own)
    qkv_part = dot_t(n1_late, d_projs[0])

    qkv_grad = lax.psum_scatter(with_shares(qkv_part, qkv_shares), "dp", scatter_dimension=0, tiled=True)
    d_n1_got, mlp_got = lax.optimization_barrier((d_n1_got, mlp_got))
    gain_one_grad, gain_two_grad = after((gain_one_grad, gain_two_grad), d_n1_got)
    gains = scatter_rows(jnp.concatenate(
        [v.reshape(lax.axis_size("dp") * places, -1) for v in (gain_one_grad, gain_two_grad)], axis=1))[0]
    output = (h + sum(v.astype(F32) for v in mlp_got) + mlp_parts[0].astype(F32)).astype(BF)
    input_grad = finish(tokens, gain_one, d_n1_own, summed(d_n1_got) if len(d_n1_got) > 1 else d_n1_got[0], dh)
    gu_grad, out_grad_w, qkv_grad = after((gu_grad, out_grad_w, qkv_grad), input_grad)
    gate_grad, up_grad = gu_grad[:, :ff], gu_grad[:, gu_grad.shape[1] // 2:gu_grad.shape[1] // 2 + ff]
    out_grad_w, qkv_grad = out_grad_w.T.astype(F32), qkv_grad.astype(F32)

    return (
        output,
        input_grad,
        gains[:gains.shape[0] // 2],
        qkv_grad[:, :q_width],
        qkv_grad[:, q_width:q_width + k_width],
        qkv_grad[:, q_width + k_width:used],
        out_grad_w,
        gains[gains.shape[0] // 2:],
        gate_grad.astype(F32),
        up_grad.astype(F32),
        down_grad.T.astype(F32),
    )


def solution(mesh):
    rows, weight_in, weight_out = P(("dp", "tensor"), None), P("dp", "tensor"), P("tensor", "dp")
    in_specs = (rows, P("dp", None), P("dp"), weight_in, weight_in, weight_in, weight_out, P("dp"),
                weight_in, weight_in, weight_out, rows)
    gain = P(("dp", "tensor"))
    out_specs = (rows, rows, gain, weight_in, weight_in, weight_in, weight_out, gain, weight_in, weight_in, weight_out)
    return jax.shard_map(body, mesh=mesh, in_specs=in_specs, out_specs=out_specs, check_vma=False)
```
